256 devices in a mesh: group: 8 (over y, core), dev: 32 (over x, z).
Axes of the slice: x: 4, y: 4, z: 8, core: 2. Of those that a mesh axis runs over, the one named last changes fastest.
Arguments:
- fine_state: float32 [256, 19, 4096], P(('group', 'dev')), may hold values from 0.01 to 0.6, as said below
- coarse_state: float32 [256, 19, 4096], P(('group', 'dev')), may hold values from 0.01 to 0.6, as said below
- fine_depth: int32 [256, 4096], P(('group', 'dev')), may hold values from -30 to 119, as said below
- coarse_depth: int32 [256, 4096], P(('group', 'dev')), may hold values from -30 to 119, as said below
- fine_links: int32 [8, 32, 6], P('group'), may hold values from -1 to 31, as said below
- coarse_links: int32 [8, 32, 6], P('group'), may hold values from -2 to 31, as said below
- parents: int32 [8, 32, 2], P('group'), may hold values from 0 to 31, as said below
Outputs:
- fine_out: float32 [256, 19, 4096], P(('group', 'dev'))
- coarse_out: float32 [256, 19, 4096], P(('group', 'dev'))
The draws below stay inside these ranges and needn't reach their ends.
Inputs may be any that keep to these rules, and one draw needn't show every extreme that they name: `fine_state`: each population is its weight w_q times a factor between 0.4 and 1.6. `coarse_state`: each population is its weight w_q times a factor between 0.4 and 1.6. `fine_depth`: in units of 1 / 7 cell: the distance from the cell to the surface of a union of two balls placed in the block, negative inside, rounded down and clipped. `coarse_depth`: in units of 1 / 7 cell: the distance from the cell to the surface of a union of two balls placed in the block, negative inside, rounded down and clipped. `fine_links`: entry (group, device, face) is the device of the same group holding the fine block across that face, or -1 where the fine region ends; neighbours are mutual (a block is its neighbour's neighbour across the opposite face) and the six neighbours of a block are distinct or -1. `coarse_links`: entry (group, device, face) is the device of the same group holding the coarse block across that face, -2 on faces 2 and 3 where the block across lies on the same device of the neighbouring group, or -1 where the domain ends; neighbours are mutual and the six of a block are distinct or negative. Each region's coarse blocks sit on devices in the same arrangement in every group. `parents`: column 0 is a device of the same group, column 1 an octant 0..7; no two fine blocks of a group share a parent device and octant.
All inputs are finite; a program needn't handle non-finite values.
Results may differ from the reference program's by a relative error of at most 0.0003.
Values sent between devices are 32-bit elements; how exact they have to be, the bound alone decides.
No kernel may reach another device: no remote copies, remote signals or barrier semaphores. Data moves between devices by JAX's collectives and lax.ppermute only.
A program may use at most 128 MiB of HBM per device.

```python
import jax
import jax.numpy as jnp
import numpy as np
from jax import lax

B = 16
H = 8
CELLS = 4096
BLOCKS = 256
N_GROUP = 8
N_DEV = 32


WEIGHT_TABLE = [1.0 / 3.0] + [1.0 / 18.0] * 6 + [1.0 / 36.0] * 12


def layout():
    bits = N_DEV.bit_length() - 1
    sizes = (2 ** ((bits + 2) // 3), 2 ** ((bits + 1) // 3), 2 ** (bits // 3))
    cells = np.arange(N_DEV)
    coords = np.stack([cells // (sizes[1] * sizes[2]), cells // sizes[2] % sizes[1], cells % sizes[2]], 1)
    beside = np.full((N_DEV, 6), -1)
    for cell in range(N_DEV):
        for face in range(6):
            point = coords[cell].copy()
            point[face // 2] += 2 * (face % 2) - 1
            if 0 <= point[face // 2] < sizes[face // 2]:
                beside[cell, face] = (point[0] * sizes[1] + point[1]) * sizes[2] + point[2]
    return (sizes, coords, beside)


def group_offset(key, sizes, group):
    group_key = jax.random.fold_in(key, 100 + group)
    offset = jax.random.randint(jax.random.fold_in(group_key, 1), (3,), 0, jnp.asarray(np.array(sizes) // 2 + 1, jnp.int32))
    return (group_key, offset)


def geometry(key):
    sizes, coords, beside = layout()
    valid = jnp.asarray(beside >= 0)
    safe = jnp.asarray(np.maximum(beside, 0), jnp.int32)
    coarse_order = jax.random.permutation(jax.random.fold_in(key, 1), N_DEV).astype(jnp.int32)
    first_key, first_offset = group_offset(key, sizes, 0)
    target = (first_offset[0] * sizes[1] + first_offset[1]) * sizes[2] + first_offset[2]
    top_place = jnp.argmax((coarse_order == N_DEV - 1).astype(jnp.int32))
    displaced = coarse_order[target]
    coarse_order = coarse_order.at[top_place].set(displaced).at[target].set(N_DEV - 1)
    coarse_place = jnp.argsort(coarse_order)
    coarse_cells = jnp.where(valid, coarse_order[safe], -1)
    octant = jnp.asarray(coords[:, 0] % 2 * 4 + coords[:, 1] % 2 * 2 + coords[:, 2] % 2, jnp.int32)
    halves = jnp.asarray(coords // 2, jnp.int32)
    coarse_rows = []
    fine_rows = []
    parent_rows = []
    for group in range(N_GROUP):
        edge = np.full((N_DEV, 6), -1)
        if group > 0:
            edge[:, 2] = -2
        if group < N_GROUP - 1:
            edge[:, 3] = -2
        codes = jnp.where(valid, coarse_cells, jnp.asarray(edge, jnp.int32))
        coarse_rows.append(codes[coarse_place])
        group_key, offset = group_offset(key, sizes, group)
        fine_order = jax.random.permutation(group_key, N_DEV).astype(jnp.int32)
        fine_place = jnp.argsort(fine_order)
        fine_cells = jnp.where(valid, fine_order[safe], -1)
        fine_rows.append(fine_cells[fine_place])
        upper = halves + offset[None, :]
        parent_cell = (upper[:, 0] * sizes[1] + upper[:, 1]) * sizes[2] + upper[:, 2]
        parent_dev = coarse_order[parent_cell]
        parent_rows.append(jnp.stack([parent_dev, octant], 1)[fine_place])
    return (jnp.stack(fine_rows).astype(jnp.int32), jnp.stack(coarse_rows).astype(jnp.int32), jnp.stack(parent_rows).astype(jnp.int32))


def draw_fine_links(key, part):
    return geometry(key)[0]


def draw_coarse_links(key, part):
    return geometry(key)[1]


def draw_parents(key, part):
    return geometry(key)[2]


def obstacle(key):
    count = BLOCKS
    units = 120 // B
    centres = jax.random.randint(jax.random.fold_in(key, 1), (count, 2, 3), 0, B)
    radii = jax.random.randint(jax.random.fold_in(key, 2), (count, 2), max(B // 4, 1), B // 2 + 1)
    line = jnp.arange(B, dtype=jnp.int32)
    along_x = (line[None, None, :, None, None] - centres[:, :, 0, None, None, None]) ** 2
    along_y = (line[None, None, None, :, None] - centres[:, :, 1, None, None, None]) ** 2
    along_z = (line[None, None, None, None, :] - centres[:, :, 2, None, None, None]) ** 2
    squared = along_x + along_y + along_z
    radius = radii[:, :, None, None, None]
    scaled = units * (squared - radius * radius) // (2 * radius)
    nearest = jnp.min(scaled, axis=1)
    return jnp.clip(nearest, -30, 119).reshape(count, CELLS).astype(jnp.int32)


def draw_fine_depth(key, part):
    key = jax.random.fold_in(key, 37)
    return obstacle(key)


def draw_coarse_depth(key, part):
    key = jax.random.fold_in(key, 41)
    return obstacle(key)


def draw_fine_state(key, part):
    key = jax.random.fold_in(key, 11)
    shape = (BLOCKS, 19, CELLS)
    weights = jnp.asarray(WEIGHT_TABLE, jnp.float32)[None, :, None]
    noise = jnp.clip(0.15 * jax.random.normal(key, shape, jnp.float32), -0.55, 0.55)
    return weights * (1.0 + noise)


def draw_coarse_state(key, part):
    key = jax.random.fold_in(key, 23)
    shape = (BLOCKS, 19, CELLS)
    weights = jnp.asarray(WEIGHT_TABLE, jnp.float32)[None, :, None]
    noise = jnp.clip(0.15 * jax.random.normal(key, shape, jnp.float32), -0.55, 0.55)
    return weights * (1.0 + noise)


def setup_inputs(seed: int = 0) -> dict:
    key_list = jax.random.split(jax.random.key(seed), 8)
    return {
        "fine_state": draw_fine_state(jax.random.fold_in(key_list[7], 71), 0),
        "coarse_state": draw_coarse_state(jax.random.fold_in(key_list[7], 71), 0),
        "fine_depth": draw_fine_depth(jax.random.fold_in(key_list[7], 71), 0),
        "coarse_depth": draw_coarse_depth(jax.random.fold_in(key_list[7], 71), 0),
        "fine_links": draw_fine_links(jax.random.fold_in(key_list[7], 71), 0),
        "coarse_links": draw_coarse_links(jax.random.fold_in(key_list[7], 71), 0),
        "parents": draw_parents(jax.random.fold_in(key_list[7], 71), 0),
    }


VELOCITIES = [(0, 0, 0), (1, 0, 0), (-1, 0, 0), (0, 1, 0), (0, -1, 0), (0, 0, 1), (0, 0, -1),
              (1, 1, 0), (-1, -1, 0), (1, -1, 0), (-1, 1, 0), (1, 0, 1), (-1, 0, -1), (1, 0, -1),
              (-1, 0, 1), (0, 1, 1), (0, -1, -1), (0, 1, -1), (0, -1, 1)]
WEIGHTS = [1.0 / 3.0] + [1.0 / 18.0] * 6 + [1.0 / 36.0] * 12
OPPOSITE = [VELOCITIES.index((-v[0], -v[1], -v[2])) for v in VELOCITIES]
OUTGOING = [[q for q in range(19) if VELOCITIES[q][face // 2] == 2 * (face % 2) - 1] for face in range(6)]
OMEGA_FINE = 1.25
OMEGA_COARSE = 1.0 / 0.65
INFLOW = 0.05


def project(field, axis):
    total = jnp.zeros_like(field[0])
    for index in range(19):
        if VELOCITIES[index][axis] != 0:
            total = total + VELOCITIES[index][axis] * field[index]
    return total


def moments(field):
    density = jnp.sum(field, axis=0)
    return density, (project(field, 0) / density, project(field, 1) / density, project(field, 2) / density)


def stacked_moments(field):
    density, velocity = moments(field)
    return jnp.stack([density, velocity[0], velocity[1], velocity[2]])


def equilibrium(density, velocity, chosen):
    square = velocity[0] * velocity[0] + velocity[1] * velocity[1] + velocity[2] * velocity[2]
    rows = []
    for index in chosen:
        along = 0.0
        for axis in range(3):
            if VELOCITIES[index][axis] != 0:
                along = along + VELOCITIES[index][axis] * velocity[axis]
        rows.append(WEIGHTS[index] * density * (1.0 + 3.0 * along + 4.5 * along * along - 1.5 * square))
    return jnp.stack(rows)


def collide(field, omega):
    density, velocity = moments(field)
    return field + omega * (equilibrium(density, velocity, range(19)) - field)


def pack(post):
    width = post.shape[1]
    planes = []
    for face in range(6):
        chosen = jnp.stack([post[index] for index in OUTGOING[face]])
        layer = 0 if face % 2 == 0 else width - 1
        planes.append(lax.index_in_dim(chosen, layer, face // 2 + 1, keepdims=False).reshape(5, width * width))
    return jnp.stack(planes)


def stream(post, start, depth, ghosts):
    width = post.shape[1]
    solid = depth <= 0
    depth_pad = jnp.pad(depth, 1, constant_values=1)
    coords = jnp.arange(width)
    rows = []
    for index in range(19):
        shift = VELOCITIES[index]
        padded = jnp.pad(post[index], 1)
        for face in range(6):
            axis = face // 2
            sign = 2 * (face % 2) - 1
            if shift[axis] == -sign:
                slot = OUTGOING[face ^ 1].index(index)
                plane = ghosts[face, slot].reshape(width, width)
                position = 0 if sign < 0 else width + 1
                if axis == 0:
                    padded = padded.at[position, 1:width + 1, 1:width + 1].set(plane)
                elif axis == 1:
                    padded = padded.at[1:width + 1, position, 1:width + 1].set(plane)
                else:
                    padded = padded.at[1:width + 1, 1:width + 1, position].set(plane)
        lows = [1 - shift[0], 1 - shift[1], 1 - shift[2]]
        source = padded[lows[0]:lows[0] + width, lows[1]:lows[1] + width, lows[2]:lows[2] + width]
        source_depth = depth_pad[lows[0]:lows[0] + width, lows[1]:lows[1] + width, lows[2]:lows[2] + width]
        outside = []
        for axis in range(3):
            line = ((coords - shift[axis] < 0) | (coords - shift[axis] >= width)).astype(jnp.int32)
            shape = [1, 1, 1]
            shape[axis] = width
            outside.append(line.reshape(shape))
        corner = (outside[0] + outside[1] + outside[2]) >= 2
        wall = jnp.logical_not(solid) & (source_depth <= 0)
        gap = jnp.where(wall, depth - source_depth, 1).astype(jnp.float32)
        fraction = jnp.where(wall, depth.astype(jnp.float32) / gap, 1.0)
        weight = jnp.where(fraction >= 0.5, 0.5 / fraction, 2.0 * fraction)
        reflected = weight * post[OPPOSITE[index]] + (1.0 - weight) * post[index]
        value = jnp.where(corner, post[OPPOSITE[index]], source)
        value = jnp.where(wall, reflected, value)
        rows.append(jnp.where(solid, start[index], value))
    return jnp.stack(rows)


def interface_planes(moment):
    half = moment.shape[1]
    planes = []
    for face in range(6):
        layer = lax.index_in_dim(moment, 0 if face % 2 == 0 else half - 1, face // 2 + 1, keepdims=False)
        layer = jnp.repeat(jnp.repeat(layer, 2, axis=1), 2, axis=2)
        planes.append(equilibrium(layer[0], (layer[1], layer[2], layer[3]), OUTGOING[face ^ 1]).reshape(5, 4 * half * half))
    return jnp.stack(planes)


def boundary_planes(width):
    ones = jnp.ones((width, width), jnp.float32)
    flow = (INFLOW * ones, 0.0 * ones, 0.0 * ones)
    return jnp.stack([equilibrium(ones, flow, OUTGOING[face ^ 1]).reshape(5, width * width) for face in range(6)])


def octants(field):
    channels, width = field.shape[0], field.shape[1]
    half = width // 2
    split = field.reshape(channels, 2, half, 2, half, 2, half).transpose(1, 3, 5, 0, 2, 4, 6)
    return split.reshape(8, channels, half * half * half)


def restrict(field):
    width = field.shape[1]
    half = width // 2
    whole = jnp.stack([jnp.sum(field, axis=0), project(field, 0), project(field, 1), project(field, 2)])
    return jnp.mean(whole.reshape(4, half, 2, half, 2, half, 2), axis=(2, 4, 6)).reshape(4, half * half * half)


def apply_restriction(coarse_new, gathered, present):
    width = coarse_new.shape[1]
    half = width // 2
    whole = gathered.reshape(2, 2, 2, 4, half, half, half).transpose(3, 0, 4, 1, 5, 2, 6).reshape(4, width, width, width)
    cover = jnp.broadcast_to(present.reshape(2, 1, 2, 1, 2, 1), (2, half, 2, half, 2, half)).reshape(width, width, width) > 0.5
    dense = jnp.where(cover, whole[0], 1.0)
    fine_eq = equilibrium(dense, (whole[1] / dense, whole[2] / dense, whole[3] / dense), range(19))
    density, velocity = moments(coarse_new)
    coarse_eq = equilibrium(density, velocity, range(19))
    return coarse_new + jnp.where(cover, fine_eq - coarse_eq, 0.0)


def reference(fine_state, coarse_state, fine_depth, coarse_depth, fine_links, coarse_links, parents):
    groups = N_GROUP
    members = N_DEV
    total = groups * members
    rows_index = jnp.arange(groups)[:, None]
    cols_index = jnp.arange(members)[None, :]
    coarse_in = coarse_state.reshape(total, 19, B, B, B)
    coarse_post = lax.map(lambda field: collide(field, OMEGA_COARSE), coarse_in)
    coarse_packets = lax.map(pack, coarse_post).reshape(groups, members, 6, 5, B * B)
    border = boundary_planes(B)
    ghosts = []
    for face in range(6):
        codes = coarse_links[:, :, face][:, :, None, None]
        local = coarse_packets[rows_index, jnp.maximum(coarse_links[:, :, face], 0), face ^ 1]
        value = jnp.where(codes >= 0, local, border[face])
        if face == 2 or face == 3:
            other = coarse_packets[jnp.clip(rows_index + (2 * face - 5), 0, groups - 1), cols_index, face ^ 1]
            value = jnp.where(codes == -2, other, value)
        ghosts.append(value)
    coarse_ghosts = jnp.stack(ghosts, axis=2).reshape(total, 6, 5, B * B)
    coarse_new = lax.map(lambda items: stream(items[0], items[1], items[2], items[3]),
                         (coarse_post, coarse_in, coarse_depth.reshape(total, B, B, B), coarse_ghosts))
    old = lax.map(stacked_moments, coarse_in)
    new = lax.map(stacked_moments, coarse_new)
    mid = (old + new) * 0.5
    parts = lax.map(octants, jnp.concatenate([old, mid], axis=1)).reshape(groups, members, 8, 8, H * H * H)
    mine = parts[rows_index, parents[:, :, 0], parents[:, :, 1]]
    state = fine_state.reshape(total, 19, B, B, B)
    depth = fine_depth.reshape(total, B, B, B)
    for turn in range(2):
        post = lax.map(lambda field: collide(field, OMEGA_FINE), state)
        packets = lax.map(pack, post).reshape(groups, members, 6, 5, B * B)
        moment = mine[:, :, 4 * turn:4 * turn + 4].reshape(total, 4, H, H, H)
        below = lax.map(interface_planes, moment).reshape(groups, members, 6, 5, B * B)
        ghosts = []
        for face in range(6):
            codes = fine_links[:, :, face]
            local = packets[rows_index, jnp.maximum(codes, 0), face ^ 1]
            ghosts.append(jnp.where(codes[:, :, None, None] >= 0, local, below[:, :, face]))
        fine_ghosts = jnp.stack(ghosts, axis=2).reshape(total, 6, 5, B * B)
        state = lax.map(lambda items: stream(items[0], items[1], items[2], items[3]), (post, state, depth, fine_ghosts))
    restricted = lax.map(restrict, state).reshape(groups, members, 4, H * H * H)
    owner = parents[:, :, 0][:, :, None, None] == jnp.arange(members)[None, None, :, None]
    octant = parents[:, :, 1][:, :, None, None] == jnp.arange(8)[None, None, None, :]
    select = (owner & octant).astype(jnp.float32)
    gathered = jnp.einsum("gcpo,gckx->gpokx", select, restricted, precision=lax.Precision.HIGHEST)
    present = jnp.sum(select, axis=1)
    coarse_out = lax.map(lambda items: apply_restriction(items[0], items[1], items[2]),
                         (coarse_new, gathered.reshape(total, 8, 4, H * H * H), present.reshape(total, 8)))
    return state.reshape(total, 19, CELLS), coarse_out.reshape(total, 19, CELLS)
```

```python
import jax
import jax.numpy as jnp
from jax import lax
from jax.experimental import pallas as pl
from jax.experimental.pallas import tpu as pltpu
from jax.sharding import PartitionSpec as P

VELOCITIES = [
    (0, 0, 0),
    (1, 0, 0),
    (-1, 0, 0),
    (0, 1, 0),
    (0, -1, 0),
    (0, 0, 1),
    (0, 0, -1),
    (1, 1, 0),
    (-1, -1, 0),
    (1, -1, 0),
    (-1, 1, 0),
    (1, 0, 1),
    (-1, 0, -1),
    (1, 0, -1),
    (-1, 0, 1),
    (0, 1, 1),
    (0, -1, -1),
    (0, 1, -1),
    (0, -1, 1),
]
WEIGHTS = [1.0 / 3.0] + [1.0 / 18.0] * 6 + [1.0 / 36.0] * 12
OPPOSITE = [VELOCITIES.index((-v[0], -v[1], -v[2])) for v in VELOCITIES]
OUTGOING = [
    [q for q in range(19) if VELOCITIES[q][face // 2] == 2 * (face % 2) - 1] for face in range(6)
]
OMEGA_FINE = 1.25
OMEGA_COARSE = 1.0 / 0.65
INFLOW = 0.05
F32 = jnp.float32
FIELD = (19, 16, 256)
SLOT1 = 40
SLOT2 = 32
SLOT3 = 16


def inflow_value(q):
    along = VELOCITIES[q][0] * INFLOW
    return WEIGHTS[q] * (1.0 + 3.0 * along + 4.5 * along * along - 1.5 * INFLOW * INFLOW)


def iota(shape, dim):
    return lax.broadcasted_iota(jnp.int32, shape, dim)


def tile(value, row, half):
    return value[8 * row : 8 * row + 8, 128 * half : 128 * half + 128]


def join(tiles):
    return jnp.concatenate([jnp.concatenate(line, axis=1) for line in tiles], axis=0)


def pick(value, index, axis):
    return jnp.take_along_axis(value, index, axis=axis, mode="promise_in_bounds")


def sums(f):
    density = f[0]
    for q in range(1, 19):
        density = density + f[q]
    momentum = []
    for axis in range(3):
        plus = [f[q] for q in range(19) if VELOCITIES[q][axis] == 1]
        minus = [f[q] for q in range(19) if VELOCITIES[q][axis] == -1]
        total = plus[0] - minus[0]
        for a, b in zip(plus[1:], minus[1:]):
            total = total + (a - b)
        momentum.append(total)
    return density, momentum


def moments(f):
    density, momentum = sums(f)
    inverse = 1.0 / density
    return density, [m * inverse for m in momentum]


def equilibrium(density, u, chosen):
    base = 1.0 - 1.5 * (u[0] * u[0] + u[1] * u[1] + u[2] * u[2])
    scaled = {}
    for q in chosen:
        if WEIGHTS[q] not in scaled:
            scaled[WEIGHTS[q]] = WEIGHTS[q] * density
    even, out = {}, {}
    for q in chosen:
        v = VELOCITIES[q]
        weight = scaled[WEIGHTS[q]]
        if q == 0:
            out[q] = weight * base
            continue
        lead = q if q % 2 == 1 else q - 1
        if lead not in even:
            along = None
            for axis in range(3):
                c = VELOCITIES[lead][axis]
                if c != 0:
                    if along is None:
                        along = u[axis]
                    else:
                        along = along + u[axis] if c > 0 else along - u[axis]
            even[lead] = (base + 4.5 * along * along, 3.0 * along)
        part, odd = even[lead]
        out[q] = weight * (part + odd) if q == lead else weight * (part - odd)
    return out


def collide(f, omega):
    density, u = moments(f)
    rest = equilibrium(density, u, range(19))
    return [(1.0 - omega) * f[q] + omega * rest[q] for q in range(19)]


def pack_face(post, face, offset):
    axis, side = face // 2, face % 2
    lane = iota((8, 128), 1)
    sub = iota((8, 128), 0)
    chosen = [post[q] for q in OUTGOING[face]]
    if axis == 0:
        at = 15 * side
        rows = [f[at : at + 1, :] for f in chosen]
        first = None
        for i in range(4):
            for half in range(2):
                line = jnp.broadcast_to(rows[i][:, 128 * half : 128 * half + 128], (8, 128))
                first = line if first is None else jnp.where(sub == 2 * i + half, line, first)
        second = None
        for half in range(2):
            line = jnp.broadcast_to(rows[4][:, 128 * half : 128 * half + 128], (8, 128))
            turned = pltpu.roll(line, 64, 1)
            low, high = (line, turned) if offset == 0 else (turned, line)
            for k, value in ((2 * half, low), (2 * half + 1, high)):
                second = value if second is None else jnp.where(sub == k, value, second)
        return first, second
    strips = []
    for f in chosen:
        for row in range(2):
            if axis == 1:
                strips.append(pick(tile(f, row, side), lane % 16 + 112 * side, 1))
            else:
                index = (lane % 8) * 16 + 15 * side
                a = pick(tile(f, row, 0), index, 1)
                b = pick(tile(f, row, 1), index, 1)
                strips.append(jnp.where(lane % 16 < 8, a, b))
    first = strips[0]
    for t in range(1, 8):
        first = jnp.where(lane // 16 == t, strips[t], first)
    second = jnp.where((lane // 16) % 2 == 0, strips[8], strips[9])
    return first, second


def unpack_face(first, second, offset, face):
    axis, side = face // 2, face % 2
    lane = iota((8, 128), 1)
    out = {}
    for i, q in enumerate(OUTGOING[face ^ 1]):
        if axis == 0:
            halves = []
            for half in range(2):
                if i < 4:
                    line = first[2 * i + half : 2 * i + half + 1, :]
                else:
                    turned = pltpu.roll(second, 64, 1)
                    low, high = (second, turned) if offset == 0 else (turned, second)
                    line = jnp.where(
                        lane[0:1] < 64,
                        low[2 * half : 2 * half + 1, :],
                        high[2 * half + 1 : 2 * half + 2, :],
                    )
                halves.append(jnp.broadcast_to(line, (16, 128)))
            out[q] = jnp.concatenate(halves, axis=1)
            continue
        rows = []
        for row in range(2):
            source, base = (first, 16 * (2 * i + row)) if i < 4 else (second, offset + 16 * row)
            if axis == 1:
                piece = pick(source, base + lane % 16, 1)
                rows.append([piece, piece])
            else:
                step = 1 if side == 0 else 15
                rows.append(
                    [
                        pick(source, base + (8 * half + lane // 16 + step) % 16, 1)
                        for half in range(2)
                    ]
                )
        out[q] = join(rows)
    return out


def shifted(value, v):
    if v[0] != 0:
        value = pltpu.roll(value, v[0] % 16, 0)
    lanes = (16 * v[1] + v[2]) % 256
    if lanes != 0:
        value = pltpu.roll(value, lanes, 1)
    return value


def positions():
    row = iota((16, 256), 0)
    lane = iota((16, 256), 1)
    return row, lane // 16, lane % 16


def wall_weights(depth):
    place = positions()
    solid = depth <= 0
    here = depth.astype(F32)
    out = [jnp.where(solid, 1.0, 0.0).astype(F32)]
    for q in range(1, 19):
        v = VELOCITIES[q]
        outside = []
        for axis in range(3):
            if v[axis] != 0:
                outside.append(place[axis] == (0 if v[axis] > 0 else 15))
        away = outside[0] if len(outside) == 1 else outside[0] | outside[1]
        there = shifted(here, v)
        wall = (there <= 0.0) & jnp.logical_not(away) & jnp.logical_not(solid)
        gap = jnp.where(wall, here - there, 1.0)
        own = jnp.where(wall, here, 1.0)
        far = own + own >= gap
        weight = jnp.where(far, 0.5 * gap, 2.0 * own) / jnp.where(far, own, gap)
        value = jnp.where(wall, weight, -1.0)
        if len(outside) == 2:
            value = jnp.where(outside[0] & outside[1], 1.0, value)
        out.append(value)
    return out


def stream(post, start, weights, ghosts):
    place = positions()
    solid = weights(0) > 0.5
    out = [jnp.where(solid, start(0), post(0))]
    for q in range(1, 19):
        v = VELOCITIES[q]
        own = post(q)
        value = own
        for axis in (1, 0, 2):
            if v[axis] != 0:
                edge = place[axis] == (15 if v[axis] > 0 else 0)
                value = jnp.where(edge, ghosts[axis][q], value)
        value = shifted(value, v)
        weight = weights(q)
        value = jnp.where(weight >= 0.0, own + weight * (post(OPPOSITE[q]) - own), value)
        out.append(jnp.where(solid, start(q), value))
    return out


def pack_octants(fields):
    low = iota((8, 128), 1) % 16 < 8
    out = {}
    for ox in range(2):
        for oy in range(2):
            a, b, c, d = [tile(f, ox, oy) for f in fields]
            out[4 * ox + 2 * oy] = (
                jnp.where(low, a, pltpu.roll(b, 8, 1)),
                jnp.where(low, c, pltpu.roll(d, 8, 1)),
            )
            out[4 * ox + 2 * oy + 1] = (
                jnp.where(low, pltpu.roll(a, 120, 1), b),
                jnp.where(low, pltpu.roll(c, 120, 1), d),
            )
    return out


def upsample(pair):
    lane = iota((8, 128), 1)
    sub = iota((8, 128), 0)
    fields = []
    for k in range(4):
        source = pair[k // 2]
        halves = []
        for half in range(2):
            index = (4 * half + lane // 32) * 16 + (lane % 16) // 2 + 8 * (k % 2)
            halves.append(pick(source, index, 1))
        fields.append(
            join([[pick(h, 4 * row + sub // 2, 0) for h in halves] for row in range(2)])
        )
    return fields


def below(fields):
    place = positions()
    out = []
    for axis in range(3):
        step = [0, 0, 0]
        step[axis] = 1
        back = [0, 0, 0]
        back[axis] = -1
        last = place[axis] == 15
        crossed = [jnp.where(last, shifted(f, back), shifted(f, step)) for f in fields]
        chosen = [q for q in range(19) if VELOCITIES[q][axis] != 0]
        out.append(equilibrium(crossed[0], crossed[1:], chosen))
    return out


def restrict(f):
    lane = iota((8, 128), 1)
    sub = iota((8, 128), 0)
    density, momentum = sums(f)
    packed = []
    for field in [density] + momentum:
        field = field + pltpu.roll(field, 255, 1)
        field = field + pltpu.roll(field, 240, 1)
        field = 0.125 * (field + pltpu.roll(field, 15, 0))
        index = ((lane // 16) % 4) * 32 + (lane % 8) * 2
        halves = []
        for half in range(2):
            upper = pick(tile(field, 0, half), (2 * sub) % 8, 0)
            lower = pick(tile(field, 1, half), (2 * sub) % 8, 0)
            halves.append(pick(jnp.where(sub < 4, upper, lower), index, 1))
        packed.append(jnp.where(lane < 64, halves[0], halves[1]))
    low = lane % 16 < 8
    return jnp.where(low, packed[0], packed[1]), jnp.where(low, packed[2], packed[3])


def load(ref):
    return [ref[q] for q in range(19)]


def send_kernel(coarse, fine, coarse_links, fine_links, parents, out, region, octs, work):
    me = lax.axis_index("dev")
    work[...] = coarse[0].reshape(FIELD)
    f = load(work)
    density, u = moments(f)
    for o, pair in pack_octants([density] + u).items():
        octs[o, 0:8, :] = pair[0]
        octs[o, 8:16, :] = pair[1]

    def give(d, carry):
        @pl.when(parents[0, d, 0] == me)
        def _():
            out[d, 24:40, :] = octs[parents[0, d, 1]]

        return carry

    lax.fori_loop(0, 32, give, 0)
    post = collide(f, OMEGA_COARSE)
    for face in range(6):
        first, second = pack_face(post, face, 0)
        if face in (2, 3):
            region[face - 2, 0:8, :] = first
            region[face - 2, 8:16, :] = second
        code = coarse_links[0, me, face]

        @pl.when(code >= 0)
        def _():
            out[code, 0:8, :] = first
            out[code, 16:24, 0:64] = second[:, 0:64]

    work[...] = fine[0].reshape(FIELD)
    post = collide(load(work), OMEGA_FINE)
    for face in range(6):
        first, second = pack_face(post, face, 64)
        code = fine_links[0, me, face]

        @pl.when(code >= 0)
        def _():
            out[code, 8:16, :] = first
            out[code, 16:24, 64:128] = second[:, 64:128]


def prepare_kernel(state, depth, post, start, weights, *, omega):
    start[...] = state[0].reshape(FIELD)
    for q, value in enumerate(collide(load(start), omega)):
        post[q] = value
    for q, value in enumerate(wall_weights(depth[...].reshape(16, 256))):
        weights[q] = value


def merge_ghosts(take):
    ghosts = [{}, {}, {}]
    for face in range(6):
        ghosts[face // 2].update(take(face))
    return ghosts


def middle_kernel(
    received, from_low, from_high, c_post, c_start, c_weights, f_post, f_start, f_weights,
    coarse_links, fine_links, parents, out, coarse_new, state, post, octs,
):
    me = lax.axis_index("dev")

    def coarse_ghost(face):
        code = coarse_links[0, me, face]
        slot = jnp.maximum(code, 0)
        first = received[slot, 0:8, :]
        second = received[slot, 16:24, :]
        if face in (2, 3):
            beside = from_low if face == 2 else from_high
            first = jnp.where(code == -2, beside[0, 0:8, :], first)
            second = jnp.where(code == -2, beside[0, 8:16, :], second)
        plane = unpack_face(first, second, 0, face)
        return {q: jnp.where(code == -1, inflow_value(q), plane[q]) for q in plane}

    new = stream(
        lambda q: c_post[q], lambda q: c_start[q], lambda q: c_weights[q], merge_ghosts(coarse_ghost)
    )
    for q in range(19):
        coarse_new[q] = new[q]
    old_density, old_u = moments([c_start[q] for q in range(19)])
    density, u = moments(new)
    mid = [0.5 * (old_density + density)] + [0.5 * (a + b) for a, b in zip(old_u, u)]
    for o, pair in pack_octants(mid).items():
        octs[o, 0:8, :] = pair[0]
        octs[o, 8:16, :] = pair[1]

    def give(d, carry):
        @pl.when(parents[0, d, 0] == me)
        def _():
            out[d, 16:32, :] = octs[parents[0, d, 1]]

        return carry

    lax.fori_loop(0, 32, give, 0)
    parent = parents[0, me, 0]
    under = below(upsample((received[parent, 24:32, :], received[parent, 32:40, :])))

    def fine_ghost(face):
        code = fine_links[0, me, face]
        slot = jnp.maximum(code, 0)
        plane = unpack_face(received[slot, 8:16, :], received[slot, 16:24, :], 64, face)
        return {q: jnp.where(code >= 0, plane[q], under[face // 2][q]) for q in plane}

    new = stream(
        lambda q: f_post[q], lambda q: f_start[q], lambda q: f_weights[q], merge_ghosts(fine_ghost)
    )
    for q in range(19):
        state[q] = new[q]
    after = collide(new, OMEGA_FINE)
    for q in range(19):
        post[q] = after[q]
    for face in range(6):
        first, second = pack_face(after, face, 0)
        code = fine_links[0, me, face]

        @pl.when(code >= 0)
        def _():
            out[code, 0:8, :] = first
            out[code, 8:16, :] = second


def last_kernel(received, f_post, f_start, f_weights, fine_links, parents, out, state):
    me = lax.axis_index("dev")
    parent = parents[0, me, 0]
    under = below(upsample((received[parent, 16:24, :], received[parent, 24:32, :])))

    def fine_ghost(face):
        code = fine_links[0, me, face]
        slot = jnp.maximum(code, 0)
        plane = unpack_face(received[slot, 0:8, :], received[slot, 8:16, :], 0, face)
        return {q: jnp.where(code >= 0, plane[q], under[face // 2][q]) for q in plane}

    new = stream(
        lambda q: f_post[q], lambda q: f_start[q], lambda q: f_weights[q], merge_ghosts(fine_ghost)
    )
    for q in range(19):
        state[q] = new[q]
    first, second = restrict(new)
    out[parent, 0:8, :] = first
    out[parent, 8:16, :] = second


def finish_kernel(state, fine_out):
    fine_out[0] = state[...].reshape(19, 4096)


def coarse_kernel(received, coarse_new, parents, coarse_out, octs, cover):
    me = lax.axis_index("dev")
    for o in range(8):
        cover[o] = 0

    def take(d, carry):
        @pl.when(parents[0, d, 0] == me)
        def _():
            octs[parents[0, d, 1]] = received[d]
            cover[parents[0, d, 1]] = 1

        return carry

    lax.fori_loop(0, 32, take, 0)
    low = iota((8, 128), 1) % 16 < 8
    tiles = [[[None, None], [None, None]] for _ in range(5)]
    for ox in range(2):
        for oy in range(2):
            o = 4 * ox + 2 * oy
            for k in range(2):
                a = octs[o, 8 * k : 8 * k + 8, :]
                b = octs[o + 1, 8 * k : 8 * k + 8, :]
                tiles[2 * k][ox][oy] = jnp.where(low, a, pltpu.roll(b, 8, 1))
                tiles[2 * k + 1][ox][oy] = jnp.where(low, pltpu.roll(a, 120, 1), b)
            tiles[4][ox][oy] = jnp.where(low, cover[o], cover[o + 1])
    density, jx, jy, jz, covered = [join(t) for t in tiles]
    covered = covered > 0
    density = jnp.where(covered, density, 1.0)
    inverse = 1.0 / density
    fine_eq = equilibrium(density, [jx * inverse, jy * inverse, jz * inverse], range(19))
    new = load(coarse_new)
    own_density, own_u = moments(new)
    own_eq = equilibrium(own_density, own_u, range(19))
    result = [new[q] + jnp.where(covered, fine_eq[q] - own_eq[q], 0.0) for q in range(19)]
    coarse_out[0] = jnp.stack(result).reshape(19, 4096)


VMEM = pl.BlockSpec(memory_space=pltpu.VMEM)
SMEM = pl.BlockSpec(memory_space=pltpu.SMEM)
PARAMS = pltpu.CompilerParams(vmem_limit_bytes=24 * 1024 * 1024)


def call(kernel, outs, ins, smem=(), scratch=(), cost=2_000_000, name=None):
    shapes = [jax.ShapeDtypeStruct(s, F32) for s in outs]
    return pl.pallas_call(
        kernel,
        out_shape=shapes,
        in_specs=[SMEM if i in smem else VMEM for i in range(len(ins))],
        out_specs=[VMEM] * len(outs),
        scratch_shapes=list(scratch),
        compiler_params=PARAMS,
        cost_estimate=pl.CostEstimate(flops=cost, bytes_accessed=2_000_000, transcendentals=0),
        name=name,
    )(*ins)


def swap(value):
    return lax.all_to_all(value, "dev", split_axis=0, concat_axis=0, tiled=True)


def body(fine_state, coarse_state, fine_depth, coarse_depth, fine_links, coarse_links, parents):
    count = lax.axis_size("group")
    octs = pltpu.VMEM((8, 16, 128), F32)
    sent, region = call(
        send_kernel,
        [(32, SLOT1, 128), (2, 16, 128)],
        [coarse_state, fine_state, coarse_links, fine_links, parents],
        smem=(2, 3, 4),
        scratch=[octs, pltpu.VMEM(FIELD, F32)],
        name="send",
    )
    up = [(i, i + 1) for i in range(count - 1)]
    down = [(b, a) for a, b in up]
    received = swap(sent)
    from_low = lax.ppermute(region[1:2], "group", up)
    from_high = lax.ppermute(region[0:1], "group", down)

    def prepare(state, depth, omega, name):
        def kernel(*refs):
            prepare_kernel(*refs, omega=omega)

        return call(kernel, [FIELD, FIELD, FIELD], [state, depth], name=name)

    c_post, c_start, c_weights = prepare(coarse_state, coarse_depth, OMEGA_COARSE, "prepare_coarse")
    f_post, f_start, f_weights = prepare(fine_state, fine_depth, OMEGA_FINE, "prepare_fine")
    sent, coarse_new, state, post = call(
        middle_kernel,
        [(32, SLOT2, 128), FIELD, FIELD, FIELD],
        [
            received, from_low, from_high, c_post, c_start, c_weights, f_post, f_start, f_weights,
            coarse_links, fine_links, parents,
        ],
        smem=(9, 10, 11),
        scratch=[octs],
        name="middle",
    )
    received = swap(sent)
    sent, state = call(
        last_kernel,
        [(32, SLOT3, 128), FIELD],
        [received, post, state, f_weights, fine_links, parents],
        smem=(4, 5),
        name="last",
    )
    received = swap(sent)
    (fine_out,) = call(finish_kernel, [(1, 19, 4096)], [state], name="finish")
    (coarse_out,) = call(
        coarse_kernel,
        [(1, 19, 4096)],
        [received, coarse_new, parents],
        smem=(2,),
        scratch=[octs, pltpu.SMEM((8,), jnp.int32)],
        name="coarse",
    )
    return fine_out, coarse_out


def solution(mesh):
    placed = (
        P(("group", "dev"), None, None),
        P(("group", "dev"), None, None),
        P(("group", "dev"), None),
        P(("group", "dev"), None),
        P("group", None, None),
        P("group", None, None),
        P("group", None, None),
    )
    return jax.shard_map(
        body,
        mesh=mesh,
        in_specs=placed,
        out_specs=(P(("group", "dev"), None, None), P(("group", "dev"), None, None)),
        check_vma=False,
    )
```

```python
import jax
import jax.numpy as jnp
from jax import lax
from jax.experimental import pallas as pl
from jax.experimental.pallas import tpu as pltpu
from jax.sharding import PartitionSpec as P

VELOCITIES = [
    (0, 0, 0),
    (1, 0, 0),
    (-1, 0, 0),
    (0, 1, 0),
    (0, -1, 0),
    (0, 0, 1),
    (0, 0, -1),
    (1, 1, 0),
    (-1, -1, 0),
    (1, -1, 0),
    (-1, 1, 0),
    (1, 0, 1),
    (-1, 0, -1),
    (1, 0, -1),
    (-1, 0, 1),
    (0, 1, 1),
    (0, -1, -1),
    (0, 1, -1),
    (0, -1, 1),
]
WEIGHTS = [1.0 / 3.0] + [1.0 / 18.0] * 6 + [1.0 / 36.0] * 12
OPPOSITE = [VELOCITIES.index((-v[0], -v[1], -v[2])) for v in VELOCITIES]
OUTGOING = [
    [q for q in range(19) if VELOCITIES[q][face // 2] == 2 * (face % 2) - 1] for face in range(6)
]
OMEGA_FINE = 1.25
OMEGA_COARSE = 1.0 / 0.65
INFLOW = 0.05
F32 = jnp.float32
FIELD = (19, 16, 256)
CELL_ROWS = (19, 32, 128)
SLOT1 = 32
SLOT2 = 24
SLOT3 = 16


def inflow_value(q):
    along = VELOCITIES[q][0] * INFLOW
    return WEIGHTS[q] * (1.0 + 3.0 * along + 4.5 * along * along - 1.5 * INFLOW * INFLOW)


def iota(shape, dim):
    return lax.broadcasted_iota(jnp.int32, shape, dim)


def tile(value, row, half):
    return value[8 * row : 8 * row + 8, 128 * half : 128 * half + 128]


def join(tiles):
    return jnp.concatenate([jnp.concatenate(line, axis=1) for line in tiles], axis=0)


def pick(value, index, axis):
    return jnp.take_along_axis(value, index, axis=axis, mode="promise_in_bounds")


def sums(f):
    density = f[0]
    for q in range(1, 19):
        density = density + f[q]
    momentum = []
    for axis in range(3):
        plus = [f[q] for q in range(19) if VELOCITIES[q][axis] == 1]
        minus = [f[q] for q in range(19) if VELOCITIES[q][axis] == -1]
        total = plus[0] - minus[0]
        for a, b in zip(plus[1:], minus[1:]):
            total = total + (a - b)
        momentum.append(total)
    return density, momentum


def moments(f):
    density, momentum = sums(f)
    inverse = 1.0 / density
    return density, [m * inverse for m in momentum]


def equilibrium(density, u, chosen):
    base = 1.0 - 1.5 * (u[0] * u[0] + u[1] * u[1] + u[2] * u[2])
    scaled = {}
    for q in chosen:
        if WEIGHTS[q] not in scaled:
            scaled[WEIGHTS[q]] = WEIGHTS[q] * density
    even, out = {}, {}
    for q in chosen:
        v = VELOCITIES[q]
        weight = scaled[WEIGHTS[q]]
        if q == 0:
            out[q] = weight * base
            continue
        lead = q if q % 2 == 1 else q - 1
        if lead not in even:
            along = None
            for axis in range(3):
                c = VELOCITIES[lead][axis]
                if c != 0:
                    if along is None:
                        along = u[axis]
                    else:
                        along = along + u[axis] if c > 0 else along - u[axis]
            even[lead] = (base + 4.5 * along * along, 3.0 * along)
        part, odd = even[lead]
        out[q] = weight * (part + odd) if q == lead else weight * (part - odd)
    return out


def collide(f, omega):
    density, u = moments(f)
    rest = equilibrium(density, u, range(19))
    return [(1.0 - omega) * f[q] + omega * rest[q] for q in range(19)]


def row_parts(top, bottom, lane, sub):
    both = jnp.where(sub < 4, jnp.broadcast_to(top, (8, 128)), jnp.broadcast_to(bottom, (8, 128)))
    return pick(both, 32 * (sub & 3) + (lane & 31), 1)


def pack_face(post, face):
    axis, side = face // 2, face % 2
    lane = iota((8, 128), 1)
    sub = iota((8, 128), 0)
    chosen = [post[q] for q in OUTGOING[face]]
    if axis == 0:
        at = 15 * side
        rows = [[f[at : at + 1, 128 * h : 128 * h + 128] for h in range(2)] for f in chosen]
        first = None
        for i in range(4):
            for half in range(2):
                line = jnp.broadcast_to(rows[i][half], (8, 128))
                first = line if first is None else jnp.where(sub == 2 * i + half, line, first)
        return first, row_parts(rows[4][0], rows[4][1], lane, sub)
    strips = []
    for f in chosen:
        for row in range(2):
            if axis == 1:
                strips.append(pick(tile(f, row, side), (lane & 15) + 112 * side, 1))
            else:
                index = (lane & 7) * 16 + 15 * side
                a = pick(tile(f, row, 0), index, 1)
                b = pick(tile(f, row, 1), index, 1)
                strips.append(jnp.where((lane & 15) < 8, a, b))
    first = strips[0]
    for t in range(1, 8):
        first = jnp.where((lane >> 4) == t, strips[t], first)
    second = jnp.where(((lane >> 4) & 1) == 0, strips[8], strips[9])
    return first, second


def unpack_face(first, second, offset, face):
    axis, side = face // 2, face % 2
    lane = iota((8, 128), 1)
    out = {}
    for i, q in enumerate(OUTGOING[face ^ 1]):
        if axis == 0:
            halves = []
            for half in range(2):
                if i < 4:
                    line = jnp.broadcast_to(first[2 * i + half : 2 * i + half + 1, :], (8, 128))
                else:
                    line = pick(pick(second, offset + (lane & 31), 1), 4 * half + (lane >> 5), 0)
                halves.append(line)
            out[q] = join([halves, halves])
            continue
        rows = []
        for row in range(2):
            source, base = (first, 16 * (2 * i + row)) if i < 4 else (second, offset + 16 * row)
            if axis == 1:
                piece = pick(source, base + (lane & 15), 1)
                rows.append([piece, piece])
            else:
                step = 1 if side == 0 else 15
                rows.append(
                    [
                        pick(source, base + ((8 * half + (lane >> 4) + step) & 15), 1)
                        for half in range(2)
                    ]
                )
        out[q] = join(rows)
    return out


def pack_shell(pair):
    lane = iota((8, 128), 1)
    sub = iota((8, 128), 0)
    part = lane & 31
    along_y = part + 96 * (part >> 4)
    which = part & 3
    along_z = (part >> 2) * 16 + 8 * (which >> 1) + 7 * (which & 1)
    segment = lane >> 5
    a, b = pair
    rows_a = row_parts(a[0:1, :], a[7:8, :], lane, sub)
    rows_b = row_parts(b[0:1, :], b[7:8, :], lane, sub)
    rest = pick(a, jnp.where(segment == 1, along_y, along_z), 1)
    first = jnp.where(segment == 0, rows_a, jnp.where(segment == 3, rows_b, rest))
    second = pick(b, jnp.where(segment == 2, along_y, along_z), 1)
    return first, second


def unpack_shell(first, second):
    lane = iota((8, 128), 1)
    sub = iota((8, 128), 0)
    part = lane & 31
    line = (lane >> 5) + jnp.where(sub == 7, 4, 0)
    along_y = (lane & 15) + jnp.where(lane >= 112, 16, 0)
    z = lane & 15
    along_z = (lane >> 4) * 4 + 2 * (z >> 3) + jnp.where((z & 7) == 7, 1, 0)
    on_y = (lane < 16) | (lane >= 112)
    on_x = (sub == 0) | (sub == 7)
    out = []
    for rows, base_x, rest, base_y, base_z in (
        (first, 0, first, 32, 64),
        (first, 96, second, 64, 96),
    ):
        x = pick(pick(rows, base_x + part, 1), line, 0)
        other = pick(rest, jnp.where(on_y, base_y + along_y, base_z + along_z), 1)
        out.append(jnp.where(on_x, x, other))
    return out


def shifted(value, v):
    if v[0] != 0:
        value = pltpu.roll(value, v[0] % 16, 0)
    lanes = (16 * v[1] + v[2]) % 256
    if lanes != 0:
        value = pltpu.roll(value, lanes, 1)
    return value


def positions():
    row = iota((16, 256), 0)
    lane = iota((16, 256), 1)
    return row, lane >> 4, lane & 15


def wall_weights(depth):
    place = positions()
    solid = depth <= 0
    here = depth.astype(F32)
    out = [jnp.where(solid, 1.0, 0.0).astype(F32)]
    for q in range(1, 19):
        v = VELOCITIES[q]
        outside = []
        for axis in range(3):
            if v[axis] != 0:
                outside.append(place[axis] == (0 if v[axis] > 0 else 15))
        away = outside[0] if len(outside) == 1 else outside[0] | outside[1]
        there = shifted(here, v)
        wall = (there <= 0.0) & jnp.logical_not(away) & jnp.logical_not(solid)
        gap = jnp.where(wall, here - there, 1.0)
        own = jnp.where(wall, here, 1.0)
        far = own + own >= gap
        weight = jnp.where(far, 0.5 * gap, 2.0 * own) / jnp.where(far, own, gap)
        value = jnp.where(wall, weight, -1.0)
        if len(outside) == 2:
            value = jnp.where(outside[0] & outside[1], 1.0, value)
        out.append(value)
    return out


def stream(post, start, weights, ghosts):
    place = positions()
    solid = weights(0) > 0.5
    out = [jnp.where(solid, start(0), post(0))]
    for q in range(1, 19):
        v = VELOCITIES[q]
        own = post(q)
        value = own
        for axis in (1, 0, 2):
            if v[axis] != 0:
                edge = place[axis] == (15 if v[axis] > 0 else 0)
                value = jnp.where(edge, ghosts[axis][q], value)
        value = shifted(value, v)
        weight = weights(q)
        value = jnp.where(weight >= 0.0, own + weight * (post(OPPOSITE[q]) - own), value)
        out.append(jnp.where(solid, start(q), value))
    return out


def pack_octants(fields):
    low = (iota((8, 128), 1) & 15) < 8
    out = {}
    for ox in range(2):
        for oy in range(2):
            a, b, c, d = [tile(f, ox, oy) for f in fields]
            out[4 * ox + 2 * oy] = (
                jnp.where(low, a, pltpu.roll(b, 8, 1)),
                jnp.where(low, c, pltpu.roll(d, 8, 1)),
            )
            out[4 * ox + 2 * oy + 1] = (
                jnp.where(low, pltpu.roll(a, 120, 1), b),
                jnp.where(low, pltpu.roll(c, 120, 1), d),
            )
    return out


def upsample(pair):
    lane = iota((8, 128), 1)
    sub = iota((8, 128), 0)
    fields = []
    for k in range(4):
        source = pair[k // 2]
        halves = []
        for half in range(2):
            index = (4 * half + (lane >> 5)) * 16 + ((lane & 15) >> 1) + 8 * (k % 2)
            halves.append(pick(source, index, 1))
        fields.append(
            join([[pick(h, 4 * row + (sub >> 1), 0) for h in halves] for row in range(2)])
        )
    return fields


def below(fields):
    place = positions()
    out = []
    for axis in range(3):
        step = [0, 0, 0]
        step[axis] = 1
        back = [0, 0, 0]
        back[axis] = -1
        last = place[axis] == 15
        crossed = [jnp.where(last, shifted(f, back), shifted(f, step)) for f in fields]
        chosen = [q for q in range(19) if VELOCITIES[q][axis] != 0]
        out.append(equilibrium(crossed[0], crossed[1:], chosen))
    return out


def restrict(f):
    lane = iota((8, 128), 1)
    sub = iota((8, 128), 0)
    density, momentum = sums(f)
    packed = []
    for field in [density] + momentum:
        field = field + pltpu.roll(field, 255, 1)
        field = field + pltpu.roll(field, 240, 1)
        field = 0.125 * (field + pltpu.roll(field, 15, 0))
        index = ((lane >> 4) & 3) * 32 + (lane & 7) * 2
        halves = []
        for half in range(2):
            upper = pick(tile(field, 0, half), (2 * sub) & 7, 0)
            lower = pick(tile(field, 1, half), (2 * sub) & 7, 0)
            halves.append(pick(jnp.where(sub < 4, upper, lower), index, 1))
        packed.append(jnp.where(lane < 64, halves[0], halves[1]))
    low = (lane & 15) < 8
    return jnp.where(low, packed[0], packed[1]), jnp.where(low, packed[2], packed[3])


def load(ref):
    return [ref[q] for q in range(19)]


def load_cells(ref, q):
    halves = [ref[q, pl.ds(half, 16, stride=2), :] for half in range(2)]
    return jnp.concatenate(halves, axis=1)


def store_cells(ref, q, value):
    for half in range(2):
        ref[q, pl.ds(half, 16, stride=2), :] = value[:, 128 * half : 128 * half + 128]


def store_octants(fields, octs):
    for o, pair in pack_octants(fields).items():
        first, second = pack_shell(pair)
        octs[o, 0:8, :] = first
        octs[o, 8:16, :] = second


def give_octants(octs, parents, out, at, shared):
    for d in range(32):
        o = parents[1, 0, d]
        out[d, at : at + 8, :] = octs[o, 0:8, :]
        out[d, shared : shared + 8, 64:128] = octs[o, 8:16, 64:128]


def give_face(post, face, code, me, out, at, shared, lanes):
    first, second = pack_face(post, face)
    slot = jnp.where(code >= 0, code, me)
    out[slot, at : at + 8, :] = first
    out[slot, shared : shared + 8, lanes : lanes + 32] = second[:, lanes : lanes + 32]
    return first, second


def send_kernel(coarse, fine, coarse_links, fine_links, parents, out, region, octs):
    me = lax.axis_index("dev")
    f = [load_cells(coarse, q) for q in range(19)]
    density, u = moments(f)
    store_octants([density] + u, octs)
    post = collide(f, OMEGA_COARSE)
    for face in range(6):
        first, second = give_face(post, face, coarse_links[face, 0, me], me, out, 0, 16, 0)
        if face in (2, 3):
            region[face - 2, 0:8, :] = first
            region[face - 2, 8:16, :] = second
    post = collide([load_cells(fine, q) for q in range(19)], OMEGA_FINE)
    for face in range(6):
        give_face(post, face, fine_links[face, 0, me], me, out, 8, 16, 32)
    give_octants(octs, parents, out, 24, 16)


def prepare_kernel(state, depth, post, start, weights, *, omega):
    f = [load_cells(state, q) for q in range(19)]
    for q in range(19):
        start[q] = f[q]
    for q, value in enumerate(collide(f, omega)):
        post[q] = value
    halves = [depth[pl.ds(half, 16, stride=2), :] for half in range(2)]
    for q, value in enumerate(wall_weights(jnp.concatenate(halves, axis=1))):
        weights[q] = value


def merge_ghosts(take):
    ghosts = [{}, {}, {}]
    for face in range(6):
        ghosts[face // 2].update(take(face))
    return ghosts


def fine_ghosts(received, links, parents, me, plane_at, shared, moment_at):
    parent = parents[0, 0, me]
    shell = unpack_shell(
        received[parent, moment_at : moment_at + 8, :], received[parent, shared : shared + 8, :]
    )
    under = below(upsample(shell))

    def take(face):
        code = links[face, 0, me]
        slot = jnp.maximum(code, 0)
        plane = unpack_face(
            received[slot, plane_at : plane_at + 8, :],
            received[slot, shared : shared + 8, :],
            32,
            face,
        )
        return {q: jnp.where(code >= 0, plane[q], under[face // 2][q]) for q in plane}

    return merge_ghosts(take)


def middle_kernel(
    received, from_low, from_high, c_post, c_start, c_weights, f_post, f_start, f_weights,
    coarse_links, fine_links, parents, out, coarse_new, state, post, octs,
):
    me = lax.axis_index("dev")

    def coarse_ghost(face):
        code = coarse_links[face, 0, me]
        slot = jnp.maximum(code, 0)
        first = received[slot, 0:8, :]
        second = received[slot, 16:24, :]
        if face in (2, 3):
            beside = from_low if face == 2 else from_high
            first = jnp.where(code == -2, beside[0, 0:8, :], first)
            second = jnp.where(code == -2, beside[0, 8:16, :], second)
        plane = unpack_face(first, second, 0, face)
        return {q: jnp.where(code == -1, inflow_value(q), plane[q]) for q in plane}

    new = stream(
        lambda q: c_post[q], lambda q: c_start[q], lambda q: c_weights[q], merge_ghosts(coarse_ghost)
    )
    for q in range(19):
        coarse_new[q] = new[q]
    old_density, old_u = moments([c_start[q] for q in range(19)])
    density, u = moments(new)
    mid = [0.5 * (old_density + density)] + [0.5 * (a + b) for a, b in zip(old_u, u)]
    store_octants(mid, octs)
    ghosts = fine_ghosts(received, fine_links, parents, me, 8, 16, 24)
    new = stream(lambda q: f_post[q], lambda q: f_start[q], lambda q: f_weights[q], ghosts)
    for q in range(19):
        state[q] = new[q]
    after = collide(new, OMEGA_FINE)
    for q in range(19):
        post[q] = after[q]
    for face in range(6):
        give_face(after, face, fine_links[face, 0, me], me, out, 0, 8, 32)
    give_octants(octs, parents, out, 16, 8)


def last_kernel(received, f_post, f_start, f_weights, fine_links, parents, out, state):
    me = lax.axis_index("dev")
    ghosts = fine_ghosts(received, fine_links, parents, me, 0, 8, 16)
    new = stream(lambda q: f_post[q], lambda q: f_start[q], lambda q: f_weights[q], ghosts)
    for q in range(19):
        state[q] = new[q]
    first, second = restrict(new)
    parent = parents[0, 0, me]
    out[parent, 0:8, :] = first
    out[parent, 8:16, :] = second


def finish_kernel(state, coarse_new, parents, fine_out, base, children):
    me = lax.axis_index("dev")
    for q in range(19):
        store_cells(fine_out, q, state[q])
    for o in range(8):
        children[o] = -1

    def note(d, carry):
        @pl.when(parents[0, 0, d] == me)
        def _():
            children[parents[1, 0, d]] = d

        return carry

    lax.fori_loop(0, 32, note, 0)
    covered = cover(children)
    new = load(coarse_new)
    density, u = moments(new)
    own = equilibrium(density, u, range(19))
    for q in range(19):
        base[q] = jnp.where(covered, new[q] - own[q], new[q])


def cover(children):
    low = (iota((8, 128), 1) & 15) < 8
    tiles = [[None, None], [None, None]]
    for ox in range(2):
        for oy in range(2):
            o = 4 * ox + 2 * oy
            tiles[ox][oy] = jnp.where(low, children[o], children[o + 1])
    return join(tiles) >= 0


def coarse_kernel(received, base, children, coarse_out):
    low = (iota((8, 128), 1) & 15) < 8
    tiles = [[[None, None], [None, None]] for _ in range(4)]
    for ox in range(2):
        for oy in range(2):
            o = 4 * ox + 2 * oy
            near = jnp.maximum(children[o], 0)
            far = jnp.maximum(children[o + 1], 0)
            for k in range(2):
                a = received[near, 8 * k : 8 * k + 8, :]
                b = received[far, 8 * k : 8 * k + 8, :]
                tiles[2 * k][ox][oy] = jnp.where(low, a, pltpu.roll(b, 8, 1))
                tiles[2 * k + 1][ox][oy] = jnp.where(low, pltpu.roll(a, 120, 1), b)
    density, jx, jy, jz = [join(t) for t in tiles]
    covered = cover(children)
    density = jnp.where(covered, density, 1.0)
    inverse = 1.0 / density
    fine_eq = equilibrium(density, [jx * inverse, jy * inverse, jz * inverse], range(19))
    for q in range(19):
        store_cells(coarse_out, q, base[q] + jnp.where(covered, fine_eq[q], 0.0))


VMEM = pl.BlockSpec(memory_space=pltpu.VMEM)
SMEM = pl.BlockSpec(memory_space=pltpu.SMEM)
PARAMS = pltpu.CompilerParams(vmem_limit_bytes=24 * 1024 * 1024)


def call(kernel, outs, ins, smem=(), scratch=(), name=None):
    ints = [not isinstance(s, tuple) for s in outs]
    return pl.pallas_call(
        kernel,
        out_shape=[
            jax.ShapeDtypeStruct((s,), jnp.int32) if i else jax.ShapeDtypeStruct(s, F32)
            for s, i in zip(outs, ints)
        ],
        in_specs=[SMEM if i in smem else VMEM for i in range(len(ins))],
        out_specs=[SMEM if i else VMEM for i in ints],
        scratch_shapes=list(scratch),
        compiler_params=PARAMS,
        cost_estimate=pl.CostEstimate(
            flops=2_000_000, bytes_accessed=2_000_000, transcendentals=0
        ),
        name=name,
    )(*ins)


def swap(value):
    return lax.all_to_all(value, "dev", split_axis=0, concat_axis=0, tiled=True)


def body(fine_state, coarse_state, fine_depth, coarse_depth, fine_links, coarse_links, parents):
    count = lax.axis_size("group")
    fine_state, coarse_state = fine_state.reshape(CELL_ROWS), coarse_state.reshape(CELL_ROWS)
    fine_depth, coarse_depth = fine_depth.reshape(32, 128), coarse_depth.reshape(32, 128)
    fine_links = fine_links.transpose(2, 0, 1)
    coarse_links = coarse_links.transpose(2, 0, 1)
    parents = parents.transpose(2, 0, 1)
    octs = pltpu.VMEM((8, 16, 128), F32)
    sent, region = call(
        send_kernel,
        [(32, SLOT1, 128), (2, 16, 128)],
        [coarse_state, fine_state, coarse_links, fine_links, parents],
        smem=(2, 3, 4),
        scratch=[octs],
        name="send",
    )
    up = [(i, i + 1) for i in range(count - 1)]
    down = [(b, a) for a, b in up]
    received = swap(sent)
    from_low = lax.ppermute(region[1:2], "group", up)
    from_high = lax.ppermute(region[0:1], "group", down)

    def prepare(state, depth, omega, name):
        def kernel(*refs):
            prepare_kernel(*refs, omega=omega)

        return call(kernel, [FIELD, FIELD, FIELD], [state, depth], name=name)

    c_post, c_start, c_weights = prepare(coarse_state, coarse_depth, OMEGA_COARSE, "prepare_coarse")
    f_post, f_start, f_weights = prepare(fine_state, fine_depth, OMEGA_FINE, "prepare_fine")
    sent, coarse_new, state, post = call(
        middle_kernel,
        [(32, SLOT2, 128), FIELD, FIELD, FIELD],
        [
            received, from_low, from_high, c_post, c_start, c_weights, f_post, f_start, f_weights,
            coarse_links, fine_links, parents,
        ],
        smem=(9, 10, 11),
        scratch=[octs],
        name="middle",
    )
    received = swap(sent)
    sent, state = call(
        last_kernel,
        [(32, SLOT3, 128), FIELD],
        [received, post, state, f_weights, fine_links, parents],
        smem=(4, 5),
        name="last",
    )
    received = swap(sent)
    fine_out, base, children = call(
        finish_kernel,
        [CELL_ROWS, FIELD, 8],
        [state, coarse_new, parents],
        smem=(2,),
        name="finish",
    )
    (coarse_out,) = call(
        coarse_kernel,
        [CELL_ROWS],
        [received, base, children],
        smem=(2,),
        name="coarse",
    )
    return fine_out.reshape(1, 19, 4096), coarse_out.reshape(1, 19, 4096)


def solution(mesh):
    placed = (
        P(("group", "dev"), None, None),
        P(("group", "dev"), None, None),
        P(("group", "dev"), None),
        P(("group", "dev"), None),
        P("group", None, None),
        P("group", None, None),
        P("group", None, None),
    )
    return jax.shard_map(
        body,
        mesh=mesh,
        in_specs=placed,
        out_specs=(P(("group", "dev"), None, None), P(("group", "dev"), None, None)),
        check_vma=False,
    )
```

```python
import jax
import jax.numpy as jnp
from jax import lax
from jax.experimental import pallas as pl
from jax.experimental.pallas import tpu as pltpu
from jax.sharding import PartitionSpec as P

VELOCITIES = [
    (0, 0, 0),
    (1, 0, 0),
    (-1, 0, 0),
    (0, 1, 0),
    (0, -1, 0),
    (0, 0, 1),
    (0, 0, -1),
    (1, 1, 0),
    (-1, -1, 0),
    (1, -1, 0),
    (-1, 1, 0),
    (1, 0, 1),
    (-1, 0, -1),
    (1, 0, -1),
    (-1, 0, 1),
    (0, 1, 1),
    (0, -1, -1),
    (0, 1, -1),
    (0, -1, 1),
]
WEIGHTS = [1.0 / 3.0] + [1.0 / 18.0] * 6 + [1.0 / 36.0] * 12
OPPOSITE = [VELOCITIES.index((-v[0], -v[1], -v[2])) for v in VELOCITIES]
OUTGOING = [
    [q for q in range(19) if VELOCITIES[q][face // 2] == 2 * (face % 2) - 1] for face in range(6)
]
OMEGA_FINE = 1.25
OMEGA_COARSE = 1.0 / 0.65
INFLOW = 0.05
F32 = jnp.float32
FIELD = (19, 16, 256)
CELL_ROWS = (19, 32, 128)
SLOT1 = 32
SLOT2 = 24
SLOT3 = 16
FINE_LINKS, COARSE_LINKS, PARENT, CHILDREN, OCTANTS, CODES = 0, 8, 16, 24, 32, 64
COARSE_PARTS = ((0, 7), (7, 6), (13, 6))


def inflow_value(q):
    along = VELOCITIES[q][0] * INFLOW
    return WEIGHTS[q] * (1.0 + 3.0 * along + 4.5 * along * along - 1.5 * INFLOW * INFLOW)


def iota(shape, dim):
    return lax.broadcasted_iota(jnp.int32, shape, dim)


def tile(value, row, half):
    return value[8 * row : 8 * row + 8, 128 * half : 128 * half + 128]


def join(tiles):
    return jnp.concatenate([jnp.concatenate(line, axis=1) for line in tiles], axis=0)


def pick(value, index, axis):
    return jnp.take_along_axis(value, index, axis=axis, mode="promise_in_bounds")


def sums(f):
    density = f[0]
    for q in range(1, 19):
        density = density + f[q]
    momentum = []
    for axis in range(3):
        plus = [f[q] for q in range(19) if VELOCITIES[q][axis] == 1]
        minus = [f[q] for q in range(19) if VELOCITIES[q][axis] == -1]
        total = plus[0] - minus[0]
        for a, b in zip(plus[1:], minus[1:]):
            total = total + (a - b)
        momentum.append(total)
    return density, momentum


def moments(f):
    density, momentum = sums(f)
    inverse = 1.0 / density
    return density, [m * inverse for m in momentum]


def equilibrium(density, u, chosen):
    base = 1.0 - 1.5 * (u[0] * u[0] + u[1] * u[1] + u[2] * u[2])
    scaled = {}
    for q in chosen:
        if WEIGHTS[q] not in scaled:
            scaled[WEIGHTS[q]] = WEIGHTS[q] * density
    even, out = {}, {}
    for q in chosen:
        v = VELOCITIES[q]
        weight = scaled[WEIGHTS[q]]
        if q == 0:
            out[q] = weight * base
            continue
        lead = q if q % 2 == 1 else q - 1
        if lead not in even:
            along = None
            for axis in range(3):
                c = VELOCITIES[lead][axis]
                if c != 0:
                    if along is None:
                        along = u[axis]
                    else:
                        along = along + u[axis] if c > 0 else along - u[axis]
            even[lead] = (base + 4.5 * along * along, 3.0 * along)
        part, odd = even[lead]
        out[q] = weight * (part + odd) if q == lead else weight * (part - odd)
    return out


def collide(f, omega):
    density, u = moments(f)
    rest = equilibrium(density, u, range(19))
    return [(1.0 - omega) * f[q] + omega * rest[q] for q in range(19)]


def row_parts(top, bottom, lane, sub):
    both = jnp.where(sub < 4, jnp.broadcast_to(top, (8, 128)), jnp.broadcast_to(bottom, (8, 128)))
    return pick(both, 32 * (sub & 3) + (lane & 31), 1)


def pack_face(post, face):
    axis, side = face // 2, face % 2
    lane = iota((8, 128), 1)
    sub = iota((8, 128), 0)
    chosen = [post[q] for q in OUTGOING[face]]
    if axis == 0:
        at = 15 * side
        rows = [[f[at : at + 1, 128 * h : 128 * h + 128] for h in range(2)] for f in chosen]
        first = None
        for i in range(4):
            for half in range(2):
                line = jnp.broadcast_to(rows[i][half], (8, 128))
                first = line if first is None else jnp.where(sub == 2 * i + half, line, first)
        return first, row_parts(rows[4][0], rows[4][1], lane, sub)
    strips = []
    for f in chosen:
        for row in range(2):
            if axis == 1:
                strips.append(pick(tile(f, row, side), (lane & 15) + 112 * side, 1))
            else:
                index = (lane & 7) * 16 + 15 * side
                a = pick(tile(f, row, 0), index, 1)
                b = pick(tile(f, row, 1), index, 1)
                strips.append(jnp.where((lane & 15) < 8, a, b))
    first = strips[0]
    for t in range(1, 8):
        first = jnp.where((lane >> 4) == t, strips[t], first)
    second = jnp.where(((lane >> 4) & 1) == 0, strips[8], strips[9])
    return first, second


def unpack_face(first, second, offset, face):
    axis, side = face // 2, face % 2
    lane = iota((8, 128), 1)
    out = {}
    for i, q in enumerate(OUTGOING[face ^ 1]):
        if axis == 0:
            halves = []
            for half in range(2):
                if i < 4:
                    line = jnp.broadcast_to(first[2 * i + half : 2 * i + half + 1, :], (8, 128))
                else:
                    line = pick(pick(second, offset + (lane & 31), 1), 4 * half + (lane >> 5), 0)
                halves.append(line)
            out[q] = join([halves, halves])
            continue
        rows = []
        for row in range(2):
            source, base = (first, 16 * (2 * i + row)) if i < 4 else (second, offset + 16 * row)
            if axis == 1:
                piece = pick(source, base + (lane & 15), 1)
                rows.append([piece, piece])
            else:
                step = 1 if side == 0 else 15
                rows.append(
                    [
                        pick(source, base + ((8 * half + (lane >> 4) + step) & 15), 1)
                        for half in range(2)
                    ]
                )
        out[q] = join(rows)
    return out


def pack_shell(pair):
    lane = iota((8, 128), 1)
    sub = iota((8, 128), 0)
    part = lane & 31
    along_y = part + 96 * (part >> 4)
    which = part & 3
    along_z = (part >> 2) * 16 + 8 * (which >> 1) + 7 * (which & 1)
    segment = lane >> 5
    a, b = pair
    rows_a = row_parts(a[0:1, :], a[7:8, :], lane, sub)
    rows_b = row_parts(b[0:1, :], b[7:8, :], lane, sub)
    rest = pick(a, jnp.where(segment == 1, along_y, along_z), 1)
    first = jnp.where(segment == 0, rows_a, jnp.where(segment == 3, rows_b, rest))
    second = pick(b, jnp.where(segment == 2, along_y, along_z), 1)
    return first, second


def shifted(value, v):
    if v[0] != 0:
        value = pltpu.roll(value, v[0] % 16, 0)
    lanes = (16 * v[1] + v[2]) % 256
    if lanes != 0:
        value = pltpu.roll(value, lanes, 1)
    return value


def positions():
    row = iota((16, 256), 0)
    lane = iota((16, 256), 1)
    return row, lane >> 4, lane & 15


def wall_weights(depth):
    place = positions()
    solid = depth <= 0
    here = depth.astype(F32)
    out = [jnp.where(solid, 1.0, 0.0).astype(F32)]
    for q in range(1, 19):
        v = VELOCITIES[q]
        outside = []
        for axis in range(3):
            if v[axis] != 0:
                outside.append(place[axis] == (0 if v[axis] > 0 else 15))
        away = outside[0] if len(outside) == 1 else outside[0] | outside[1]
        there = shifted(here, v)
        wall = (there <= 0.0) & jnp.logical_not(away) & jnp.logical_not(solid)
        gap = jnp.where(wall, here - there, 1.0)
        own = jnp.where(wall, here, 1.0)
        far = own + own >= gap
        weight = jnp.where(far, 0.5 * gap, 2.0 * own) / jnp.where(far, own, gap)
        value = jnp.where(wall, weight, -1.0)
        if len(outside) == 2:
            value = jnp.where(outside[0] & outside[1], 1.0, value)
        out.append(value)
    return out


def stream(post, start, weights, ghosts):
    place = positions()
    solid = weights(0) > 0.5
    out = [jnp.where(solid, start(0), post(0))]
    for q in range(1, 19):
        v = VELOCITIES[q]
        own = post(q)
        value = own
        for axis in (1, 0, 2):
            if v[axis] != 0:
                edge = place[axis] == (15 if v[axis] > 0 else 0)
                value = jnp.where(edge, ghosts[axis][q], value)
        value = shifted(value, v)
        weight = weights(q)
        value = jnp.where(weight >= 0.0, own + weight * (post(OPPOSITE[q]) - own), value)
        out.append(jnp.where(solid, start(q), value))
    return out


def pack_octants(fields):
    low = (iota((8, 128), 1) & 15) < 8
    out = {}
    for ox in range(2):
        for oy in range(2):
            a, b, c, d = [tile(f, ox, oy) for f in fields]
            out[4 * ox + 2 * oy] = (
                jnp.where(low, a, pltpu.roll(b, 8, 1)),
                jnp.where(low, c, pltpu.roll(d, 8, 1)),
            )
            out[4 * ox + 2 * oy + 1] = (
                jnp.where(low, pltpu.roll(a, 120, 1), b),
                jnp.where(low, pltpu.roll(c, 120, 1), d),
            )
    return out


def below(first, second):
    lane = iota((8, 128), 1)
    sub = iota((8, 128), 0)
    z = lane & 15
    fields = [[], [], []]
    for k in range(4):
        other = k % 2
        inner = (z >> 1) + 8 * other
        base = 0 if k < 2 else 96
        tiles = [[None, None], [None, None]]
        for half in range(2):
            rows = pick(first, base + ((lane >> 5) & 1) * 16 + inner, 1)
            for row in range(2):
                tiles[row][half] = pick(rows, 2 * half + (lane >> 6) + 4 * (1 - row), 0)
        fields[0].append(join(tiles))
        rest, base = (first, 32) if k < 2 else (second, 64)
        for half in range(2):
            line = pick(rest, base + 16 * (1 - half) + inner, 1)
            for row in range(2):
                tiles[row][half] = pick(line, 4 * row + (sub >> 1), 0)
        fields[1].append(join(tiles))
        base += 32
        for half in range(2):
            y = 8 * half + (lane >> 4)
            far = 4 * (((y + 1) & 15) >> 1)
            near = 4 * (((y + 15) & 15) >> 1) + 1
            line = pick(rest, base + 2 * other + jnp.where(z == 15, far, near), 1)
            for row in range(2):
                tiles[row][half] = pick(line, 4 * row + (sub >> 1), 0)
        fields[2].append(join(tiles))
    out = []
    for axis in range(3):
        chosen = [q for q in range(19) if VELOCITIES[q][axis] != 0]
        out.append(equilibrium(fields[axis][0], fields[axis][1:], chosen))
    return out


def restrict(f):
    lane = iota((8, 128), 1)
    sub = iota((8, 128), 0)
    density, momentum = sums(f)
    index = ((lane >> 4) & 3) * 32 + (lane & 7) * 2
    even = (2 * sub) & 7
    packed = []
    for field in [density] + momentum:
        halves = []
        for half in range(2):
            lines = [
                jnp.where(
                    sub < 4,
                    pick(tile(field, 0, half), even + odd, 0),
                    pick(tile(field, 1, half), even + odd, 0),
                )
                for odd in range(2)
            ]
            line = lines[0] + lines[1]
            parts = [pick(line, index + step, 1) for step in (0, 1, 16, 17)]
            halves.append(0.125 * ((parts[0] + parts[1]) + (parts[2] + parts[3])))
        packed.append(jnp.where(lane < 64, halves[0], halves[1]))
    low = (lane & 15) < 8
    return jnp.where(low, packed[0], packed[1]), jnp.where(low, packed[2], packed[3])


def load(ref):
    return [ref[q] for q in range(19)]


def load_cells(ref, q):
    halves = [ref[q, pl.ds(half, 16, stride=2), :] for half in range(2)]
    return jnp.concatenate(halves, axis=1)


def store_cells(ref, q, value):
    for half in range(2):
        ref[q, pl.ds(half, 16, stride=2), :] = value[:, 128 * half : 128 * half + 128]


def store_octants(fields, octs):
    for o, pair in pack_octants(fields).items():
        first, second = pack_shell(pair)
        octs[o, 0:8, :] = first
        octs[o, 8:16, :] = second


def give_octants(octs, octant, out, at, shared):
    for d in range(32):
        o = octant(d)
        out[d, at : at + 8, :] = octs[o, 0:8, :]
        out[d, shared : shared + 8, 64:128] = octs[o, 8:16, 64:128]


def give_face(post, face, code, me, out, at, shared, lanes):
    first, second = pack_face(post, face)
    slot = jnp.where(code >= 0, code, me)
    out[slot, at : at + 8, :] = first
    out[slot, shared : shared + 8, lanes : lanes + 32] = second[:, lanes : lanes + 32]
    return first, second


def send_kernel(
    coarse_in, fine_in, coarse_table, fine_table, parent_table, out, region,
    coarse, fine, coarse_links, fine_links, parents, slots, octs, sems,
):
    fetch = [
        pltpu.make_async_copy(source, target, sems.at[i])
        for i, (source, target) in enumerate(
            (
                (coarse_in, coarse),
                (coarse_table, coarse_links),
                (fine_in, fine),
                (fine_table, fine_links),
                (parent_table, parents),
            )
        )
    ]
    for copy in fetch:
        copy.start()

    def put(part):
        rows = pl.ds(8 * part, 8)
        return pltpu.make_async_copy(slots.at[:, rows, :], out.at[:, rows, :], sems.at[5 + part])

    me = lax.axis_index("dev")
    fetch[0].wait()
    fetch[1].wait()
    f = [load_cells(coarse, q) for q in range(19)]
    density, u = moments(f)
    store_octants([density] + u, octs)
    post = collide(f, OMEGA_COARSE)
    for face in range(6):
        first, second = give_face(post, face, coarse_links[face, 0, me], me, slots, 0, 16, 0)
        if face in (2, 3):
            region[face - 2, 0:8, :] = first
            region[face - 2, 8:16, :] = second
    put(0).start()
    fetch[4].wait()
    give_octants(octs, lambda d: parents[1, 0, d], slots, 24, 16)
    put(3).start()
    fetch[2].wait()
    fetch[3].wait()
    post = collide([load_cells(fine, q) for q in range(19)], OMEGA_FINE)
    for face in range(6):
        give_face(post, face, fine_links[face, 0, me], me, slots, 8, 16, 32)
    put(1).start()
    put(2).start()
    for part in range(4):
        put(part).wait()


def prepare_kernel(state, depth, post, start, weights, *, omega):
    f = [load_cells(state, q) for q in range(19)]
    for q in range(19):
        start[q] = f[q]
    for q, value in enumerate(collide(f, omega)):
        post[q] = value
    halves = [depth[pl.ds(half, 16, stride=2), :] for half in range(2)]
    for q, value in enumerate(wall_weights(jnp.concatenate(halves, axis=1))):
        weights[q] = value


def codes_kernel(coarse_links, fine_links, parents, codes):
    me = lax.axis_index("dev")
    for face in range(6):
        codes[FINE_LINKS + face] = fine_links[face, 0, me]
        codes[COARSE_LINKS + face] = coarse_links[face, 0, me]
    codes[PARENT] = parents[0, 0, me]
    for o in range(8):
        codes[CHILDREN + o] = -1

    def note(d, carry):
        codes[OCTANTS + d] = parents[1, 0, d]

        @pl.when(parents[0, 0, d] == me)
        def _():
            codes[CHILDREN + parents[1, 0, d]] = d

        return carry

    lax.fori_loop(0, 32, note, 0)


def merge_ghosts(take):
    ghosts = [{}, {}, {}]
    for face in range(6):
        ghosts[face // 2].update(take(face))
    return ghosts


def fine_ghosts(received, codes, plane_at, shared, moment_at):
    parent = codes[PARENT]
    under = below(
        received[parent, moment_at : moment_at + 8, :], received[parent, shared : shared + 8, :]
    )

    def take(face):
        code = codes[FINE_LINKS + face]
        slot = jnp.maximum(code, 0)
        plane = unpack_face(
            received[slot, plane_at : plane_at + 8, :],
            received[slot, shared : shared + 8, :],
            32,
            face,
        )
        return {q: jnp.where(code >= 0, plane[q], under[face // 2][q]) for q in plane}

    return merge_ghosts(take)


def middle_kernel(
    received, from_low, from_high, c_post, c_start, c_weights, f_post, f_start, f_weights,
    codes, out, coarse_new, state, post, octs,
):
    me = lax.axis_index("dev")

    def coarse_ghost(face):
        code = codes[COARSE_LINKS + face]
        slot = jnp.maximum(code, 0)
        first = received[slot, 0:8, :]
        second = received[slot, 16:24, :]
        if face in (2, 3):
            beside = from_low if face == 2 else from_high
            first = jnp.where(code == -2, beside[0, 0:8, :], first)
            second = jnp.where(code == -2, beside[0, 8:16, :], second)
        plane = unpack_face(first, second, 0, face)
        return {q: jnp.where(code == -1, inflow_value(q), plane[q]) for q in plane}

    new = stream(
        lambda q: c_post[q], lambda q: c_start[q], lambda q: c_weights[q], merge_ghosts(coarse_ghost)
    )
    for q in range(19):
        coarse_new[q] = new[q]
    old_density, old_u = moments([c_start[q] for q in range(19)])
    density, u = moments(new)
    mid = [0.5 * (old_density + density)] + [0.5 * (a + b) for a, b in zip(old_u, u)]
    store_octants(mid, octs)
    ghosts = fine_ghosts(received, codes, 8, 16, 24)
    new = stream(lambda q: f_post[q], lambda q: f_start[q], lambda q: f_weights[q], ghosts)
    for q in range(19):
        state[q] = new[q]
    after = collide(new, OMEGA_FINE)
    for q in range(19):
        post[q] = after[q]
    for face in range(6):
        give_face(after, face, codes[FINE_LINKS + face], me, out, 0, 8, 32)
    give_octants(octs, lambda d: codes[OCTANTS + d], out, 16, 8)


def last_kernel(received, f_post, f_start, f_weights, codes, out, state, slot, sem):
    ghosts = fine_ghosts(received, codes, 0, 8, 16)
    new = stream(lambda q: f_post[q], lambda q: f_start[q], lambda q: f_weights[q], ghosts)
    first, second = restrict(new)
    slot[0:8, :] = first
    slot[8:16, :] = second
    copy = pltpu.make_async_copy(slot, out.at[codes[PARENT]], sem)
    copy.start()
    for q in range(19):
        state[q] = new[q]
    copy.wait()


def finish_kernel(state, coarse_new, codes, fine_out, base):
    for q in range(19):
        store_cells(fine_out, q, state[q])
    covered = cover(codes)
    new = load(coarse_new)
    density, u = moments(new)
    own = equilibrium(density, u, range(19))
    for q in range(19):
        base[q] = jnp.where(covered, new[q] - own[q], new[q])


def cover(codes):
    low = (iota((8, 128), 1) & 15) < 8
    tiles = [[None, None], [None, None]]
    for ox in range(2):
        for oy in range(2):
            o = 4 * ox + 2 * oy
            tiles[ox][oy] = jnp.where(low, codes[CHILDREN + o], codes[CHILDREN + o + 1])
    return join(tiles) >= 0


def coarse_kernel(received, base, codes, coarse_out, cells, sems):
    low = (iota((8, 128), 1) & 15) < 8
    tiles = [[[None, None], [None, None]] for _ in range(4)]
    for ox in range(2):
        for oy in range(2):
            o = 4 * ox + 2 * oy
            near = jnp.maximum(codes[CHILDREN + o], 0)
            far = jnp.maximum(codes[CHILDREN + o + 1], 0)
            for k in range(2):
                a = received[near, 8 * k : 8 * k + 8, :]
                b = received[far, 8 * k : 8 * k + 8, :]
                tiles[2 * k][ox][oy] = jnp.where(low, a, pltpu.roll(b, 8, 1))
                tiles[2 * k + 1][ox][oy] = jnp.where(low, pltpu.roll(a, 120, 1), b)
    density, jx, jy, jz = [join(t) for t in tiles]
    covered = cover(codes)
    density = jnp.where(covered, density, 1.0)
    inverse = 1.0 / density
    fine_eq = equilibrium(density, [jx * inverse, jy * inverse, jz * inverse], range(19))
    copies = []
    for i, (low_q, count) in enumerate(COARSE_PARTS):
        for q in range(low_q, low_q + count):
            store_cells(cells, q, base[q] + jnp.where(covered, fine_eq[q], 0.0))
        part = pl.ds(low_q, count)
        copies.append(pltpu.make_async_copy(cells.at[part], coarse_out.at[part], sems.at[i]))
        copies[-1].start()
    for copy in copies:
        copy.wait()


VMEM = pl.BlockSpec(memory_space=pltpu.VMEM)
SMEM = pl.BlockSpec(memory_space=pltpu.SMEM)
HBM = pl.BlockSpec(memory_space=pltpu.HBM)
SOME_VMEM = 24 * 1024 * 1024
MOST_VMEM = 60 * 1024 * 1024


OCTS = pltpu.VMEM((8, 16, 128), F32)
LINKS = pltpu.SMEM((6, 1, 32), jnp.int32)
SEND_SCRATCH = [
    pltpu.VMEM(CELL_ROWS, F32),
    pltpu.VMEM(CELL_ROWS, F32),
    LINKS,
    LINKS,
    pltpu.SMEM((2, 1, 32), jnp.int32),
    pltpu.VMEM((32, SLOT1, 128), F32),
    OCTS,
    pltpu.SemaphoreType.DMA((9,)),
]
LAST_SCRATCH = [pltpu.VMEM((SLOT3, 128), F32), pltpu.SemaphoreType.DMA]
COARSE_SCRATCH = [pltpu.VMEM(CELL_ROWS, F32), pltpu.SemaphoreType.DMA((len(COARSE_PARTS),))]


def call(kernel, outs, ins, smem=(), hbm=(), hbm_outs=(), scratch=(), vmem=SOME_VMEM, name=None):
    def space(i, scalars, far):
        return SMEM if scalars else HBM if i in far else VMEM

    ints = [not isinstance(s, tuple) for s in outs]
    return pl.pallas_call(
        kernel,
        out_shape=[
            jax.ShapeDtypeStruct((s,), jnp.int32) if i else jax.ShapeDtypeStruct(s, F32)
            for s, i in zip(outs, ints)
        ],
        in_specs=[space(i, i in smem, hbm) for i in range(len(ins))],
        out_specs=[space(i, scalars, hbm_outs) for i, scalars in enumerate(ints)],
        scratch_shapes=list(scratch),
        compiler_params=pltpu.CompilerParams(vmem_limit_bytes=vmem),
        cost_estimate=pl.CostEstimate(
            flops=2_000_000, bytes_accessed=2_000_000, transcendentals=0
        ),
        name=name,
    )(*ins)


def swap(value):
    return lax.all_to_all(value, "dev", split_axis=0, concat_axis=0, tiled=True)


def body(fine_state, coarse_state, fine_depth, coarse_depth, fine_links, coarse_links, parents):
    count = lax.axis_size("group")
    fine_state, coarse_state = fine_state.reshape(CELL_ROWS), coarse_state.reshape(CELL_ROWS)
    fine_depth, coarse_depth = fine_depth.reshape(32, 128), coarse_depth.reshape(32, 128)
    fine_links = fine_links.transpose(2, 0, 1)
    coarse_links = coarse_links.transpose(2, 0, 1)
    parents = parents.transpose(2, 0, 1)
    sent, region = call(
        send_kernel,
        [(32, SLOT1, 128), (2, 16, 128)],
        [coarse_state, fine_state, coarse_links, fine_links, parents],
        hbm=(0, 1, 2, 3, 4),
        hbm_outs=(0,),
        scratch=SEND_SCRATCH,
        vmem=MOST_VMEM,
        name="send",
    )
    up = [(i, i + 1) for i in range(count - 1)]
    down = [(b, a) for a, b in up]
    received = swap(sent)
    from_low = lax.ppermute(region[1:2], "group", up)
    from_high = lax.ppermute(region[0:1], "group", down)

    def prepare(state, depth, omega, name):
        def kernel(*refs):
            prepare_kernel(*refs, omega=omega)

        return call(kernel, [FIELD, FIELD, FIELD], [state, depth], name=name)

    c_post, c_start, c_weights = prepare(coarse_state, coarse_depth, OMEGA_COARSE, "prepare_coarse")
    f_post, f_start, f_weights = prepare(fine_state, fine_depth, OMEGA_FINE, "prepare_fine")
    (codes,) = call(
        codes_kernel, [CODES], [coarse_links, fine_links, parents], smem=(0, 1, 2), name="codes"
    )
    sent, coarse_new, state, post = call(
        middle_kernel,
        [(32, SLOT2, 128), FIELD, FIELD, FIELD],
        [
            received, from_low, from_high, c_post, c_start, c_weights, f_post, f_start, f_weights,
            codes,
        ],
        smem=(9,),
        scratch=[OCTS],
        name="middle",
    )
    received = swap(sent)
    sent, state = call(
        last_kernel,
        [(32, SLOT3, 128), FIELD],
        [received, post, state, f_weights, codes],
        smem=(4,),
        hbm_outs=(0,),
        scratch=LAST_SCRATCH,
        name="last",
    )
    received = swap(sent)
    fine_out, base = call(
        finish_kernel,
        [CELL_ROWS, FIELD],
        [state, coarse_new, codes],
        smem=(2,),
        name="finish",
    )
    (coarse_out,) = call(
        coarse_kernel,
        [CELL_ROWS],
        [received, base, codes],
        smem=(2,),
        hbm_outs=(0,),
        scratch=COARSE_SCRATCH,
        name="coarse",
    )
    return fine_out.reshape(1, 19, 4096), coarse_out.reshape(1, 19, 4096)


def solution(mesh):
    placed = (
        P(("group", "dev"), None, None),
        P(("group", "dev"), None, None),
        P(("group", "dev"), None),
        P(("group", "dev"), None),
        P("group", None, None),
        P("group", None, None),
        P("group", None, None),
    )
    return jax.shard_map(
        body,
        mesh=mesh,
        in_specs=placed,
        out_specs=(P(("group", "dev"), None, None), P(("group", "dev"), None, None)),
        check_vma=False,
    )
```

```python
import jax
import jax.numpy as jnp
from jax import lax
from jax.experimental import pallas as pl
from jax.experimental.pallas import tpu as pltpu
from jax.sharding import PartitionSpec as P

VELOCITIES = [
    (0, 0, 0),
    (1, 0, 0),
    (-1, 0, 0),
    (0, 1, 0),
    (0, -1, 0),
    (0, 0, 1),
    (0, 0, -1),
    (1, 1, 0),
    (-1, -1, 0),
    (1, -1, 0),
    (-1, 1, 0),
    (1, 0, 1),
    (-1, 0, -1),
    (1, 0, -1),
    (-1, 0, 1),
    (0, 1, 1),
    (0, -1, -1),
    (0, 1, -1),
    (0, -1, 1),
]
WEIGHTS = [1.0 / 3.0] + [1.0 / 18.0] * 6 + [1.0 / 36.0] * 12
OPPOSITE = [VELOCITIES.index((-v[0], -v[1], -v[2])) for v in VELOCITIES]
OUTGOING = [
    [q for q in range(19) if VELOCITIES[q][face // 2] == 2 * (face % 2) - 1] for face in range(6)
]
OMEGA_FINE = 1.25
OMEGA_COARSE = 1.0 / 0.65
INFLOW = 0.05
F32 = jnp.float32
FIELD = (19, 16, 256)
CELL_ROWS = (19, 32, 128)
SLOT1 = 32
SLOT2 = (32, 5, 4, 128)
SLOT3 = 16
FINE_LINKS, COARSE_LINKS, PARENT, CHILDREN, OCTANTS, CODES = 0, 8, 16, 24, 32, 64
COARSE_PARTS = ((0, 7), (7, 6), (13, 6))


def inflow_value(q):
    along = VELOCITIES[q][0] * INFLOW
    return WEIGHTS[q] * (1.0 + 3.0 * along + 4.5 * along * along - 1.5 * INFLOW * INFLOW)


def iota(shape, dim):
    return lax.broadcasted_iota(jnp.int32, shape, dim)


def tile(value, row, half):
    return value[8 * row : 8 * row + 8, 128 * half : 128 * half + 128]


def join(tiles):
    return jnp.concatenate([jnp.concatenate(line, axis=1) for line in tiles], axis=0)


def pick(value, index, axis):
    return jnp.take_along_axis(value, index, axis=axis, mode="promise_in_bounds")


def sums(f):
    density = f[0]
    for q in range(1, 19):
        density = density + f[q]
    momentum = []
    for axis in range(3):
        plus = [f[q] for q in range(19) if VELOCITIES[q][axis] == 1]
        minus = [f[q] for q in range(19) if VELOCITIES[q][axis] == -1]
        total = plus[0] - minus[0]
        for a, b in zip(plus[1:], minus[1:]):
            total = total + (a - b)
        momentum.append(total)
    return density, momentum


def moments(f):
    density, momentum = sums(f)
    inverse = 1.0 / density
    return density, [m * inverse for m in momentum]


def equilibrium(density, u, chosen):
    base = 1.0 - 1.5 * (u[0] * u[0] + u[1] * u[1] + u[2] * u[2])
    scaled = {}
    for q in chosen:
        if WEIGHTS[q] not in scaled:
            scaled[WEIGHTS[q]] = WEIGHTS[q] * density
    even, out = {}, {}
    for q in chosen:
        v = VELOCITIES[q]
        weight = scaled[WEIGHTS[q]]
        if q == 0:
            out[q] = weight * base
            continue
        lead = q if q % 2 == 1 else q - 1
        if lead not in even:
            along = None
            for axis in range(3):
                c = VELOCITIES[lead][axis]
                if c != 0:
                    if along is None:
                        along = u[axis]
                    else:
                        along = along + u[axis] if c > 0 else along - u[axis]
            even[lead] = (base + 4.5 * along * along, 3.0 * along)
        part, odd = even[lead]
        out[q] = weight * (part + odd) if q == lead else weight * (part - odd)
    return out


def collide(f, omega):
    density, u = moments(f)
    rest = equilibrium(density, u, range(19))
    return [(1.0 - omega) * f[q] + omega * rest[q] for q in range(19)]


def row_parts(top, bottom, lane, sub):
    both = jnp.where(sub < 4, jnp.broadcast_to(top, (8, 128)), jnp.broadcast_to(bottom, (8, 128)))
    return pick(both, 32 * (sub & 3) + (lane & 31), 1)


def pack_face(post, face):
    axis, side = face // 2, face % 2
    lane = iota((8, 128), 1)
    sub = iota((8, 128), 0)
    chosen = [post[q] for q in OUTGOING[face]]
    if axis == 0:
        at = 15 * side
        rows = [[f[at : at + 1, 128 * h : 128 * h + 128] for h in range(2)] for f in chosen]
        first = None
        for i in range(4):
            for half in range(2):
                line = jnp.broadcast_to(rows[i][half], (8, 128))
                first = line if first is None else jnp.where(sub == 2 * i + half, line, first)
        return first, row_parts(rows[4][0], rows[4][1], lane, sub)
    strips = []
    for f in chosen:
        for row in range(2):
            if axis == 1:
                strips.append(pick(tile(f, row, side), (lane & 15) + 112 * side, 1))
            else:
                index = (lane & 7) * 16 + 15 * side
                a = pick(tile(f, row, 0), index, 1)
                b = pick(tile(f, row, 1), index, 1)
                strips.append(jnp.where((lane & 15) < 8, a, b))
    first = strips[0]
    for t in range(1, 8):
        first = jnp.where((lane >> 4) == t, strips[t], first)
    second = jnp.where(((lane >> 4) & 1) == 0, strips[8], strips[9])
    return first, second


def unpack_face(first, second, offset, face):
    axis, side = face // 2, face % 2
    lane = iota((8, 128), 1)
    out = {}
    for i, q in enumerate(OUTGOING[face ^ 1]):
        if axis == 0:
            halves = []
            for half in range(2):
                if i < 4:
                    line = jnp.broadcast_to(first[2 * i + half : 2 * i + half + 1, :], (8, 128))
                else:
                    line = pick(pick(second, offset + (lane & 31), 1), 4 * half + (lane >> 5), 0)
                halves.append(line)
            out[q] = join([halves, halves])
            continue
        rows = []
        for row in range(2):
            source, base = (first, 16 * (2 * i + row)) if i < 4 else (second, offset + 16 * row)
            if axis == 1:
                piece = pick(source, base + (lane & 15), 1)
                rows.append([piece, piece])
            else:
                step = 1 if side == 0 else 15
                rows.append(
                    [
                        pick(source, base + ((8 * half + (lane >> 4) + step) & 15), 1)
                        for half in range(2)
                    ]
                )
        out[q] = join(rows)
    return out


def join_rows(upper, lower):
    return jnp.concatenate([upper, lower], axis=0)


def shell_places(lane):
    entry = lane - jnp.where(lane < 120, 96, 120)
    along_z = (1 + (entry >> 2)) * 16 + 8 * ((entry >> 1) & 1) + 7 * (entry & 1)
    part = lane & 31
    return jnp.where(lane < 96, part + 96 * (part >> 4), along_z)


def pack_thin_shell(pair):
    lane = iota((8, 128), 1)
    sub = iota((8, 128), 0)
    a, b = pair
    index = shell_places(lane) & 127
    first = (lane < 64) | ((lane >= 96) & (lane < 120))
    inside = jnp.where(first, pick(a, index, 1), pick(b, index, 1))
    entry = 8 + (lane & 15)
    rest = pick(b, (1 + (entry >> 2)) * 16 + 8 * ((entry >> 1) & 1) + 7 * (entry & 1), 1)
    block = ((lane >> 4) - 2) & 3
    rest = pick(rest, jnp.where(sub == 0, 1, 4) + block, 0)
    shared = jnp.where((sub == 0) | (sub == 7), rest, inside)
    rows = jnp.concatenate([a[0:1], a[7:8], b[0:1], b[7:8]], axis=0)
    return shared, rows


def unpack_thin_shell(shared, rows):
    lane = iota((8, 128), 1)
    sub = iota((8, 128), 0)
    rows = join_rows(rows, rows)
    edge = (lane & 15) + jnp.where(lane >= 112, 16, 0)
    z = lane & 15
    entry = 4 * ((lane >> 4) - 1) + 2 * (z >> 3) + jnp.where((z & 7) == 7, 1, 0)
    on_y = (lane < 16) | (lane >= 112)
    block = sub - jnp.where(sub > 3, 4, 1)
    moved = pick(pick(shared, jnp.where(sub <= 3, 0, 7), 0), (24 + 16 * block + entry) & 127, 1)
    out = []
    for k in range(2):
        start = 96 if k == 0 else 120
        tile_k = pick(shared, jnp.where(on_y, 32 + 32 * k + edge, start + entry) & 127, 1)
        if k == 1:
            tile_k = jnp.where(on_y | (entry < 8), tile_k, moved)
        line = pick(rows, 2 * k + jnp.where(sub == 7, 1, 0), 0)
        out.append(jnp.where((sub == 0) | (sub == 7), line, tile_k))
    return out


def pack_shell(pair):
    lane = iota((8, 128), 1)
    sub = iota((8, 128), 0)
    part = lane & 31
    along_y = part + 96 * (part >> 4)
    which = part & 3
    along_z = (part >> 2) * 16 + 8 * (which >> 1) + 7 * (which & 1)
    segment = lane >> 5
    a, b = pair
    rows_a = row_parts(a[0:1, :], a[7:8, :], lane, sub)
    rows_b = row_parts(b[0:1, :], b[7:8, :], lane, sub)
    rest = pick(a, jnp.where(segment == 1, along_y, along_z), 1)
    first = jnp.where(segment == 0, rows_a, jnp.where(segment == 3, rows_b, rest))
    second = pick(b, jnp.where(segment == 2, along_y, along_z), 1)
    return first, second


def shifted(value, v):
    if v[0] != 0:
        value = pltpu.roll(value, v[0] % 16, 0)
    lanes = (16 * v[1] + v[2]) % 256
    if lanes != 0:
        value = pltpu.roll(value, lanes, 1)
    return value


def positions():
    row = iota((16, 256), 0)
    lane = iota((16, 256), 1)
    return row, lane >> 4, lane & 15


def wall_weights(depth):
    place = positions()
    solid = depth <= 0
    here = depth.astype(F32)
    out = [jnp.where(solid, 1.0, 0.0).astype(F32)]
    for q in range(1, 19):
        v = VELOCITIES[q]
        outside = []
        for axis in range(3):
            if v[axis] != 0:
                outside.append(place[axis] == (0 if v[axis] > 0 else 15))
        away = outside[0] if len(outside) == 1 else outside[0] | outside[1]
        there = shifted(here, v)
        wall = (there <= 0.0) & jnp.logical_not(away) & jnp.logical_not(solid)
        gap = jnp.where(wall, here - there, 1.0)
        own = jnp.where(wall, here, 1.0)
        far = own + own >= gap
        weight = jnp.where(far, 0.5 * gap, 2.0 * own) / jnp.where(far, own, gap)
        value = jnp.where(wall, weight, -1.0)
        if len(outside) == 2:
            value = jnp.where(outside[0] & outside[1], 1.0, value)
        out.append(value)
    return out


def stream(post, start, weights, ghosts):
    place = positions()
    solid = weights(0) > 0.5
    out = [jnp.where(solid, start(0), post(0))]
    for q in range(1, 19):
        v = VELOCITIES[q]
        own = post(q)
        value = own
        for axis in (1, 0, 2):
            if v[axis] != 0:
                edge = place[axis] == (15 if v[axis] > 0 else 0)
                value = jnp.where(edge, ghosts[axis][q], value)
        value = shifted(value, v)
        weight = weights(q)
        value = jnp.where(weight >= 0.0, own + weight * (post(OPPOSITE[q]) - own), value)
        out.append(jnp.where(solid, start(q), value))
    return out


def pack_octants(fields):
    low = (iota((8, 128), 1) & 15) < 8
    out = {}
    for ox in range(2):
        for oy in range(2):
            a, b, c, d = [tile(f, ox, oy) for f in fields]
            out[4 * ox + 2 * oy] = (
                jnp.where(low, a, pltpu.roll(b, 8, 1)),
                jnp.where(low, c, pltpu.roll(d, 8, 1)),
            )
            out[4 * ox + 2 * oy + 1] = (
                jnp.where(low, pltpu.roll(a, 120, 1), b),
                jnp.where(low, pltpu.roll(c, 120, 1), d),
            )
    return out


def packed_lines(first, second):
    lane = iota((8, 128), 1)

    def at_x(k, half, inner):
        base = 0 if k < 2 else 96
        return pick(first, base + ((lane >> 5) & 1) * 16 + inner, 1)

    def row_of(k, half, side):
        return 2 * half + (lane >> 6) + 4 * side

    def at_y(k, side, inner):
        rest, base = (first, 32) if k < 2 else (second, 64)
        return pick(rest, base + 16 * side + inner, 1)

    def at_z(k, y, side):
        rest, base = (first, 64) if k < 2 else (second, 96)
        return pick(rest, base + 4 * y + 2 * (k % 2) + side, 1)

    return at_x, row_of, at_y, at_z


def tile_lines(tiles):
    lane = iota((8, 128), 1)

    def at_x(k, half, inner):
        return pick(tiles[k // 2], (4 * half + (lane >> 5)) * 16 + inner, 1)

    def row_of(k, half, side):
        return jnp.full((8, 128), 7 * side, jnp.int32)

    def at_y(k, side, inner):
        return pick(tiles[k // 2], 112 * side + inner, 1)

    def at_z(k, y, side):
        return pick(tiles[k // 2], 16 * y + 8 * (k % 2) + 7 * side, 1)

    return at_x, row_of, at_y, at_z


def below(lines):
    at_x, row_of, at_y, at_z = lines
    lane = iota((8, 128), 1)
    sub = iota((8, 128), 0)
    z = lane & 15
    fields = [[], [], []]
    for k in range(4):
        inner = (z >> 1) + 8 * (k % 2)
        tiles = [[None, None], [None, None]]
        for half in range(2):
            rows = at_x(k, half, inner)
            for row in range(2):
                tiles[row][half] = pick(rows, row_of(k, half, 1 - row), 0)
        fields[0].append(join(tiles))
        for half in range(2):
            line = at_y(k, 1 - half, inner)
            for row in range(2):
                tiles[row][half] = pick(line, 4 * row + (sub >> 1), 0)
        fields[1].append(join(tiles))
        for half in range(2):
            y = 8 * half + (lane >> 4)
            far = z == 15
            line = at_z(k, ((y + jnp.where(far, 1, 15)) & 15) >> 1, jnp.where(far, 0, 1))
            for row in range(2):
                tiles[row][half] = pick(line, 4 * row + (sub >> 1), 0)
        fields[2].append(join(tiles))
    out = []
    for axis in range(3):
        chosen = [q for q in range(19) if VELOCITIES[q][axis] != 0]
        out.append(equilibrium(fields[axis][0], fields[axis][1:], chosen))
    return out


def restrict(f):
    lane = iota((8, 128), 1)
    sub = iota((8, 128), 0)
    density, momentum = sums(f)
    index = ((lane >> 4) & 3) * 32 + (lane & 7) * 2
    even = (2 * sub) & 7
    packed = []
    for field in [density] + momentum:
        halves = []
        for half in range(2):
            lines = [
                jnp.where(
                    sub < 4,
                    pick(tile(field, 0, half), even + odd, 0),
                    pick(tile(field, 1, half), even + odd, 0),
                )
                for odd in range(2)
            ]
            line = lines[0] + lines[1]
            parts = [pick(line, index + step, 1) for step in (0, 1, 16, 17)]
            halves.append(0.125 * ((parts[0] + parts[1]) + (parts[2] + parts[3])))
        packed.append(jnp.where(lane < 64, halves[0], halves[1]))
    low = (lane & 15) < 8
    return jnp.where(low, packed[0], packed[1]), jnp.where(low, packed[2], packed[3])


def load(ref):
    return [ref[q] for q in range(19)]


def load_cells(ref, q):
    halves = [ref[q, pl.ds(half, 16, stride=2), :] for half in range(2)]
    return jnp.concatenate(halves, axis=1)


def store_cells(ref, q, value):
    for half in range(2):
        ref[q, pl.ds(half, 16, stride=2), :] = value[:, 128 * half : 128 * half + 128]


def store_octants(fields, octs):
    for o, pair in pack_octants(fields).items():
        first, second = pack_shell(pair)
        octs[o, 0:8, :] = first
        octs[o, 8:16, :] = second


def give_octants(octs, parents, out):
    for d in range(32):
        o = parents[1, 0, d]
        out[d, 24:32, :] = octs[o, 0:8, :]
        out[d, 16:24, 64:128] = octs[o, 8:16, 64:128]


def give_face(post, face, code, me, out, at, shared, lanes):
    first, second = pack_face(post, face)
    slot = jnp.where(code >= 0, code, me)
    out[slot, at : at + 8, :] = first
    out[slot, shared : shared + 8, lanes : lanes + 32] = second[:, lanes : lanes + 32]
    return first, second


def send_kernel(
    coarse_in, fine_in, coarse_table, fine_table, parent_table, out, region_out,
    coarse, fine, coarse_links, fine_links, parents, slots, region, octs, sems,
):
    fetch = [
        pltpu.make_async_copy(source, target, sems.at[i])
        for i, (source, target) in enumerate(
            (
                (coarse_in, coarse),
                (coarse_table, coarse_links),
                (fine_in, fine),
                (fine_table, fine_links),
                (parent_table, parents),
            )
        )
    ]
    for copy in fetch:
        copy.start()

    def put(part):
        rows = pl.ds(8 * part, 8)
        return pltpu.make_async_copy(slots.at[:, rows, :], out.at[:, rows, :], sems.at[5 + part])

    me = lax.axis_index("dev")
    fetch[0].wait()
    fetch[1].wait()
    f = [load_cells(coarse, q) for q in range(19)]
    density, u = moments(f)
    store_octants([density] + u, octs)
    post = collide(f, OMEGA_COARSE)
    for face in range(6):
        first, second = give_face(post, face, coarse_links[face, 0, me], me, slots, 0, 16, 0)
        if face in (2, 3):
            region[face - 2, 0:8, :] = first
            region[face - 2, 8:16, :] = second
    put(0).start()
    beside = pltpu.make_async_copy(region, region_out, sems.at[9])
    beside.start()
    fetch[4].wait()
    give_octants(octs, parents, slots)
    put(3).start()
    fetch[2].wait()
    fetch[3].wait()
    post = collide([load_cells(fine, q) for q in range(19)], OMEGA_FINE)
    for face in range(6):
        give_face(post, face, fine_links[face, 0, me], me, slots, 8, 16, 32)
    put(1).start()
    put(2).start()
    for part in range(4):
        put(part).wait()
    beside.wait()


def prepare_kernel(state, depth, post, start, weights, *, omega):
    f = [load_cells(state, q) for q in range(19)]
    for q in range(19):
        start[q] = f[q]
    for q, value in enumerate(collide(f, omega)):
        post[q] = value
    halves = [depth[pl.ds(half, 16, stride=2), :] for half in range(2)]
    for q, value in enumerate(wall_weights(jnp.concatenate(halves, axis=1))):
        weights[q] = value


def codes_kernel(coarse_links, fine_links, parents, codes):
    me = lax.axis_index("dev")
    for face in range(6):
        codes[FINE_LINKS + face] = fine_links[face, 0, me]
        codes[COARSE_LINKS + face] = coarse_links[face, 0, me]
    codes[PARENT] = parents[0, 0, me]
    for o in range(8):
        codes[CHILDREN + o] = -1

    def note(d, carry):
        codes[OCTANTS + d] = parents[1, 0, d]

        @pl.when(parents[0, 0, d] == me)
        def _():
            codes[CHILDREN + parents[1, 0, d]] = d

        return carry

    lax.fori_loop(0, 32, note, 0)


def merge_ghosts(take):
    ghosts = [{}, {}, {}]
    for face in range(6):
        ghosts[face // 2].update(take(face))
    return ghosts


def fine_ghosts(codes, plane_of, lanes, under):
    def take(face):
        code = codes[FINE_LINKS + face]
        first, second = plane_of(jnp.maximum(code, 0))
        plane = unpack_face(first, second, lanes, face)
        return {q: jnp.where(code >= 0, plane[q], under[face // 2][q]) for q in plane}

    return merge_ghosts(take)


def middle_kernel(
    received, from_low, from_high, c_post, c_start, c_weights, f_post, f_start, f_weights,
    codes, out, coarse_new, state, post, octs,
):
    me = lax.axis_index("dev")

    def coarse_ghost(face):
        code = codes[COARSE_LINKS + face]
        slot = jnp.maximum(code, 0)
        first = received[slot, 0:8, :]
        second = received[slot, 16:24, :]
        if face in (2, 3):
            beside = from_low if face == 2 else from_high
            first = jnp.where(code == -2, beside[0, 0:8, :], first)
            second = jnp.where(code == -2, beside[0, 8:16, :], second)
        plane = unpack_face(first, second, 0, face)
        return {q: jnp.where(code == -1, inflow_value(q), plane[q]) for q in plane}

    new = stream(
        lambda q: c_post[q], lambda q: c_start[q], lambda q: c_weights[q], merge_ghosts(coarse_ghost)
    )
    for q in range(19):
        coarse_new[q] = new[q]
    old_density, old_u = moments([c_start[q] for q in range(19)])
    density, u = moments(new)
    mid = [0.5 * (old_density + density)] + [0.5 * (a + b) for a, b in zip(old_u, u)]
    for o, pair in pack_octants(mid).items():
        shared, rows = pack_thin_shell(pair)
        octs[o, 0] = shared[0:4]
        octs[o, 1] = shared[4:8]
        octs[o, 2] = rows
    parent = codes[PARENT]
    under = below(packed_lines(received[parent, 24:32, :], received[parent, 16:24, :]))
    ghosts = fine_ghosts(
        codes, lambda d: (received[d, 8:16, :], received[d, 16:24, :]), 32, under
    )
    new = stream(lambda q: f_post[q], lambda q: f_start[q], lambda q: f_weights[q], ghosts)
    for q in range(19):
        state[q] = new[q]
    after = collide(new, OMEGA_FINE)
    for q in range(19):
        post[q] = after[q]
    for face in range(6):
        first, second = pack_face(after, face)
        code = codes[FINE_LINKS + face]
        slot = jnp.where(code >= 0, code, me)
        for part in range(2):
            out[slot, part] = first[4 * part : 4 * part + 4]
            out[slot, 2 + part, :, 0:32] = second[4 * part : 4 * part + 4, 0:32]
    for d in range(32):
        o = codes[OCTANTS + d]
        out[d, 2, :, 32:128] = octs[o, 0, :, 32:128]
        out[d, 3, :, 32:128] = octs[o, 1, :, 32:128]
        out[d, 4] = octs[o, 2]


def last_kernel(received, f_post, f_start, f_weights, codes, out, state, slot, sem):
    def rows_of(d, part):
        return join_rows(received[d, part], received[d, part + 1])

    parent = codes[PARENT]
    under = below(tile_lines(unpack_thin_shell(rows_of(parent, 2), received[parent, 4])))
    ghosts = fine_ghosts(codes, lambda d: (rows_of(d, 0), rows_of(d, 2)), 0, under)
    new = stream(lambda q: f_post[q], lambda q: f_start[q], lambda q: f_weights[q], ghosts)
    first, second = restrict(new)
    slot[0:8, :] = first
    slot[8:16, :] = second
    copy = pltpu.make_async_copy(slot, out.at[parent], sem)
    copy.start()
    for q in range(19):
        state[q] = new[q]
    copy.wait()


def finish_kernel(state, coarse_new, codes, fine_out, base):
    for q in range(19):
        store_cells(fine_out, q, state[q])
    covered = cover(codes)
    new = load(coarse_new)
    density, u = moments(new)
    own = equilibrium(density, u, range(19))
    for q in range(19):
        base[q] = jnp.where(covered, new[q] - own[q], new[q])


def cover(codes):
    low = (iota((8, 128), 1) & 15) < 8
    tiles = [[None, None], [None, None]]
    for ox in range(2):
        for oy in range(2):
            o = 4 * ox + 2 * oy
            tiles[ox][oy] = jnp.where(low, codes[CHILDREN + o], codes[CHILDREN + o + 1])
    return join(tiles) >= 0


def coarse_kernel(received, base, codes, coarse_out, cells, sems):
    low = (iota((8, 128), 1) & 15) < 8
    tiles = [[[None, None], [None, None]] for _ in range(4)]
    for ox in range(2):
        for oy in range(2):
            o = 4 * ox + 2 * oy
            near = jnp.maximum(codes[CHILDREN + o], 0)
            far = jnp.maximum(codes[CHILDREN + o + 1], 0)
            for k in range(2):
                a = received[near, 8 * k : 8 * k + 8, :]
                b = received[far, 8 * k : 8 * k + 8, :]
                tiles[2 * k][ox][oy] = jnp.where(low, a, pltpu.roll(b, 8, 1))
                tiles[2 * k + 1][ox][oy] = jnp.where(low, pltpu.roll(a, 120, 1), b)
    density, jx, jy, jz = [join(t) for t in tiles]
    covered = cover(codes)
    density = jnp.where(covered, density, 1.0)
    inverse = 1.0 / density
    fine_eq = equilibrium(density, [jx * inverse, jy * inverse, jz * inverse], range(19))
    copies = []
    for i, (low_q, count) in enumerate(COARSE_PARTS):
        for q in range(low_q, low_q + count):
            store_cells(cells, q, base[q] + jnp.where(covered, fine_eq[q], 0.0))
        part = pl.ds(low_q, count)
        copies.append(pltpu.make_async_copy(cells.at[part], coarse_out.at[part], sems.at[i]))
        copies[-1].start()
    for copy in copies:
        copy.wait()


VMEM = pl.BlockSpec(memory_space=pltpu.VMEM)
SMEM = pl.BlockSpec(memory_space=pltpu.SMEM)
HBM = pl.BlockSpec(memory_space=pltpu.HBM)
SOME_VMEM = 24 * 1024 * 1024
MOST_VMEM = 60 * 1024 * 1024


OCTS = pltpu.VMEM((8, 16, 128), F32)
LINKS = pltpu.SMEM((6, 1, 32), jnp.int32)
SEND_SCRATCH = [
    pltpu.VMEM(CELL_ROWS, F32),
    pltpu.VMEM(CELL_ROWS, F32),
    LINKS,
    LINKS,
    pltpu.SMEM((2, 1, 32), jnp.int32),
    pltpu.VMEM((32, SLOT1, 128), F32),
    pltpu.VMEM((2, 16, 128), F32),
    OCTS,
    pltpu.SemaphoreType.DMA((10,)),
]
LAST_SCRATCH = [pltpu.VMEM((SLOT3, 128), F32), pltpu.SemaphoreType.DMA]
COARSE_SCRATCH = [pltpu.VMEM(CELL_ROWS, F32), pltpu.SemaphoreType.DMA((len(COARSE_PARTS),))]


def call(kernel, outs, ins, smem=(), hbm=(), hbm_outs=(), scratch=(), vmem=SOME_VMEM, name=None):
    def space(i, scalars, far):
        return SMEM if scalars else HBM if i in far else VMEM

    ints = [not isinstance(s, tuple) for s in outs]
    return pl.pallas_call(
        kernel,
        out_shape=[
            jax.ShapeDtypeStruct((s,), jnp.int32) if i else jax.ShapeDtypeStruct(s, F32)
            for s, i in zip(outs, ints)
        ],
        in_specs=[space(i, i in smem, hbm) for i in range(len(ins))],
        out_specs=[space(i, scalars, hbm_outs) for i, scalars in enumerate(ints)],
        scratch_shapes=list(scratch),
        compiler_params=pltpu.CompilerParams(vmem_limit_bytes=vmem),
        cost_estimate=pl.CostEstimate(
            flops=2_000_000, bytes_accessed=2_000_000, transcendentals=0
        ),
        name=name,
    )(*ins)


def swap(value):
    return lax.all_to_all(value, "dev", split_axis=0, concat_axis=0, tiled=True)


def body(fine_state, coarse_state, fine_depth, coarse_depth, fine_links, coarse_links, parents):
    count = lax.axis_size("group")
    fine_state, coarse_state = fine_state.reshape(CELL_ROWS), coarse_state.reshape(CELL_ROWS)
    fine_depth, coarse_depth = fine_depth.reshape(32, 128), coarse_depth.reshape(32, 128)
    fine_links = fine_links.transpose(2, 0, 1)
    coarse_links = coarse_links.transpose(2, 0, 1)
    parents = parents.transpose(2, 0, 1)
    sent, region = call(
        send_kernel,
        [(32, SLOT1, 128), (2, 16, 128)],
        [coarse_state, fine_state, coarse_links, fine_links, parents],
        hbm=(0, 1, 2, 3, 4),
        hbm_outs=(0, 1),
        scratch=SEND_SCRATCH,
        vmem=MOST_VMEM,
        name="send",
    )
    up = [(i, i + 1) for i in range(count - 1)]
    down = [(b, a) for a, b in up]
    received = swap(sent)
    from_low = lax.ppermute(region[1:2], "group", up)
    from_high = lax.ppermute(region[0:1], "group", down)

    def prepare(state, depth, omega, name):
        def kernel(*refs):
            prepare_kernel(*refs, omega=omega)

        return call(kernel, [FIELD, FIELD, FIELD], [state, depth], name=name)

    c_post, c_start, c_weights = prepare(coarse_state, coarse_depth, OMEGA_COARSE, "prepare_coarse")
    f_post, f_start, f_weights = prepare(fine_state, fine_depth, OMEGA_FINE, "prepare_fine")
    (codes,) = call(
        codes_kernel, [CODES], [coarse_links, fine_links, parents], smem=(0, 1, 2), name="codes"
    )
    sent, coarse_new, state, post = call(
        middle_kernel,
        [SLOT2, FIELD, FIELD, FIELD],
        [
            received, from_low, from_high, c_post, c_start, c_weights, f_post, f_start, f_weights,
            codes,
        ],
        smem=(9,),
        scratch=[pltpu.VMEM((8, 3, 4, 128), F32)],
        name="middle",
    )
    received = swap(sent)
    sent, state = call(
        last_kernel,
        [(32, SLOT3, 128), FIELD],
        [received, post, state, f_weights, codes],
        smem=(4,),
        hbm_outs=(0,),
        scratch=LAST_SCRATCH,
        name="last",
    )
    received = swap(sent)
    fine_out, base = call(
        finish_kernel,
        [CELL_ROWS, FIELD],
        [state, coarse_new, codes],
        smem=(2,),
        name="finish",
    )
    (coarse_out,) = call(
        coarse_kernel,
        [CELL_ROWS],
        [received, base, codes],
        smem=(2,),
        hbm_outs=(0,),
        scratch=COARSE_SCRATCH,
        name="coarse",
    )
    return fine_out.reshape(1, 19, 4096), coarse_out.reshape(1, 19, 4096)


def solution(mesh):
    placed = (
        P(("group", "dev"), None, None),
        P(("group", "dev"), None, None),
        P(("group", "dev"), None),
        P(("group", "dev"), None),
        P("group", None, None),
        P("group", None, None),
        P("group", None, None),
    )
    return jax.shard_map(
        body,
        mesh=mesh,
        in_specs=placed,
        out_specs=(P(("group", "dev"), None, None), P(("group", "dev"), None, None)),
        check_vma=False,
    )
```

```python
import jax
import jax.numpy as jnp
from jax import lax
from jax.experimental import pallas as pl
from jax.experimental.pallas import tpu as pltpu
from jax.sharding import PartitionSpec as P

VELOCITIES = [
    (0, 0, 0),
    (1, 0, 0),
    (-1, 0, 0),
    (0, 1, 0),
    (0, -1, 0),
    (0, 0, 1),
    (0, 0, -1),
    (1, 1, 0),
    (-1, -1, 0),
    (1, -1, 0),
    (-1, 1, 0),
    (1, 0, 1),
    (-1, 0, -1),
    (1, 0, -1),
    (-1, 0, 1),
    (0, 1, 1),
    (0, -1, -1),
    (0, 1, -1),
    (0, -1, 1),
]
WEIGHTS = [1.0 / 3.0] + [1.0 / 18.0] * 6 + [1.0 / 36.0] * 12
OPPOSITE = [VELOCITIES.index((-v[0], -v[1], -v[2])) for v in VELOCITIES]
OUTGOING = [
    [q for q in range(19) if VELOCITIES[q][face // 2] == 2 * (face % 2) - 1] for face in range(6)
]
OMEGA_FINE = 1.25
OMEGA_COARSE = 1.0 / 0.65
INFLOW = 0.05
F32 = jnp.float32
FIELD = (19, 16, 256)
CELL_ROWS = (19, 32, 128)
SLOT1 = 32
SLOT2 = (32, 5, 4, 128)
SLOT3 = 16
FINE_LINKS, COARSE_LINKS, PARENT, CHILDREN, OCTANTS, CODES = 0, 8, 16, 24, 32, 64


def inflow_value(q):
    along = VELOCITIES[q][0] * INFLOW
    return WEIGHTS[q] * (1.0 + 3.0 * along + 4.5 * along * along - 1.5 * INFLOW * INFLOW)


def iota(shape, dim):
    return lax.broadcasted_iota(jnp.int32, shape, dim)


def tile(value, row, half):
    return value[8 * row : 8 * row + 8, 128 * half : 128 * half + 128]


def join(tiles):
    return jnp.concatenate([jnp.concatenate(line, axis=1) for line in tiles], axis=0)


def pick(value, index, axis):
    return jnp.take_along_axis(value, index, axis=axis, mode="promise_in_bounds")


def sums(f):
    density = f[0]
    for q in range(1, 19):
        density = density + f[q]
    momentum = []
    for axis in range(3):
        plus = [f[q] for q in range(19) if VELOCITIES[q][axis] == 1]
        minus = [f[q] for q in range(19) if VELOCITIES[q][axis] == -1]
        total = plus[0] - minus[0]
        for a, b in zip(plus[1:], minus[1:]):
            total = total + (a - b)
        momentum.append(total)
    return density, momentum


def moments(f):
    density, momentum = sums(f)
    inverse = 1.0 / density
    return density, [m * inverse for m in momentum]


def equilibrium(density, u, chosen):
    base = 1.0 - 1.5 * (u[0] * u[0] + u[1] * u[1] + u[2] * u[2])
    scaled = {}
    for q in chosen:
        if WEIGHTS[q] not in scaled:
            scaled[WEIGHTS[q]] = WEIGHTS[q] * density
    even, out = {}, {}
    for q in chosen:
        v = VELOCITIES[q]
        weight = scaled[WEIGHTS[q]]
        if q == 0:
            out[q] = weight * base
            continue
        lead = q if q % 2 == 1 else q - 1
        if lead not in even:
            along = None
            for axis in range(3):
                c = VELOCITIES[lead][axis]
                if c != 0:
                    if along is None:
                        along = u[axis]
                    else:
                        along = along + u[axis] if c > 0 else along - u[axis]
            even[lead] = (base + 4.5 * along * along, 3.0 * along)
        part, odd = even[lead]
        out[q] = weight * (part + odd) if q == lead else weight * (part - odd)
    return out


def collide(f, omega):
    density, u = moments(f)
    rest = equilibrium(density, u, range(19))
    return [(1.0 - omega) * f[q] + omega * rest[q] for q in range(19)]


def row_parts(top, bottom, lane, sub):
    both = jnp.where(sub < 4, jnp.broadcast_to(top, (8, 128)), jnp.broadcast_to(bottom, (8, 128)))
    return pick(both, 32 * (sub & 3) + (lane & 31), 1)


def pack_face(post, face):
    axis, side = face // 2, face % 2
    lane = iota((8, 128), 1)
    sub = iota((8, 128), 0)
    chosen = [post[q] for q in OUTGOING[face]]
    if axis == 0:
        at = 15 * side
        rows = [[f[at : at + 1, 128 * h : 128 * h + 128] for h in range(2)] for f in chosen]
        first = None
        for i in range(4):
            for half in range(2):
                line = jnp.broadcast_to(rows[i][half], (8, 128))
                first = line if first is None else jnp.where(sub == 2 * i + half, line, first)
        return first, row_parts(rows[4][0], rows[4][1], lane, sub)
    strips = []
    for f in chosen:
        for row in range(2):
            if axis == 1:
                strips.append(pick(tile(f, row, side), (lane & 15) + 112 * side, 1))
            else:
                index = (lane & 7) * 16 + 15 * side
                a = pick(tile(f, row, 0), index, 1)
                b = pick(tile(f, row, 1), index, 1)
                strips.append(jnp.where((lane & 15) < 8, a, b))
    first = strips[0]
    for t in range(1, 8):
        first = jnp.where((lane >> 4) == t, strips[t], first)
    second = jnp.where(((lane >> 4) & 1) == 0, strips[8], strips[9])
    return first, second


def unpack_face(first, second, offset, face):
    axis, side = face // 2, face % 2
    lane = iota((8, 128), 1)
    out = {}
    for i, q in enumerate(OUTGOING[face ^ 1]):
        if axis == 0:
            halves = []
            for half in range(2):
                if i < 4:
                    line = jnp.broadcast_to(first[2 * i + half : 2 * i + half + 1, :], (8, 128))
                else:
                    line = pick(pick(second, offset + (lane & 31), 1), 4 * half + (lane >> 5), 0)
                halves.append(line)
            out[q] = join([halves, halves])
            continue
        rows = []
        for row in range(2):
            source, base = (first, 16 * (2 * i + row)) if i < 4 else (second, offset + 16 * row)
            if axis == 1:
                piece = pick(source, base + (lane & 15), 1)
                rows.append([piece, piece])
            else:
                step = 1 if side == 0 else 15
                rows.append(
                    [
                        pick(source, base + ((8 * half + (lane >> 4) + step) & 15), 1)
                        for half in range(2)
                    ]
                )
        out[q] = join(rows)
    return out


def join_rows(upper, lower):
    return jnp.concatenate([upper, lower], axis=0)


def shell_places(lane):
    entry = lane - jnp.where(lane < 120, 96, 120)
    along_z = (1 + (entry >> 2)) * 16 + 8 * ((entry >> 1) & 1) + 7 * (entry & 1)
    part = lane & 31
    return jnp.where(lane < 96, part + 96 * (part >> 4), along_z)


def pack_thin_shell(pair):
    lane = iota((8, 128), 1)
    sub = iota((8, 128), 0)
    a, b = pair
    index = shell_places(lane) & 127
    first = (lane < 64) | ((lane >= 96) & (lane < 120))
    inside = jnp.where(first, pick(a, index, 1), pick(b, index, 1))
    entry = 8 + (lane & 15)
    rest = pick(b, (1 + (entry >> 2)) * 16 + 8 * ((entry >> 1) & 1) + 7 * (entry & 1), 1)
    block = ((lane >> 4) - 2) & 3
    rest = pick(rest, jnp.where(sub == 0, 1, 4) + block, 0)
    shared = jnp.where((sub == 0) | (sub == 7), rest, inside)
    rows = jnp.concatenate([a[0:1], a[7:8], b[0:1], b[7:8]], axis=0)
    return shared, rows


def unpack_thin_shell(shared, rows):
    lane = iota((8, 128), 1)
    sub = iota((8, 128), 0)
    rows = join_rows(rows, rows)
    edge = (lane & 15) + jnp.where(lane >= 112, 16, 0)
    z = lane & 15
    entry = 4 * ((lane >> 4) - 1) + 2 * (z >> 3) + jnp.where((z & 7) == 7, 1, 0)
    on_y = (lane < 16) | (lane >= 112)
    block = sub - jnp.where(sub > 3, 4, 1)
    moved = pick(pick(shared, jnp.where(sub <= 3, 0, 7), 0), (24 + 16 * block + entry) & 127, 1)
    out = []
    for k in range(2):
        start = 96 if k == 0 else 120
        tile_k = pick(shared, jnp.where(on_y, 32 + 32 * k + edge, start + entry) & 127, 1)
        if k == 1:
            tile_k = jnp.where(on_y | (entry < 8), tile_k, moved)
        line = pick(rows, 2 * k + jnp.where(sub == 7, 1, 0), 0)
        out.append(jnp.where((sub == 0) | (sub == 7), line, tile_k))
    return out


def pack_shell(pair):
    lane = iota((8, 128), 1)
    sub = iota((8, 128), 0)
    part = lane & 31
    along_y = part + 96 * (part >> 4)
    which = part & 3
    along_z = (part >> 2) * 16 + 8 * (which >> 1) + 7 * (which & 1)
    segment = lane >> 5
    a, b = pair
    rows_a = row_parts(a[0:1, :], a[7:8, :], lane, sub)
    rows_b = row_parts(b[0:1, :], b[7:8, :], lane, sub)
    rest = pick(a, jnp.where(segment == 1, along_y, along_z), 1)
    first = jnp.where(segment == 0, rows_a, jnp.where(segment == 3, rows_b, rest))
    second = pick(b, jnp.where(segment == 2, along_y, along_z), 1)
    return first, second


def shifted(value, v):
    if v[0] != 0:
        value = pltpu.roll(value, v[0] % 16, 0)
    lanes = (16 * v[1] + v[2]) % 256
    if lanes != 0:
        value = pltpu.roll(value, lanes, 1)
    return value


def positions():
    row = iota((16, 256), 0)
    lane = iota((16, 256), 1)
    return row, lane >> 4, lane & 15


def wall_weights(depth):
    place = positions()
    solid = depth <= 0
    here = depth.astype(F32)
    out = [jnp.where(solid, 1.0, 0.0).astype(F32)]
    for q in range(1, 19):
        v = VELOCITIES[q]
        outside = []
        for axis in range(3):
            if v[axis] != 0:
                outside.append(place[axis] == (0 if v[axis] > 0 else 15))
        away = outside[0] if len(outside) == 1 else outside[0] | outside[1]
        there = shifted(here, v)
        wall = (there <= 0.0) & jnp.logical_not(away) & jnp.logical_not(solid)
        gap = jnp.where(wall, here - there, 1.0)
        own = jnp.where(wall, here, 1.0)
        far = own + own >= gap
        weight = jnp.where(far, 0.5 * gap, 2.0 * own) / jnp.where(far, own, gap)
        value = jnp.where(wall, weight, -1.0)
        if len(outside) == 2:
            value = jnp.where(outside[0] & outside[1], 1.0, value)
        out.append(value)
    return out


def stream(post, start, weights, ghosts):
    place = positions()
    solid = weights(0) > 0.5
    out = [jnp.where(solid, start(0), post(0))]
    for q in range(1, 19):
        v = VELOCITIES[q]
        own = post(q)
        value = own
        for axis in (1, 0, 2):
            if v[axis] != 0:
                edge = place[axis] == (15 if v[axis] > 0 else 0)
                value = jnp.where(edge, ghosts[axis][q], value)
        value = shifted(value, v)
        weight = weights(q)
        value = jnp.where(weight >= 0.0, own + weight * (post(OPPOSITE[q]) - own), value)
        out.append(jnp.where(solid, start(q), value))
    return out


def pack_octants(fields):
    low = (iota((8, 128), 1) & 15) < 8
    out = {}
    for ox in range(2):
        for oy in range(2):
            a, b, c, d = [tile(f, ox, oy) for f in fields]
            out[4 * ox + 2 * oy] = (
                jnp.where(low, a, pltpu.roll(b, 8, 1)),
                jnp.where(low, c, pltpu.roll(d, 8, 1)),
            )
            out[4 * ox + 2 * oy + 1] = (
                jnp.where(low, pltpu.roll(a, 120, 1), b),
                jnp.where(low, pltpu.roll(c, 120, 1), d),
            )
    return out


def packed_lines(first, second):
    lane = iota((8, 128), 1)

    def at_x(k, half, inner):
        base = 0 if k < 2 else 96
        return pick(first, base + ((lane >> 5) & 1) * 16 + inner, 1)

    def row_of(k, half, side):
        return 2 * half + (lane >> 6) + 4 * side

    def at_y(k, side, inner):
        rest, base = (first, 32) if k < 2 else (second, 64)
        return pick(rest, base + 16 * side + inner, 1)

    def at_z(k, y, side):
        rest, base = (first, 64) if k < 2 else (second, 96)
        return pick(rest, base + 4 * y + 2 * (k % 2) + side, 1)

    return at_x, row_of, at_y, at_z


def tile_lines(tiles):
    lane = iota((8, 128), 1)

    def at_x(k, half, inner):
        return pick(tiles[k // 2], (4 * half + (lane >> 5)) * 16 + inner, 1)

    def row_of(k, half, side):
        return jnp.full((8, 128), 7 * side, jnp.int32)

    def at_y(k, side, inner):
        return pick(tiles[k // 2], 112 * side + inner, 1)

    def at_z(k, y, side):
        return pick(tiles[k // 2], 16 * y + 8 * (k % 2) + 7 * side, 1)

    return at_x, row_of, at_y, at_z


def below(lines):
    at_x, row_of, at_y, at_z = lines
    lane = iota((8, 128), 1)
    sub = iota((8, 128), 0)
    z = lane & 15
    fields = [[], [], []]
    for k in range(4):
        inner = (z >> 1) + 8 * (k % 2)
        tiles = [[None, None], [None, None]]
        for half in range(2):
            rows = at_x(k, half, inner)
            for row in range(2):
                tiles[row][half] = pick(rows, row_of(k, half, 1 - row), 0)
        fields[0].append(join(tiles))
        for half in range(2):
            line = at_y(k, 1 - half, inner)
            for row in range(2):
                tiles[row][half] = pick(line, 4 * row + (sub >> 1), 0)
        fields[1].append(join(tiles))
        for half in range(2):
            y = 8 * half + (lane >> 4)
            far = z == 15
            line = at_z(k, ((y + jnp.where(far, 1, 15)) & 15) >> 1, jnp.where(far, 0, 1))
            for row in range(2):
                tiles[row][half] = pick(line, 4 * row + (sub >> 1), 0)
        fields[2].append(join(tiles))
    out = []
    for axis in range(3):
        chosen = [q for q in range(19) if VELOCITIES[q][axis] != 0]
        out.append(equilibrium(fields[axis][0], fields[axis][1:], chosen))
    return out


def restrict(f):
    lane = iota((8, 128), 1)
    sub = iota((8, 128), 0)
    density, momentum = sums(f)
    index = ((lane >> 4) & 3) * 32 + (lane & 7) * 2
    even = (2 * sub) & 7
    packed = []
    for field in [density] + momentum:
        halves = []
        for half in range(2):
            lines = [
                jnp.where(
                    sub < 4,
                    pick(tile(field, 0, half), even + odd, 0),
                    pick(tile(field, 1, half), even + odd, 0),
                )
                for odd in range(2)
            ]
            line = lines[0] + lines[1]
            parts = [pick(line, index + step, 1) for step in (0, 1, 16, 17)]
            halves.append(0.125 * ((parts[0] + parts[1]) + (parts[2] + parts[3])))
        packed.append(jnp.where(lane < 64, halves[0], halves[1]))
    low = (lane & 15) < 8
    return jnp.where(low, packed[0], packed[1]), jnp.where(low, packed[2], packed[3])


def load(ref):
    return [ref[q] for q in range(19)]


def load_cells(ref, q):
    halves = [ref[q, pl.ds(half, 16, stride=2), :] for half in range(2)]
    return jnp.concatenate(halves, axis=1)


def store_cells(ref, q, value):
    for half in range(2):
        ref[q, pl.ds(half, 16, stride=2), :] = value[:, 128 * half : 128 * half + 128]


def store_octants(fields, octs):
    for o, pair in pack_octants(fields).items():
        first, second = pack_shell(pair)
        octs[o, 0:8, :] = first
        octs[o, 8:16, :] = second


def give_octants(octs, parents, out):
    for d in range(32):
        o = parents[1, 0, d]
        out[d, 24:32, :] = octs[o, 0:8, :]
        out[d, 16:24, 64:128] = octs[o, 8:16, 64:128]


def give_face(post, face, code, me, out, at, shared, lanes):
    first, second = pack_face(post, face)
    slot = jnp.where(code >= 0, code, me)
    out[slot, at : at + 8, :] = first
    out[slot, shared : shared + 8, lanes : lanes + 32] = second[:, lanes : lanes + 32]
    return first, second


def send_kernel(
    coarse_in, fine_in, coarse_table, fine_table, parent_table, out, region_out,
    coarse, fine, coarse_links, fine_links, parents, slots, region, octs, sems,
):
    fetch = [
        pltpu.make_async_copy(source, target, sems.at[i])
        for i, (source, target) in enumerate(
            (
                (coarse_in, coarse),
                (coarse_table, coarse_links),
                (fine_in, fine),
                (fine_table, fine_links),
                (parent_table, parents),
            )
        )
    ]
    for copy in fetch:
        copy.start()

    def put(part):
        rows = pl.ds(8 * part, 8)
        return pltpu.make_async_copy(slots.at[:, rows, :], out.at[:, rows, :], sems.at[5 + part])

    me = lax.axis_index("dev")
    fetch[0].wait()
    fetch[1].wait()
    f = [load_cells(coarse, q) for q in range(19)]
    density, u = moments(f)
    store_octants([density] + u, octs)
    post = collide(f, OMEGA_COARSE)
    for face in range(6):
        first, second = give_face(post, face, coarse_links[face, 0, me], me, slots, 0, 16, 0)
        if face in (2, 3):
            region[face - 2, 0:8, :] = first
            region[face - 2, 8:16, :] = second
    put(0).start()
    beside = pltpu.make_async_copy(region, region_out, sems.at[9])
    beside.start()
    fetch[4].wait()
    give_octants(octs, parents, slots)
    put(3).start()
    fetch[2].wait()
    fetch[3].wait()
    post = collide([load_cells(fine, q) for q in range(19)], OMEGA_FINE)
    for face in range(6):
        give_face(post, face, fine_links[face, 0, me], me, slots, 8, 16, 32)
    put(1).start()
    put(2).start()
    for part in range(4):
        put(part).wait()
    beside.wait()


def prepare_kernel(state, depth, post, start, weights, *, omega):
    f = [load_cells(state, q) for q in range(19)]
    for q in range(19):
        start[q] = f[q]
    for q, value in enumerate(collide(f, omega)):
        post[q] = value
    halves = [depth[pl.ds(half, 16, stride=2), :] for half in range(2)]
    for q, value in enumerate(wall_weights(jnp.concatenate(halves, axis=1))):
        weights[q] = value


def codes_kernel(coarse_links, fine_links, parents, codes):
    me = lax.axis_index("dev")
    for face in range(6):
        codes[FINE_LINKS + face] = fine_links[face, 0, me]
        codes[COARSE_LINKS + face] = coarse_links[face, 0, me]
    codes[PARENT] = parents[0, 0, me]
    for o in range(8):
        codes[CHILDREN + o] = -1

    def note(d, carry):
        codes[OCTANTS + d] = parents[1, 0, d]

        @pl.when(parents[0, 0, d] == me)
        def _():
            codes[CHILDREN + parents[1, 0, d]] = d

        return carry

    lax.fori_loop(0, 32, note, 0)


def merge_ghosts(take):
    ghosts = [{}, {}, {}]
    for face in range(6):
        ghosts[face // 2].update(take(face))
    return ghosts


def fine_ghosts(codes, plane_of, lanes, under):
    def take(face):
        code = codes[FINE_LINKS + face]
        first, second = plane_of(jnp.maximum(code, 0))
        plane = unpack_face(first, second, lanes, face)
        return {q: jnp.where(code >= 0, plane[q], under[face // 2][q]) for q in plane}

    return merge_ghosts(take)


def middle_kernel(
    received, from_low, from_high, c_post, c_start, c_weights, f_post, f_start, f_weights,
    codes, out, coarse_new, state, post, octs,
):
    me = lax.axis_index("dev")

    def coarse_ghost(face):
        code = codes[COARSE_LINKS + face]
        slot = jnp.maximum(code, 0)
        first = received[slot, 0:8, :]
        second = received[slot, 16:24, :]
        if face in (2, 3):
            beside = from_low if face == 2 else from_high
            first = jnp.where(code == -2, beside[0, 0:8, :], first)
            second = jnp.where(code == -2, beside[0, 8:16, :], second)
        plane = unpack_face(first, second, 0, face)
        return {q: jnp.where(code == -1, inflow_value(q), plane[q]) for q in plane}

    new = stream(
        lambda q: c_post[q], lambda q: c_start[q], lambda q: c_weights[q], merge_ghosts(coarse_ghost)
    )
    for q in range(19):
        coarse_new[q] = new[q]
    old_density, old_u = moments([c_start[q] for q in range(19)])
    density, u = moments(new)
    mid = [0.5 * (old_density + density)] + [0.5 * (a + b) for a, b in zip(old_u, u)]
    for o, pair in pack_octants(mid).items():
        shared, rows = pack_thin_shell(pair)
        octs[o, 0] = shared[0:4]
        octs[o, 1] = shared[4:8]
        octs[o, 2] = rows
    parent = codes[PARENT]
    under = below(packed_lines(received[parent, 24:32, :], received[parent, 16:24, :]))
    ghosts = fine_ghosts(
        codes, lambda d: (received[d, 8:16, :], received[d, 16:24, :]), 32, under
    )
    new = stream(lambda q: f_post[q], lambda q: f_start[q], lambda q: f_weights[q], ghosts)
    for q in range(19):
        state[q] = new[q]
    after = collide(new, OMEGA_FINE)
    for q in range(19):
        post[q] = after[q]
    for face in range(6):
        first, second = pack_face(after, face)
        code = codes[FINE_LINKS + face]
        slot = jnp.where(code >= 0, code, me)
        for part in range(2):
            out[slot, part] = first[4 * part : 4 * part + 4]
            out[slot, 2 + part, :, 0:32] = second[4 * part : 4 * part + 4, 0:32]
    for d in range(32):
        o = codes[OCTANTS + d]
        out[d, 2, :, 32:128] = octs[o, 0, :, 32:128]
        out[d, 3, :, 32:128] = octs[o, 1, :, 32:128]
        out[d, 4] = octs[o, 2]


def last_kernel(received, f_post, f_start, f_weights, codes, out, state):
    def rows_of(d, part):
        return join_rows(received[d, part], received[d, part + 1])

    parent = codes[PARENT]
    under = below(tile_lines(unpack_thin_shell(rows_of(parent, 2), received[parent, 4])))
    ghosts = fine_ghosts(codes, lambda d: (rows_of(d, 0), rows_of(d, 2)), 0, under)
    new = stream(lambda q: f_post[q], lambda q: f_start[q], lambda q: f_weights[q], ghosts)
    for q in range(19):
        state[q] = new[q]
    first, second = restrict(new)
    out[parent, 0:8, :] = first
    out[parent, 8:16, :] = second


def cover(codes):
    low = (iota((8, 128), 1) & 15) < 8
    tiles = [[None, None], [None, None]]
    for ox in range(2):
        for oy in range(2):
            o = 4 * ox + 2 * oy
            tiles[ox][oy] = jnp.where(low, codes[CHILDREN + o], codes[CHILDREN + o + 1])
    return join(tiles) >= 0


def final_kernel(received, state, coarse_new, codes, fine_out, coarse_out, f_cells, c_cells, sems):
    for q in range(19):
        store_cells(f_cells, q, state[q])
    fine_copy = pltpu.make_async_copy(f_cells, fine_out, sems.at[0])
    fine_copy.start()
    low = (iota((8, 128), 1) & 15) < 8
    tiles = [[[None, None], [None, None]] for _ in range(4)]
    for ox in range(2):
        for oy in range(2):
            o = 4 * ox + 2 * oy
            near = jnp.maximum(codes[CHILDREN + o], 0)
            far = jnp.maximum(codes[CHILDREN + o + 1], 0)
            for k in range(2):
                a = received[near, 8 * k : 8 * k + 8, :]
                b = received[far, 8 * k : 8 * k + 8, :]
                tiles[2 * k][ox][oy] = jnp.where(low, a, pltpu.roll(b, 8, 1))
                tiles[2 * k + 1][ox][oy] = jnp.where(low, pltpu.roll(a, 120, 1), b)
    density, jx, jy, jz = [join(t) for t in tiles]
    covered = cover(codes)
    density = jnp.where(covered, density, 1.0)
    inverse = 1.0 / density
    fine_eq = equilibrium(density, [jx * inverse, jy * inverse, jz * inverse], range(19))
    new = load(coarse_new)
    own_density, own_u = moments(new)
    own_eq = equilibrium(own_density, own_u, range(19))
    for q in range(19):
        store_cells(c_cells, q, new[q] + jnp.where(covered, fine_eq[q] - own_eq[q], 0.0))
    coarse_copy = pltpu.make_async_copy(c_cells, coarse_out, sems.at[1])
    coarse_copy.start()
    fine_copy.wait()
    coarse_copy.wait()


VMEM = pl.BlockSpec(memory_space=pltpu.VMEM)
SMEM = pl.BlockSpec(memory_space=pltpu.SMEM)
HBM = pl.BlockSpec(memory_space=pltpu.HBM)
SOME_VMEM = 24 * 1024 * 1024
MOST_VMEM = 60 * 1024 * 1024


OCTS = pltpu.VMEM((8, 16, 128), F32)
LINKS = pltpu.SMEM((6, 1, 32), jnp.int32)
SEND_SCRATCH = [
    pltpu.VMEM(CELL_ROWS, F32),
    pltpu.VMEM(CELL_ROWS, F32),
    LINKS,
    LINKS,
    pltpu.SMEM((2, 1, 32), jnp.int32),
    pltpu.VMEM((32, SLOT1, 128), F32),
    pltpu.VMEM((2, 16, 128), F32),
    OCTS,
    pltpu.SemaphoreType.DMA((10,)),
]
FINAL_SCRATCH = [
    pltpu.VMEM(CELL_ROWS, F32),
    pltpu.VMEM(CELL_ROWS, F32),
    pltpu.SemaphoreType.DMA((2,)),
]


def call(kernel, outs, ins, smem=(), hbm=(), hbm_outs=(), scratch=(), vmem=SOME_VMEM, name=None):
    def space(i, scalars, far):
        return SMEM if scalars else HBM if i in far else VMEM

    ints = [not isinstance(s, tuple) for s in outs]
    return pl.pallas_call(
        kernel,
        out_shape=[
            jax.ShapeDtypeStruct((s,), jnp.int32) if i else jax.ShapeDtypeStruct(s, F32)
            for s, i in zip(outs, ints)
        ],
        in_specs=[space(i, i in smem, hbm) for i in range(len(ins))],
        out_specs=[space(i, scalars, hbm_outs) for i, scalars in enumerate(ints)],
        scratch_shapes=list(scratch),
        compiler_params=pltpu.CompilerParams(vmem_limit_bytes=vmem),
        cost_estimate=pl.CostEstimate(
            flops=2_000_000, bytes_accessed=2_000_000, transcendentals=0
        ),
        name=name,
    )(*ins)


def swap(value):
    return lax.all_to_all(value, "dev", split_axis=0, concat_axis=0, tiled=True)


def body(fine_state, coarse_state, fine_depth, coarse_depth, fine_links, coarse_links, parents):
    count = lax.axis_size("group")
    fine_state, coarse_state = fine_state.reshape(CELL_ROWS), coarse_state.reshape(CELL_ROWS)
    fine_depth, coarse_depth = fine_depth.reshape(32, 128), coarse_depth.reshape(32, 128)
    fine_links = fine_links.transpose(2, 0, 1)
    coarse_links = coarse_links.transpose(2, 0, 1)
    parents = parents.transpose(2, 0, 1)
    sent, region = call(
        send_kernel,
        [(32, SLOT1, 128), (2, 16, 128)],
        [coarse_state, fine_state, coarse_links, fine_links, parents],
        hbm=(0, 1, 2, 3, 4),
        hbm_outs=(0, 1),
        scratch=SEND_SCRATCH,
        vmem=MOST_VMEM,
        name="send",
    )
    up = [(i, i + 1) for i in range(count - 1)]
    down = [(b, a) for a, b in up]
    received = swap(sent)
    from_low = lax.ppermute(region[1:2], "group", up)
    from_high = lax.ppermute(region[0:1], "group", down)

    def prepare(state, depth, omega, name):
        def kernel(*refs):
            prepare_kernel(*refs, omega=omega)

        return call(kernel, [FIELD, FIELD, FIELD], [state, depth], name=name)

    c_post, c_start, c_weights = prepare(coarse_state, coarse_depth, OMEGA_COARSE, "prepare_coarse")
    f_post, f_start, f_weights = prepare(fine_state, fine_depth, OMEGA_FINE, "prepare_fine")
    (codes,) = call(
        codes_kernel, [CODES], [coarse_links, fine_links, parents], smem=(0, 1, 2), name="codes"
    )
    sent, coarse_new, state, post = call(
        middle_kernel,
        [SLOT2, FIELD, FIELD, FIELD],
        [
            received, from_low, from_high, c_post, c_start, c_weights, f_post, f_start, f_weights,
            codes,
        ],
        smem=(9,),
        scratch=[pltpu.VMEM((8, 3, 4, 128), F32)],
        name="middle",
    )
    received = swap(sent)
    sent, state = call(
        last_kernel,
        [(32, SLOT3, 128), FIELD],
        [received, post, state, f_weights, codes],
        smem=(4,),
        name="last",
    )
    received = swap(sent)
    fine_out, coarse_out = call(
        final_kernel,
        [CELL_ROWS, CELL_ROWS],
        [received, state, coarse_new, codes],
        smem=(3,),
        hbm_outs=(0, 1),
        scratch=FINAL_SCRATCH,
        name="final",
    )
    return fine_out.reshape(1, 19, 4096), coarse_out.reshape(1, 19, 4096)


def solution(mesh):
    placed = (
        P(("group", "dev"), None, None),
        P(("group", "dev"), None, None),
        P(("group", "dev"), None),
        P(("group", "dev"), None),
        P("group", None, None),
        P("group", None, None),
        P("group", None, None),
    )
    return jax.shard_map(
        body,
        mesh=mesh,
        in_specs=placed,
        out_specs=(P(("group", "dev"), None, None), P(("group", "dev"), None, None)),
        check_vma=False,
    )
```

```python
import jax
import jax.numpy as jnp
from jax import lax
from jax.experimental import pallas as pl
from jax.experimental.pallas import tpu as pltpu
from jax.sharding import PartitionSpec as P

VELOCITIES = [
    (0, 0, 0),
    (1, 0, 0),
    (-1, 0, 0),
    (0, 1, 0),
    (0, -1, 0),
    (0, 0, 1),
    (0, 0, -1),
    (1, 1, 0),
    (-1, -1, 0),
    (1, -1, 0),
    (-1, 1, 0),
    (1, 0, 1),
    (-1, 0, -1),
    (1, 0, -1),
    (-1, 0, 1),
    (0, 1, 1),
    (0, -1, -1),
    (0, 1, -1),
    (0, -1, 1),
]
WEIGHTS = [1.0 / 3.0] + [1.0 / 18.0] * 6 + [1.0 / 36.0] * 12
OPPOSITE = [VELOCITIES.index((-v[0], -v[1], -v[2])) for v in VELOCITIES]
OUTGOING = [
    [q for q in range(19) if VELOCITIES[q][face // 2] == 2 * (face % 2) - 1] for face in range(6)
]
OMEGA_FINE = 1.25
OMEGA_COARSE = 1.0 / 0.65
INFLOW = 0.05
F32 = jnp.float32
FIELD = (19, 16, 256)
CELL_ROWS = (19, 32, 128)
SLOT1 = 32
SLOT2 = (32, 5, 4, 128)
SLOT3 = 16
FINE_LINKS, COARSE_LINKS, PARENT, CHILDREN, OCTANTS = (0, 0), (0, 1), (6, 0), (0, 2), (7, 32)


def inflow_value(q):
    along = VELOCITIES[q][0] * INFLOW
    return WEIGHTS[q] * (1.0 + 3.0 * along + 4.5 * along * along - 1.5 * INFLOW * INFLOW)


def iota(shape, dim):
    return lax.broadcasted_iota(jnp.int32, shape, dim)


def tile(value, row, half):
    return value[8 * row : 8 * row + 8, 128 * half : 128 * half + 128]


def join(tiles):
    return jnp.concatenate([jnp.concatenate(line, axis=1) for line in tiles], axis=0)


def pick(value, index, axis):
    return jnp.take_along_axis(value, index, axis=axis, mode="promise_in_bounds")


def sums(f):
    density = f[0]
    for q in range(1, 19):
        density = density + f[q]
    momentum = []
    for axis in range(3):
        plus = [f[q] for q in range(19) if VELOCITIES[q][axis] == 1]
        minus = [f[q] for q in range(19) if VELOCITIES[q][axis] == -1]
        total = plus[0] - minus[0]
        for a, b in zip(plus[1:], minus[1:]):
            total = total + (a - b)
        momentum.append(total)
    return density, momentum


def moments(f):
    density, momentum = sums(f)
    inverse = 1.0 / density
    return density, [m * inverse for m in momentum]


def equilibrium(density, u, chosen):
    base = 1.0 - 1.5 * (u[0] * u[0] + u[1] * u[1] + u[2] * u[2])
    scaled = {}
    for q in chosen:
        if WEIGHTS[q] not in scaled:
            scaled[WEIGHTS[q]] = WEIGHTS[q] * density
    even, out = {}, {}
    for q in chosen:
        v = VELOCITIES[q]
        weight = scaled[WEIGHTS[q]]
        if q == 0:
            out[q] = weight * base
            continue
        lead = q if q % 2 == 1 else q - 1
        if lead not in even:
            along = None
            for axis in range(3):
                c = VELOCITIES[lead][axis]
                if c != 0:
                    if along is None:
                        along = u[axis]
                    else:
                        along = along + u[axis] if c > 0 else along - u[axis]
            even[lead] = (base + 4.5 * along * along, 3.0 * along)
        part, odd = even[lead]
        out[q] = weight * (part + odd) if q == lead else weight * (part - odd)
    return out


def collide(f, omega):
    density, u = moments(f)
    rest = equilibrium(density, u, range(19))
    return [(1.0 - omega) * f[q] + omega * rest[q] for q in range(19)]


def row_parts(top, bottom, lane, sub):
    both = jnp.where(sub < 4, jnp.broadcast_to(top, (8, 128)), jnp.broadcast_to(bottom, (8, 128)))
    return pick(both, 32 * (sub & 3) + (lane & 31), 1)


def pack_face(post, face):
    axis, side = face // 2, face % 2
    lane = iota((8, 128), 1)
    sub = iota((8, 128), 0)
    chosen = [post[q] for q in OUTGOING[face]]
    if axis == 0:
        at = 15 * side
        rows = [[f[at : at + 1, 128 * h : 128 * h + 128] for h in range(2)] for f in chosen]
        first = None
        for i in range(4):
            for half in range(2):
                line = jnp.broadcast_to(rows[i][half], (8, 128))
                first = line if first is None else jnp.where(sub == 2 * i + half, line, first)
        return first, row_parts(rows[4][0], rows[4][1], lane, sub)
    strips = []
    for f in chosen:
        for row in range(2):
            if axis == 1:
                strips.append(pick(tile(f, row, side), (lane & 15) + 112 * side, 1))
            else:
                index = (lane & 7) * 16 + 15 * side
                a = pick(tile(f, row, 0), index, 1)
                b = pick(tile(f, row, 1), index, 1)
                strips.append(jnp.where((lane & 15) < 8, a, b))
    first = strips[0]
    for t in range(1, 8):
        first = jnp.where((lane >> 4) == t, strips[t], first)
    second = jnp.where(((lane >> 4) & 1) == 0, strips[8], strips[9])
    return first, second


def unpack_face(first, second, offset, face):
    axis, side = face // 2, face % 2
    lane = iota((8, 128), 1)
    out = {}
    for i, q in enumerate(OUTGOING[face ^ 1]):
        if axis == 0:
            halves = []
            for half in range(2):
                if i < 4:
                    line = jnp.broadcast_to(first[2 * i + half : 2 * i + half + 1, :], (8, 128))
                else:
                    line = pick(pick(second, offset + (lane & 31), 1), 4 * half + (lane >> 5), 0)
                halves.append(line)
            out[q] = join([halves, halves])
            continue
        rows = []
        for row in range(2):
            source, base = (first, 16 * (2 * i + row)) if i < 4 else (second, offset + 16 * row)
            if axis == 1:
                piece = pick(source, base + (lane & 15), 1)
                rows.append([piece, piece])
            else:
                step = 1 if side == 0 else 15
                rows.append(
                    [
                        pick(source, base + ((8 * half + (lane >> 4) + step) & 15), 1)
                        for half in range(2)
                    ]
                )
        out[q] = join(rows)
    return out


def join_rows(upper, lower):
    return jnp.concatenate([upper, lower], axis=0)


def shell_places(lane):
    entry = lane - jnp.where(lane < 120, 96, 120)
    along_z = (1 + (entry >> 2)) * 16 + 8 * ((entry >> 1) & 1) + 7 * (entry & 1)
    part = lane & 31
    return jnp.where(lane < 96, part + 96 * (part >> 4), along_z)


def pack_thin_shell(pair):
    lane = iota((8, 128), 1)
    sub = iota((8, 128), 0)
    a, b = pair
    index = shell_places(lane) & 127
    first = (lane < 64) | ((lane >= 96) & (lane < 120))
    inside = jnp.where(first, pick(a, index, 1), pick(b, index, 1))
    entry = 8 + (lane & 15)
    rest = pick(b, (1 + (entry >> 2)) * 16 + 8 * ((entry >> 1) & 1) + 7 * (entry & 1), 1)
    block = ((lane >> 4) - 2) & 3
    rest = pick(rest, jnp.where(sub == 0, 1, 4) + block, 0)
    shared = jnp.where((sub == 0) | (sub == 7), rest, inside)
    rows = jnp.concatenate([a[0:1], a[7:8], b[0:1], b[7:8]], axis=0)
    return shared, rows


def unpack_thin_shell(shared, rows):
    lane = iota((8, 128), 1)
    sub = iota((8, 128), 0)
    rows = join_rows(rows, rows)
    edge = (lane & 15) + jnp.where(lane >= 112, 16, 0)
    z = lane & 15
    entry = 4 * ((lane >> 4) - 1) + 2 * (z >> 3) + jnp.where((z & 7) == 7, 1, 0)
    on_y = (lane < 16) | (lane >= 112)
    block = sub - jnp.where(sub > 3, 4, 1)
    moved = pick(pick(shared, jnp.where(sub <= 3, 0, 7), 0), (24 + 16 * block + entry) & 127, 1)
    out = []
    for k in range(2):
        start = 96 if k == 0 else 120
        tile_k = pick(shared, jnp.where(on_y, 32 + 32 * k + edge, start + entry) & 127, 1)
        if k == 1:
            tile_k = jnp.where(on_y | (entry < 8), tile_k, moved)
        line = pick(rows, 2 * k + jnp.where(sub == 7, 1, 0), 0)
        out.append(jnp.where((sub == 0) | (sub == 7), line, tile_k))
    return out


def pack_shell(pair):
    lane = iota((8, 128), 1)
    sub = iota((8, 128), 0)
    part = lane & 31
    along_y = part + 96 * (part >> 4)
    which = part & 3
    along_z = (part >> 2) * 16 + 8 * (which >> 1) + 7 * (which & 1)
    segment = lane >> 5
    a, b = pair
    rows_a = row_parts(a[0:1, :], a[7:8, :], lane, sub)
    rows_b = row_parts(b[0:1, :], b[7:8, :], lane, sub)
    rest = pick(a, jnp.where(segment == 1, along_y, along_z), 1)
    first = jnp.where(segment == 0, rows_a, jnp.where(segment == 3, rows_b, rest))
    second = pick(b, jnp.where(segment == 2, along_y, along_z), 1)
    return first, second


def shifted(value, v):
    if v[0] != 0:
        value = pltpu.roll(value, v[0] % 16, 0)
    lanes = (16 * v[1] + v[2]) % 256
    if lanes != 0:
        value = pltpu.roll(value, lanes, 1)
    return value


def positions():
    row = iota((16, 256), 0)
    lane = iota((16, 256), 1)
    return row, lane >> 4, lane & 15


def wall_weights(depth):
    place = positions()
    solid = depth <= 0
    here = depth.astype(F32)
    out = [jnp.where(solid, 1.0, 0.0).astype(F32)]
    for q in range(1, 19):
        v = VELOCITIES[q]
        outside = []
        for axis in range(3):
            if v[axis] != 0:
                outside.append(place[axis] == (0 if v[axis] > 0 else 15))
        away = outside[0] if len(outside) == 1 else outside[0] | outside[1]
        there = shifted(here, v)
        wall = (there <= 0.0) & jnp.logical_not(away) & jnp.logical_not(solid)
        gap = jnp.where(wall, here - there, 1.0)
        own = jnp.where(wall, here, 1.0)
        far = own + own >= gap
        weight = jnp.where(far, 0.5 * gap, 2.0 * own) / jnp.where(far, own, gap)
        value = jnp.where(wall, weight, -1.0)
        if len(outside) == 2:
            value = jnp.where(outside[0] & outside[1], 1.0, value)
        out.append(value)
    return out


def stream(post, start, weights, ghosts):
    place = positions()
    solid = weights(0) > 0.5
    out = [jnp.where(solid, start(0), post(0))]
    for q in range(1, 19):
        v = VELOCITIES[q]
        own = post(q)
        value = own
        for axis in (1, 0, 2):
            if v[axis] != 0:
                edge = place[axis] == (15 if v[axis] > 0 else 0)
                value = jnp.where(edge, ghosts[axis][q], value)
        value = shifted(value, v)
        weight = weights(q)
        value = jnp.where(weight >= 0.0, own + weight * (post(OPPOSITE[q]) - own), value)
        out.append(jnp.where(solid, start(q), value))
    return out


def pack_octants(fields):
    low = (iota((8, 128), 1) & 15) < 8
    out = {}
    for ox in range(2):
        for oy in range(2):
            a, b, c, d = [tile(f, ox, oy) for f in fields]
            out[4 * ox + 2 * oy] = (
                jnp.where(low, a, pltpu.roll(b, 8, 1)),
                jnp.where(low, c, pltpu.roll(d, 8, 1)),
            )
            out[4 * ox + 2 * oy + 1] = (
                jnp.where(low, pltpu.roll(a, 120, 1), b),
                jnp.where(low, pltpu.roll(c, 120, 1), d),
            )
    return out


def packed_lines(first, second):
    lane = iota((8, 128), 1)

    def at_x(k, half, inner):
        base = 0 if k < 2 else 96
        return pick(first, base + ((lane >> 5) & 1) * 16 + inner, 1)

    def row_of(k, half, side):
        return 2 * half + (lane >> 6) + 4 * side

    def at_y(k, side, inner):
        rest, base = (first, 32) if k < 2 else (second, 64)
        return pick(rest, base + 16 * side + inner, 1)

    def at_z(k, y, side):
        rest, base = (first, 64) if k < 2 else (second, 96)
        return pick(rest, base + 4 * y + 2 * (k % 2) + side, 1)

    return at_x, row_of, at_y, at_z


def tile_lines(tiles):
    lane = iota((8, 128), 1)

    def at_x(k, half, inner):
        return pick(tiles[k // 2], (4 * half + (lane >> 5)) * 16 + inner, 1)

    def row_of(k, half, side):
        return jnp.full((8, 128), 7 * side, jnp.int32)

    def at_y(k, side, inner):
        return pick(tiles[k // 2], 112 * side + inner, 1)

    def at_z(k, y, side):
        return pick(tiles[k // 2], 16 * y + 8 * (k % 2) + 7 * side, 1)

    return at_x, row_of, at_y, at_z


def below(lines):
    at_x, row_of, at_y, at_z = lines
    lane = iota((8, 128), 1)
    sub = iota((8, 128), 0)
    z = lane & 15
    fields = [[], [], []]
    for k in range(4):
        inner = (z >> 1) + 8 * (k % 2)
        tiles = [[None, None], [None, None]]
        for half in range(2):
            rows = at_x(k, half, inner)
            for row in range(2):
                tiles[row][half] = pick(rows, row_of(k, half, 1 - row), 0)
        fields[0].append(join(tiles))
        for half in range(2):
            line = at_y(k, 1 - half, inner)
            for row in range(2):
                tiles[row][half] = pick(line, 4 * row + (sub >> 1), 0)
        fields[1].append(join(tiles))
        for half in range(2):
            y = 8 * half + (lane >> 4)
            far = z == 15
            line = at_z(k, ((y + jnp.where(far, 1, 15)) & 15) >> 1, jnp.where(far, 0, 1))
            for row in range(2):
                tiles[row][half] = pick(line, 4 * row + (sub >> 1), 0)
        fields[2].append(join(tiles))
    out = []
    for axis in range(3):
        chosen = [q for q in range(19) if VELOCITIES[q][axis] != 0]
        out.append(equilibrium(fields[axis][0], fields[axis][1:], chosen))
    return out


def restrict(f):
    lane = iota((8, 128), 1)
    sub = iota((8, 128), 0)
    density, momentum = sums(f)
    index = ((lane >> 4) & 3) * 32 + (lane & 7) * 2
    even = (2 * sub) & 7
    packed = []
    for field in [density] + momentum:
        halves = []
        for half in range(2):
            lines = [
                jnp.where(
                    sub < 4,
                    pick(tile(field, 0, half), even + odd, 0),
                    pick(tile(field, 1, half), even + odd, 0),
                )
                for odd in range(2)
            ]
            line = lines[0] + lines[1]
            parts = [pick(line, index + step, 1) for step in (0, 1, 16, 17)]
            halves.append(0.125 * ((parts[0] + parts[1]) + (parts[2] + parts[3])))
        packed.append(jnp.where(lane < 64, halves[0], halves[1]))
    low = (lane & 15) < 8
    return jnp.where(low, packed[0], packed[1]), jnp.where(low, packed[2], packed[3])


def load(ref):
    return [ref[q] for q in range(19)]


def load_cells(ref, q):
    halves = [ref[q, pl.ds(half, 16, stride=2), :] for half in range(2)]
    return jnp.concatenate(halves, axis=1)


def store_cells(ref, q, value):
    for half in range(2):
        ref[q, pl.ds(half, 16, stride=2), :] = value[:, 128 * half : 128 * half + 128]


def store_octants(fields, octs):
    for o, pair in pack_octants(fields).items():
        first, second = pack_shell(pair)
        octs[o, 0:8, :] = first
        octs[o, 8:16, :] = second


def give_octants(octs, parents, out):
    for d in range(32):
        o = parents[1, 0, d]
        out[d, 24:32, :] = octs[o, 0:8, :]
        out[d, 16:24, 64:128] = octs[o, 8:16, 64:128]


def give_face(post, face, code, me, out, at, shared, lanes):
    first, second = pack_face(post, face)
    slot = jnp.where(code >= 0, code, me)
    out[slot, at : at + 8, :] = first
    out[slot, shared : shared + 8, lanes : lanes + 32] = second[:, lanes : lanes + 32]
    return first, second


def send_kernel(
    coarse_in, fine_in, coarse_table, fine_table, parent_table, out, region_out,
    coarse, fine, coarse_links, fine_links, parents, slots, region, octs, sems,
):
    fetch = [
        pltpu.make_async_copy(source, target, sems.at[i])
        for i, (source, target) in enumerate(
            (
                (coarse_in, coarse),
                (coarse_table, coarse_links),
                (fine_in, fine),
                (fine_table, fine_links),
                (parent_table, parents),
            )
        )
    ]
    for copy in fetch:
        copy.start()

    def put(part):
        rows = pl.ds(8 * part, 8)
        return pltpu.make_async_copy(slots.at[:, rows, :], out.at[:, rows, :], sems.at[5 + part])

    me = lax.axis_index("dev")
    fetch[0].wait()
    fetch[1].wait()
    f = [load_cells(coarse, q) for q in range(19)]
    density, u = moments(f)
    store_octants([density] + u, octs)
    post = collide(f, OMEGA_COARSE)
    for face in range(6):
        first, second = give_face(post, face, coarse_links[face, 0, me], me, slots, 0, 16, 0)
        if face in (2, 3):
            region[face - 2, 0:8, :] = first
            region[face - 2, 8:16, :] = second
    put(0).start()
    beside = pltpu.make_async_copy(region, region_out, sems.at[9])
    beside.start()
    fetch[4].wait()
    give_octants(octs, parents, slots)
    put(3).start()
    fetch[2].wait()
    fetch[3].wait()
    post = collide([load_cells(fine, q) for q in range(19)], OMEGA_FINE)
    for face in range(6):
        give_face(post, face, fine_links[face, 0, me], me, slots, 8, 16, 32)
    put(1).start()
    put(2).start()
    for part in range(4):
        put(part).wait()
    beside.wait()


def prepare_kernel(state, depth, post, start, weights, *, omega):
    f = [load_cells(state, q) for q in range(19)]
    for q in range(19):
        start[q] = f[q]
    for q, value in enumerate(collide(f, omega)):
        post[q] = value
    halves = [depth[pl.ds(half, 16, stride=2), :] for half in range(2)]
    for q, value in enumerate(wall_weights(jnp.concatenate(halves, axis=1))):
        weights[q] = value


def codes_kernel(coarse_links, fine_links, parents, codes):
    me = lax.axis_index("dev")
    lane = iota((1, 32), 1)
    place = [iota((8, 128), 0), iota((8, 128), 1)]
    owner, octant = parents[0], parents[1]

    def own(line):
        return jnp.sum(jnp.where(lane == me, line, 0), axis=1, keepdims=True)

    values = {}
    for face in range(6):
        values[FINE_LINKS[0] + face, FINE_LINKS[1]] = own(fine_links[face])
        values[COARSE_LINKS[0] + face, COARSE_LINKS[1]] = own(coarse_links[face])
    values[PARENT] = own(owner)
    for o in range(8):
        child = jnp.where((owner == me) & (octant == o), lane, -1)
        values[CHILDREN[0] + o, CHILDREN[1]] = jnp.max(child, axis=1, keepdims=True)
    tile_of = jnp.zeros((8, 128), jnp.int32)
    for (row, at), value in values.items():
        tile_of = jnp.where((place[0] == row) & (place[1] == at), value, tile_of)
    codes[...] = tile_of
    row, at = OCTANTS
    codes[row : row + 1, at : at + 32] = octant


class Codes:
    def __init__(self, ref):
        self.tile = ref[...]
        self.seen = {}

    def __call__(self, start, step=0):
        row, at = (start[0], start[1] + step) if start == OCTANTS else (start[0] + step, start[1])
        if (row, at) not in self.seen:
            self.seen[row, at] = self.tile[row, at]
        return self.seen[row, at]


def merge_ghosts(take):
    ghosts = [{}, {}, {}]
    for face in range(6):
        ghosts[face // 2].update(take(face))
    return ghosts


def fine_ghosts(codes, plane_of, lanes, under):
    def take(face):
        code = codes(FINE_LINKS, face)
        first, second = plane_of(jnp.maximum(code, 0))
        plane = unpack_face(first, second, lanes, face)
        return {q: jnp.where(code >= 0, plane[q], under[face // 2][q]) for q in plane}

    return merge_ghosts(take)


def middle_kernel(
    received, from_low, from_high, c_post, c_start, c_weights, f_post, f_start, f_weights,
    table, out, coarse_new, state, post, octs,
):
    me = lax.axis_index("dev")
    codes = Codes(table)

    def coarse_ghost(face):
        code = codes(COARSE_LINKS, face)
        slot = jnp.maximum(code, 0)
        first = received[slot, 0:8, :]
        second = received[slot, 16:24, :]
        if face in (2, 3):
            beside = from_low if face == 2 else from_high
            first = jnp.where(code == -2, beside[0, 0:8, :], first)
            second = jnp.where(code == -2, beside[0, 8:16, :], second)
        plane = unpack_face(first, second, 0, face)
        return {q: jnp.where(code == -1, inflow_value(q), plane[q]) for q in plane}

    new = stream(
        lambda q: c_post[q], lambda q: c_start[q], lambda q: c_weights[q], merge_ghosts(coarse_ghost)
    )
    for q in range(19):
        coarse_new[q] = new[q]
    old_density, old_u = moments([c_start[q] for q in range(19)])
    density, u = moments(new)
    mid = [0.5 * (old_density + density)] + [0.5 * (a + b) for a, b in zip(old_u, u)]
    for o, pair in pack_octants(mid).items():
        shared, rows = pack_thin_shell(pair)
        octs[o, 0] = shared[0:4]
        octs[o, 1] = shared[4:8]
        octs[o, 2] = rows
    parent = codes(PARENT)
    under = below(packed_lines(received[parent, 24:32, :], received[parent, 16:24, :]))
    ghosts = fine_ghosts(
        codes, lambda d: (received[d, 8:16, :], received[d, 16:24, :]), 32, under
    )
    new = stream(lambda q: f_post[q], lambda q: f_start[q], lambda q: f_weights[q], ghosts)
    for q in range(19):
        state[q] = new[q]
    after = collide(new, OMEGA_FINE)
    for q in range(19):
        post[q] = after[q]
    for face in range(6):
        first, second = pack_face(after, face)
        code = codes(FINE_LINKS, face)
        slot = jnp.where(code >= 0, code, me)
        for part in range(2):
            out[slot, part] = first[4 * part : 4 * part + 4]
            out[slot, 2 + part, :, 0:32] = second[4 * part : 4 * part + 4, 0:32]
    for d in range(32):
        o = codes(OCTANTS, d)
        out[d, 2, :, 32:128] = octs[o, 0, :, 32:128]
        out[d, 3, :, 32:128] = octs[o, 1, :, 32:128]
        out[d, 4] = octs[o, 2]


def last_kernel(received, f_post, f_start, f_weights, table, out, state):
    codes = Codes(table)
    def rows_of(d, part):
        return join_rows(received[d, part], received[d, part + 1])

    parent = codes(PARENT)
    under = below(tile_lines(unpack_thin_shell(rows_of(parent, 2), received[parent, 4])))
    ghosts = fine_ghosts(codes, lambda d: (rows_of(d, 0), rows_of(d, 2)), 0, under)
    new = stream(lambda q: f_post[q], lambda q: f_start[q], lambda q: f_weights[q], ghosts)
    for q in range(19):
        state[q] = new[q]
    first, second = restrict(new)
    out[parent, 0:8, :] = first
    out[parent, 8:16, :] = second


def cover(codes):
    low = (iota((8, 128), 1) & 15) < 8
    tiles = [[None, None], [None, None]]
    for ox in range(2):
        for oy in range(2):
            o = 4 * ox + 2 * oy
            tiles[ox][oy] = jnp.where(low, codes(CHILDREN, o), codes(CHILDREN, o + 1))
    return join(tiles) >= 0


def final_kernel(received, state, coarse_new, table, fine_out, coarse_out, f_cells, c_cells, sems):
    codes = Codes(table)
    for q in range(19):
        store_cells(f_cells, q, state[q])
    fine_copy = pltpu.make_async_copy(f_cells, fine_out, sems.at[0])
    fine_copy.start()
    low = (iota((8, 128), 1) & 15) < 8
    tiles = [[[None, None], [None, None]] for _ in range(4)]
    for ox in range(2):
        for oy in range(2):
            o = 4 * ox + 2 * oy
            near = jnp.maximum(codes(CHILDREN, o), 0)
            far = jnp.maximum(codes(CHILDREN, o + 1), 0)
            for k in range(2):
                a = received[near, 8 * k : 8 * k + 8, :]
                b = received[far, 8 * k : 8 * k + 8, :]
                tiles[2 * k][ox][oy] = jnp.where(low, a, pltpu.roll(b, 8, 1))
                tiles[2 * k + 1][ox][oy] = jnp.where(low, pltpu.roll(a, 120, 1), b)
    density, jx, jy, jz = [join(t) for t in tiles]
    covered = cover(codes)
    density = jnp.where(covered, density, 1.0)
    inverse = 1.0 / density
    fine_eq = equilibrium(density, [jx * inverse, jy * inverse, jz * inverse], range(19))
    new = load(coarse_new)
    own_density, own_u = moments(new)
    own_eq = equilibrium(own_density, own_u, range(19))
    for q in range(19):
        store_cells(c_cells, q, new[q] + jnp.where(covered, fine_eq[q] - own_eq[q], 0.0))
    coarse_copy = pltpu.make_async_copy(c_cells, coarse_out, sems.at[1])
    coarse_copy.start()
    fine_copy.wait()
    coarse_copy.wait()


VMEM = pl.BlockSpec(memory_space=pltpu.VMEM)
HBM = pl.BlockSpec(memory_space=pltpu.HBM)
SOME_VMEM = 24 * 1024 * 1024
MOST_VMEM = 60 * 1024 * 1024


OCTS = pltpu.VMEM((8, 16, 128), F32)
LINKS = pltpu.SMEM((6, 1, 32), jnp.int32)
SEND_SCRATCH = [
    pltpu.VMEM(CELL_ROWS, F32),
    pltpu.VMEM(CELL_ROWS, F32),
    LINKS,
    LINKS,
    pltpu.SMEM((2, 1, 32), jnp.int32),
    pltpu.VMEM((32, SLOT1, 128), F32),
    pltpu.VMEM((2, 16, 128), F32),
    OCTS,
    pltpu.SemaphoreType.DMA((10,)),
]
FINAL_SCRATCH = [
    pltpu.VMEM(CELL_ROWS, F32),
    pltpu.VMEM(CELL_ROWS, F32),
    pltpu.SemaphoreType.DMA((2,)),
]


def call(kernel, outs, ins, hbm=(), hbm_outs=(), scratch=(), vmem=SOME_VMEM, name=None):
    return pl.pallas_call(
        kernel,
        out_shape=[jax.ShapeDtypeStruct(s, F32) for s in outs],
        in_specs=[HBM if i in hbm else VMEM for i in range(len(ins))],
        out_specs=[HBM if i in hbm_outs else VMEM for i in range(len(outs))],
        scratch_shapes=list(scratch),
        compiler_params=pltpu.CompilerParams(vmem_limit_bytes=vmem),
        cost_estimate=pl.CostEstimate(
            flops=2_000_000, bytes_accessed=2_000_000, transcendentals=0
        ),
        name=name,
    )(*ins)


def swap(value):
    return lax.all_to_all(value, "dev", split_axis=0, concat_axis=0, tiled=True)


def body(fine_state, coarse_state, fine_depth, coarse_depth, fine_links, coarse_links, parents):
    count = lax.axis_size("group")
    fine_state, coarse_state = fine_state.reshape(CELL_ROWS), coarse_state.reshape(CELL_ROWS)
    fine_depth, coarse_depth = fine_depth.reshape(32, 128), coarse_depth.reshape(32, 128)
    fine_links = fine_links.transpose(2, 0, 1)
    coarse_links = coarse_links.transpose(2, 0, 1)
    parents = parents.transpose(2, 0, 1)
    sent, region = call(
        send_kernel,
        [(32, SLOT1, 128), (2, 16, 128)],
        [coarse_state, fine_state, coarse_links, fine_links, parents],
        hbm=(0, 1, 2, 3, 4),
        hbm_outs=(0, 1),
        scratch=SEND_SCRATCH,
        vmem=MOST_VMEM,
        name="send",
    )
    up = [(i, i + 1) for i in range(count - 1)]
    down = [(b, a) for a, b in up]
    received = swap(sent)
    from_low = lax.ppermute(region[1:2], "group", up)
    from_high = lax.ppermute(region[0:1], "group", down)

    def prepare(state, depth, omega, name):
        def kernel(*refs):
            prepare_kernel(*refs, omega=omega)

        return call(kernel, [FIELD, FIELD, FIELD], [state, depth], name=name)

    c_post, c_start, c_weights = prepare(coarse_state, coarse_depth, OMEGA_COARSE, "prepare_coarse")
    f_post, f_start, f_weights = prepare(fine_state, fine_depth, OMEGA_FINE, "prepare_fine")
    codes = pl.pallas_call(
        codes_kernel,
        out_shape=jax.ShapeDtypeStruct((8, 128), jnp.int32),
        in_specs=[VMEM] * 3,
        out_specs=VMEM,
        compiler_params=pltpu.CompilerParams(vmem_limit_bytes=SOME_VMEM),
        name="codes",
    )(coarse_links, fine_links, parents)
    sent, coarse_new, state, post = call(
        middle_kernel,
        [SLOT2, FIELD, FIELD, FIELD],
        [
            received, from_low, from_high, c_post, c_start, c_weights, f_post, f_start, f_weights,
            codes,
        ],
        scratch=[pltpu.VMEM((8, 3, 4, 128), F32)],
        name="middle",
    )
    received = swap(sent)
    sent, state = call(
        last_kernel,
        [(32, SLOT3, 128), FIELD],
        [received, post, state, f_weights, codes],
        name="last",
    )
    received = swap(sent)
    fine_out, coarse_out = call(
        final_kernel,
        [CELL_ROWS, CELL_ROWS],
        [received, state, coarse_new, codes],
        hbm_outs=(0, 1),
        scratch=FINAL_SCRATCH,
        name="final",
    )
    return fine_out.reshape(1, 19, 4096), coarse_out.reshape(1, 19, 4096)


def solution(mesh):
    placed = (
        P(("group", "dev"), None, None),
        P(("group", "dev"), None, None),
        P(("group", "dev"), None),
        P(("group", "dev"), None),
        P("group", None, None),
        P("group", None, None),
        P("group", None, None),
    )
    return jax.shard_map(
        body,
        mesh=mesh,
        in_specs=placed,
        out_specs=(P(("group", "dev"), None, None), P(("group", "dev"), None, None)),
        check_vma=False,
    )
```

```python
import jax
import jax.numpy as jnp
from jax import lax
from jax.experimental import pallas as pl
from jax.experimental.pallas import tpu as pltpu
from jax.sharding import PartitionSpec as P

VELOCITIES = [
    (0, 0, 0),
    (1, 0, 0),
    (-1, 0, 0),
    (0, 1, 0),
    (0, -1, 0),
    (0, 0, 1),
    (0, 0, -1),
    (1, 1, 0),
    (-1, -1, 0),
    (1, -1, 0),
    (-1, 1, 0),
    (1, 0, 1),
    (-1, 0, -1),
    (1, 0, -1),
    (-1, 0, 1),
    (0, 1, 1),
    (0, -1, -1),
    (0, 1, -1),
    (0, -1, 1),
]
WEIGHTS = [1.0 / 3.0] + [1.0 / 18.0] * 6 + [1.0 / 36.0] * 12
OPPOSITE = [VELOCITIES.index((-v[0], -v[1], -v[2])) for v in VELOCITIES]
OUTGOING = [
    [q for q in range(19) if VELOCITIES[q][face // 2] == 2 * (face % 2) - 1] for face in range(6)
]
OMEGA_FINE = 1.25
OMEGA_COARSE = 1.0 / 0.65
INFLOW = 0.05
F32 = jnp.float32
FIELD = (19, 16, 256)
CELL_ROWS = (19, 32, 128)
SLOT1 = (32, 15, 2, 128)
SLOT2 = (32, 5, 4, 128)
SLOT3 = 16
FINE_LINKS, COARSE_LINKS, PARENT, CHILDREN, OCTANTS = (0, 0), (0, 1), (6, 0), (0, 2), (7, 32)


def inflow_value(q):
    along = VELOCITIES[q][0] * INFLOW
    return WEIGHTS[q] * (1.0 + 3.0 * along + 4.5 * along * along - 1.5 * INFLOW * INFLOW)


def iota(shape, dim):
    return lax.broadcasted_iota(jnp.int32, shape, dim)


def tile(value, row, half):
    return value[8 * row : 8 * row + 8, 128 * half : 128 * half + 128]


def join(tiles):
    return jnp.concatenate([jnp.concatenate(line, axis=1) for line in tiles], axis=0)


def pick(value, index, axis):
    return jnp.take_along_axis(value, index, axis=axis, mode="promise_in_bounds")


def sums(f):
    density = f[0]
    for q in range(1, 19):
        density = density + f[q]
    momentum = []
    for axis in range(3):
        plus = [f[q] for q in range(19) if VELOCITIES[q][axis] == 1]
        minus = [f[q] for q in range(19) if VELOCITIES[q][axis] == -1]
        total = plus[0] - minus[0]
        for a, b in zip(plus[1:], minus[1:]):
            total = total + (a - b)
        momentum.append(total)
    return density, momentum


def moments(f):
    density, momentum = sums(f)
    inverse = 1.0 / density
    return density, [m * inverse for m in momentum]


def equilibrium(density, u, chosen):
    base = 1.0 - 1.5 * (u[0] * u[0] + u[1] * u[1] + u[2] * u[2])
    scaled = {}
    for q in chosen:
        if WEIGHTS[q] not in scaled:
            scaled[WEIGHTS[q]] = WEIGHTS[q] * density
    even, out = {}, {}
    for q in chosen:
        v = VELOCITIES[q]
        weight = scaled[WEIGHTS[q]]
        if q == 0:
            out[q] = weight * base
            continue
        lead = q if q % 2 == 1 else q - 1
        if lead not in even:
            along = None
            for axis in range(3):
                c = VELOCITIES[lead][axis]
                if c != 0:
                    if along is None:
                        along = u[axis]
                    else:
                        along = along + u[axis] if c > 0 else along - u[axis]
            even[lead] = (base + 4.5 * along * along, 3.0 * along)
        part, odd = even[lead]
        out[q] = weight * (part + odd) if q == lead else weight * (part - odd)
    return out


def collide(f, omega):
    density, u = moments(f)
    rest = equilibrium(density, u, range(19))
    return [(1.0 - omega) * f[q] + omega * rest[q] for q in range(19)]


def row_parts(top, bottom, lane, sub):
    both = jnp.where(sub < 4, jnp.broadcast_to(top, (8, 128)), jnp.broadcast_to(bottom, (8, 128)))
    return pick(both, 32 * (sub & 3) + (lane & 31), 1)


def pack_face(post, face):
    axis, side = face // 2, face % 2
    lane = iota((8, 128), 1)
    sub = iota((8, 128), 0)
    chosen = [post[q] for q in OUTGOING[face]]
    if axis == 0:
        at = 15 * side
        rows = [[f[at : at + 1, 128 * h : 128 * h + 128] for h in range(2)] for f in chosen]
        first = None
        for i in range(4):
            for half in range(2):
                line = jnp.broadcast_to(rows[i][half], (8, 128))
                first = line if first is None else jnp.where(sub == 2 * i + half, line, first)
        return first, row_parts(rows[4][0], rows[4][1], lane, sub)
    strips = []
    for f in chosen:
        for row in range(2):
            if axis == 1:
                strips.append(pick(tile(f, row, side), (lane & 15) + 112 * side, 1))
            else:
                index = (lane & 7) * 16 + 15 * side
                a = pick(tile(f, row, 0), index, 1)
                b = pick(tile(f, row, 1), index, 1)
                strips.append(jnp.where((lane & 15) < 8, a, b))
    first = strips[0]
    for t in range(1, 8):
        first = jnp.where((lane >> 4) == t, strips[t], first)
    second = jnp.where(((lane >> 4) & 1) == 0, strips[8], strips[9])
    return first, second


def unpack_face(first, second, offset, face):
    axis, side = face // 2, face % 2
    lane = iota((8, 128), 1)
    out = {}
    for i, q in enumerate(OUTGOING[face ^ 1]):
        if axis == 0:
            halves = []
            for half in range(2):
                if i < 4:
                    line = jnp.broadcast_to(first[2 * i + half : 2 * i + half + 1, :], (8, 128))
                else:
                    line = pick(pick(second, offset + (lane & 31), 1), 4 * half + (lane >> 5), 0)
                halves.append(line)
            out[q] = join([halves, halves])
            continue
        rows = []
        for row in range(2):
            source, base = (first, 16 * (2 * i + row)) if i < 4 else (second, offset + 16 * row)
            if axis == 1:
                piece = pick(source, base + (lane & 15), 1)
                rows.append([piece, piece])
            else:
                step = 1 if side == 0 else 15
                rows.append(
                    [
                        pick(source, base + ((8 * half + (lane >> 4) + step) & 15), 1)
                        for half in range(2)
                    ]
                )
        out[q] = join(rows)
    return out


def join_rows(upper, lower):
    return jnp.concatenate([upper, lower], axis=0)


def shell_places(lane):
    entry = lane - jnp.where(lane < 120, 96, 120)
    along_z = (1 + (entry >> 2)) * 16 + 8 * ((entry >> 1) & 1) + 7 * (entry & 1)
    part = lane & 31
    return jnp.where(lane < 96, part + 96 * (part >> 4), along_z)


def pack_thin_shell(pair):
    lane = iota((8, 128), 1)
    sub = iota((8, 128), 0)
    a, b = pair
    index = shell_places(lane) & 127
    first = (lane < 64) | ((lane >= 96) & (lane < 120))
    inside = jnp.where(first, pick(a, index, 1), pick(b, index, 1))
    entry = 8 + (lane & 15)
    rest = pick(b, (1 + (entry >> 2)) * 16 + 8 * ((entry >> 1) & 1) + 7 * (entry & 1), 1)
    block = ((lane >> 4) - 2) & 3
    rest = pick(rest, jnp.where(sub == 0, 1, 4) + block, 0)
    shared = jnp.where((sub == 0) | (sub == 7), rest, inside)
    rows = jnp.concatenate([a[0:1], a[7:8], b[0:1], b[7:8]], axis=0)
    return shared, rows


def unpack_thin_shell(shared, rows):
    lane = iota((8, 128), 1)
    sub = iota((8, 128), 0)
    rows = join_rows(rows, rows)
    edge = (lane & 15) + jnp.where(lane >= 112, 16, 0)
    z = lane & 15
    entry = 4 * ((lane >> 4) - 1) + 2 * (z >> 3) + jnp.where((z & 7) == 7, 1, 0)
    on_y = (lane < 16) | (lane >= 112)
    block = sub - jnp.where(sub > 3, 4, 1)
    moved = pick(pick(shared, jnp.where(sub <= 3, 0, 7), 0), (24 + 16 * block + entry) & 127, 1)
    out = []
    for k in range(2):
        start = 96 if k == 0 else 120
        tile_k = pick(shared, jnp.where(on_y, 32 + 32 * k + edge, start + entry) & 127, 1)
        if k == 1:
            tile_k = jnp.where(on_y | (entry < 8), tile_k, moved)
        line = pick(rows, 2 * k + jnp.where(sub == 7, 1, 0), 0)
        out.append(jnp.where((sub == 0) | (sub == 7), line, tile_k))
    return out


def z_place(entry):
    return ((1 + (entry >> 2)) * 16 + 8 * ((entry >> 1) & 1) + 7 * (entry & 1)) & 127


def pack_shell(pair):
    lane = iota((8, 128), 1)
    sub = iota((8, 128), 0)
    a, b = pair
    part = lane & 31
    along_y = part + 96 * (part >> 4)
    inside = jnp.where(lane < 96, pick(a, along_y, 1), pick(b, along_y, 1))
    sixth = jnp.full((8, 128), 6, jnp.int32)
    last = [pick(pick(t, z_place(part), 1), sixth, 0) for t in pair]
    shared = jnp.where(sub == 0, last[0], jnp.where(sub == 7, last[1], inside))
    rows = jnp.concatenate([a[0:1], a[7:8], b[0:1], b[7:8]], axis=0)
    block = (lane * 171) >> 12
    lines = [pick(pick(t, z_place(lane - 24 * block), 1), 1 + block, 0) for t in pair]
    return shared, rows, jnp.concatenate([lines[0][0:1], lines[1][0:1]], axis=0)


def unpack_shell(shared, rows, extra):
    lane = iota((8, 128), 1)
    sub = iota((8, 128), 0)
    rows = join_rows(rows, rows)
    extra = jnp.concatenate([extra] * 4, axis=0)
    edge = (lane & 15) + jnp.where(lane >= 112, 16, 0)
    z = lane & 15
    entry = 4 * ((lane >> 4) - 1) + 2 * (z >> 3) + jnp.where((z & 7) == 7, 1, 0)
    on_y = (lane < 16) | (lane >= 112)
    place = (jnp.where(sub == 6, 64, 24 * (sub - 1)) + entry) & 127
    out = []
    for k in range(2):
        whole = jnp.full((8, 128), k, jnp.int32)
        source = jnp.where(sub == 6, pick(shared, 7 * whole, 0), pick(extra, whole, 0))
        along_z = pick(source, place, 1)
        along_y = pick(shared, 64 + 32 * k + edge, 1)
        line = pick(rows, 2 * k + jnp.where(sub == 7, 1, 0), 0)
        tile_k = jnp.where(on_y, along_y, along_z)
        out.append(jnp.where((sub == 0) | (sub == 7), line, tile_k))
    return out


def shifted(value, v):
    if v[0] != 0:
        value = pltpu.roll(value, v[0] % 16, 0)
    lanes = (16 * v[1] + v[2]) % 256
    if lanes != 0:
        value = pltpu.roll(value, lanes, 1)
    return value


def positions():
    row = iota((16, 256), 0)
    lane = iota((16, 256), 1)
    return row, lane >> 4, lane & 15


def wall_weights(depth):
    place = positions()
    solid = depth <= 0
    here = depth.astype(F32)
    out = [jnp.where(solid, 1.0, 0.0).astype(F32)]
    for q in range(1, 19):
        v = VELOCITIES[q]
        outside = []
        for axis in range(3):
            if v[axis] != 0:
                outside.append(place[axis] == (0 if v[axis] > 0 else 15))
        away = outside[0] if len(outside) == 1 else outside[0] | outside[1]
        there = shifted(here, v)
        wall = (there <= 0.0) & jnp.logical_not(away) & jnp.logical_not(solid)
        gap = jnp.where(wall, here - there, 1.0)
        own = jnp.where(wall, here, 1.0)
        far = own + own >= gap
        weight = jnp.where(far, 0.5 * gap, 2.0 * own) / jnp.where(far, own, gap)
        value = jnp.where(wall, weight, -1.0)
        if len(outside) == 2:
            value = jnp.where(outside[0] & outside[1], 1.0, value)
        out.append(value)
    return out


def stream(post, start, weights, ghosts):
    place = positions()
    solid = weights(0) > 0.5
    out = [jnp.where(solid, start(0), post(0))]
    for q in range(1, 19):
        v = VELOCITIES[q]
        own = post(q)
        value = own
        for axis in (1, 0, 2):
            if v[axis] != 0:
                edge = place[axis] == (15 if v[axis] > 0 else 0)
                value = jnp.where(edge, ghosts[axis][q], value)
        value = shifted(value, v)
        weight = weights(q)
        value = jnp.where(weight >= 0.0, own + weight * (post(OPPOSITE[q]) - own), value)
        out.append(jnp.where(solid, start(q), value))
    return out


def pack_octants(fields):
    low = (iota((8, 128), 1) & 15) < 8
    out = {}
    for ox in range(2):
        for oy in range(2):
            a, b, c, d = [tile(f, ox, oy) for f in fields]
            out[4 * ox + 2 * oy] = (
                jnp.where(low, a, pltpu.roll(b, 8, 1)),
                jnp.where(low, c, pltpu.roll(d, 8, 1)),
            )
            out[4 * ox + 2 * oy + 1] = (
                jnp.where(low, pltpu.roll(a, 120, 1), b),
                jnp.where(low, pltpu.roll(c, 120, 1), d),
            )
    return out


def tile_lines(tiles):
    lane = iota((8, 128), 1)

    def at_x(k, half, inner):
        return pick(tiles[k // 2], (4 * half + (lane >> 5)) * 16 + inner, 1)

    def row_of(k, half, side):
        return jnp.full((8, 128), 7 * side, jnp.int32)

    def at_y(k, side, inner):
        return pick(tiles[k // 2], 112 * side + inner, 1)

    def at_z(k, y, side):
        return pick(tiles[k // 2], 16 * y + 8 * (k % 2) + 7 * side, 1)

    return at_x, row_of, at_y, at_z


def below(lines):
    at_x, row_of, at_y, at_z = lines
    lane = iota((8, 128), 1)
    sub = iota((8, 128), 0)
    z = lane & 15
    fields = [[], [], []]
    for k in range(4):
        inner = (z >> 1) + 8 * (k % 2)
        tiles = [[None, None], [None, None]]
        for half in range(2):
            rows = at_x(k, half, inner)
            for row in range(2):
                tiles[row][half] = pick(rows, row_of(k, half, 1 - row), 0)
        fields[0].append(join(tiles))
        for half in range(2):
            line = at_y(k, 1 - half, inner)
            for row in range(2):
                tiles[row][half] = pick(line, 4 * row + (sub >> 1), 0)
        fields[1].append(join(tiles))
        for half in range(2):
            y = 8 * half + (lane >> 4)
            far = z == 15
            line = at_z(k, ((y + jnp.where(far, 1, 15)) & 15) >> 1, jnp.where(far, 0, 1))
            for row in range(2):
                tiles[row][half] = pick(line, 4 * row + (sub >> 1), 0)
        fields[2].append(join(tiles))
    out = []
    for axis in range(3):
        chosen = [q for q in range(19) if VELOCITIES[q][axis] != 0]
        out.append(equilibrium(fields[axis][0], fields[axis][1:], chosen))
    return out


def restrict(f):
    lane = iota((8, 128), 1)
    sub = iota((8, 128), 0)
    density, momentum = sums(f)
    index = ((lane >> 4) & 3) * 32 + (lane & 7) * 2
    even = (2 * sub) & 7
    packed = []
    for field in [density] + momentum:
        halves = []
        for half in range(2):
            lines = [
                jnp.where(
                    sub < 4,
                    pick(tile(field, 0, half), even + odd, 0),
                    pick(tile(field, 1, half), even + odd, 0),
                )
                for odd in range(2)
            ]
            line = lines[0] + lines[1]
            parts = [pick(line, index + step, 1) for step in (0, 1, 16, 17)]
            halves.append(0.125 * ((parts[0] + parts[1]) + (parts[2] + parts[3])))
        packed.append(jnp.where(lane < 64, halves[0], halves[1]))
    low = (lane & 15) < 8
    return jnp.where(low, packed[0], packed[1]), jnp.where(low, packed[2], packed[3])


def load(ref):
    return [ref[q] for q in range(19)]


def load_cells(ref, q):
    halves = [ref[q, pl.ds(half, 16, stride=2), :] for half in range(2)]
    return jnp.concatenate(halves, axis=1)


def store_cells(ref, q, value):
    for half in range(2):
        ref[q, pl.ds(half, 16, stride=2), :] = value[:, 128 * half : 128 * half + 128]


def store_octants(fields, octs):
    for o, pair in pack_octants(fields).items():
        shared, rows, extra = pack_shell(pair)
        for part in range(4):
            octs[o, part] = shared[2 * part : 2 * part + 2]
        for part in range(2):
            octs[o, 4 + part] = rows[2 * part : 2 * part + 2]
        octs[o, 6] = extra


def give_octants(octs, parents, out):
    for d in range(32):
        o = parents[1, 0, d]
        out[d, 8:12, :, 64:128] = octs[o, 0:4, :, 64:128]
        out[d, 12:15] = octs[o, 4:7]


def give_face(post, face, code, me, out, at, lanes):
    first, second = pack_face(post, face)
    slot = jnp.where(code >= 0, code, me)
    for part in range(4):
        rows = slice(2 * part, 2 * part + 2)
        out[slot, at + part] = first[rows]
        out[slot, 8 + part, :, lanes : lanes + 32] = second[rows, lanes : lanes + 32]
    return first, second


def rows_of_pairs(ref, slot, at):
    return jnp.concatenate([ref[slot, at + part] for part in range(4)], axis=0)


def send_kernel(
    coarse_in, fine_in, coarse_table, fine_table, parent_table, out, region_out,
    coarse, fine, coarse_links, fine_links, parents, slots, region, octs, sems,
):
    fetch = [
        pltpu.make_async_copy(source, target, sems.at[i])
        for i, (source, target) in enumerate(
            (
                (coarse_in, coarse),
                (coarse_table, coarse_links),
                (fine_in, fine),
                (fine_table, fine_links),
                (parent_table, parents),
            )
        )
    ]
    for copy in fetch:
        copy.start()

    def put(part):
        rows = pl.ds(4 * part, 4 if part < 3 else 3)
        return pltpu.make_async_copy(slots.at[:, rows], out.at[:, rows], sems.at[5 + part])

    me = lax.axis_index("dev")
    fetch[0].wait()
    fetch[1].wait()
    f = [load_cells(coarse, q) for q in range(19)]
    density, u = moments(f)
    store_octants([density] + u, octs)
    post = collide(f, OMEGA_COARSE)
    for face in range(6):
        first, second = give_face(post, face, coarse_links[face, 0, me], me, slots, 0, 0)
        if face in (2, 3):
            region[face - 2, 0:8, :] = first
            region[face - 2, 8:16, :] = second
    put(0).start()
    beside = pltpu.make_async_copy(region, region_out, sems.at[9])
    beside.start()
    fetch[4].wait()
    give_octants(octs, parents, slots)
    put(3).start()
    fetch[2].wait()
    fetch[3].wait()
    post = collide([load_cells(fine, q) for q in range(19)], OMEGA_FINE)
    for face in range(6):
        give_face(post, face, fine_links[face, 0, me], me, slots, 4, 32)
    put(1).start()
    put(2).start()
    for part in range(4):
        put(part).wait()
    beside.wait()


def prepare_kernel(state, depth, post, start, weights, *, omega):
    f = [load_cells(state, q) for q in range(19)]
    for q in range(19):
        start[q] = f[q]
    for q, value in enumerate(collide(f, omega)):
        post[q] = value
    halves = [depth[pl.ds(half, 16, stride=2), :] for half in range(2)]
    for q, value in enumerate(wall_weights(jnp.concatenate(halves, axis=1))):
        weights[q] = value


def codes_kernel(coarse_links, fine_links, parents, codes):
    me = lax.axis_index("dev")
    lane = iota((1, 32), 1)
    place = [iota((8, 128), 0), iota((8, 128), 1)]
    owner, octant = parents[0], parents[1]

    def own(line):
        return jnp.sum(jnp.where(lane == me, line, 0), axis=1, keepdims=True)

    values = {}
    for face in range(6):
        values[FINE_LINKS[0] + face, FINE_LINKS[1]] = own(fine_links[face])
        values[COARSE_LINKS[0] + face, COARSE_LINKS[1]] = own(coarse_links[face])
    values[PARENT] = own(owner)
    for o in range(8):
        child = jnp.where((owner == me) & (octant == o), lane, -1)
        values[CHILDREN[0] + o, CHILDREN[1]] = jnp.max(child, axis=1, keepdims=True)
    tile_of = jnp.zeros((8, 128), jnp.int32)
    for (row, at), value in values.items():
        tile_of = jnp.where((place[0] == row) & (place[1] == at), value, tile_of)
    codes[...] = tile_of
    row, at = OCTANTS
    codes[row : row + 1, at : at + 32] = octant


class Codes:
    def __init__(self, ref):
        self.tile = ref[...]
        self.seen = {}

    def __call__(self, start, step=0):
        row, at = (start[0], start[1] + step) if start == OCTANTS else (start[0] + step, start[1])
        if (row, at) not in self.seen:
            self.seen[row, at] = self.tile[row, at]
        return self.seen[row, at]


def merge_ghosts(take):
    ghosts = [{}, {}, {}]
    for face in range(6):
        ghosts[face // 2].update(take(face))
    return ghosts


def fine_ghosts(codes, plane_of, lanes, under):
    def take(face):
        code = codes(FINE_LINKS, face)
        first, second = plane_of(jnp.maximum(code, 0))
        plane = unpack_face(first, second, lanes, face)
        return {q: jnp.where(code >= 0, plane[q], under[face // 2][q]) for q in plane}

    return merge_ghosts(take)


def middle_kernel(
    received, from_low, from_high, c_post, c_start, c_weights, f_post, f_start, f_weights,
    table, out, coarse_new, state, post, octs,
):
    me = lax.axis_index("dev")
    codes = Codes(table)

    def coarse_ghost(face):
        code = codes(COARSE_LINKS, face)
        slot = jnp.maximum(code, 0)
        first = rows_of_pairs(received, slot, 0)
        second = rows_of_pairs(received, slot, 8)
        if face in (2, 3):
            beside = from_low if face == 2 else from_high
            first = jnp.where(code == -2, beside[0, 0:8, :], first)
            second = jnp.where(code == -2, beside[0, 8:16, :], second)
        plane = unpack_face(first, second, 0, face)
        return {q: jnp.where(code == -1, inflow_value(q), plane[q]) for q in plane}

    new = stream(
        lambda q: c_post[q], lambda q: c_start[q], lambda q: c_weights[q], merge_ghosts(coarse_ghost)
    )
    for q in range(19):
        coarse_new[q] = new[q]
    old_density, old_u = moments([c_start[q] for q in range(19)])
    density, u = moments(new)
    mid = [0.5 * (old_density + density)] + [0.5 * (a + b) for a, b in zip(old_u, u)]
    for o, pair in pack_octants(mid).items():
        shared, rows = pack_thin_shell(pair)
        octs[o, 0] = shared[0:4]
        octs[o, 1] = shared[4:8]
        octs[o, 2] = rows
    parent = codes(PARENT)
    rows = join_rows(received[parent, 12], received[parent, 13])
    shell = unpack_shell(rows_of_pairs(received, parent, 8), rows, received[parent, 14])
    under = below(tile_lines(shell))
    ghosts = fine_ghosts(
        codes,
        lambda d: (rows_of_pairs(received, d, 4), rows_of_pairs(received, d, 8)),
        32,
        under,
    )
    new = stream(lambda q: f_post[q], lambda q: f_start[q], lambda q: f_weights[q], ghosts)
    for q in range(19):
        state[q] = new[q]
    after = collide(new, OMEGA_FINE)
    for q in range(19):
        post[q] = after[q]
    for face in range(6):
        first, second = pack_face(after, face)
        code = codes(FINE_LINKS, face)
        slot = jnp.where(code >= 0, code, me)
        for part in range(2):
            out[slot, part] = first[4 * part : 4 * part + 4]
            out[slot, 2 + part, :, 0:32] = second[4 * part : 4 * part + 4, 0:32]
    for d in range(32):
        o = codes(OCTANTS, d)
        out[d, 2, :, 32:128] = octs[o, 0, :, 32:128]
        out[d, 3, :, 32:128] = octs[o, 1, :, 32:128]
        out[d, 4] = octs[o, 2]


def last_kernel(received, f_post, f_start, f_weights, table, out, state):
    codes = Codes(table)
    def rows_of(d, part):
        return join_rows(received[d, part], received[d, part + 1])

    parent = codes(PARENT)
    under = below(tile_lines(unpack_thin_shell(rows_of(parent, 2), received[parent, 4])))
    ghosts = fine_ghosts(codes, lambda d: (rows_of(d, 0), rows_of(d, 2)), 0, under)
    new = stream(lambda q: f_post[q], lambda q: f_start[q], lambda q: f_weights[q], ghosts)
    for q in range(19):
        state[q] = new[q]
    first, second = restrict(new)
    out[parent, 0:8, :] = first
    out[parent, 8:16, :] = second


def cover(codes):
    low = (iota((8, 128), 1) & 15) < 8
    tiles = [[None, None], [None, None]]
    for ox in range(2):
        for oy in range(2):
            o = 4 * ox + 2 * oy
            tiles[ox][oy] = jnp.where(low, codes(CHILDREN, o), codes(CHILDREN, o + 1))
    return join(tiles) >= 0


def final_kernel(received, state, coarse_new, table, fine_out, coarse_out, f_cells, c_cells, sems):
    codes = Codes(table)
    for q in range(19):
        store_cells(f_cells, q, state[q])
    fine_copy = pltpu.make_async_copy(f_cells, fine_out, sems.at[0])
    fine_copy.start()
    low = (iota((8, 128), 1) & 15) < 8
    tiles = [[[None, None], [None, None]] for _ in range(4)]
    for ox in range(2):
        for oy in range(2):
            o = 4 * ox + 2 * oy
            near = jnp.maximum(codes(CHILDREN, o), 0)
            far = jnp.maximum(codes(CHILDREN, o + 1), 0)
            for k in range(2):
                a = received[near, 8 * k : 8 * k + 8, :]
                b = received[far, 8 * k : 8 * k + 8, :]
                tiles[2 * k][ox][oy] = jnp.where(low, a, pltpu.roll(b, 8, 1))
                tiles[2 * k + 1][ox][oy] = jnp.where(low, pltpu.roll(a, 120, 1), b)
    density, jx, jy, jz = [join(t) for t in tiles]
    covered = cover(codes)
    density = jnp.where(covered, density, 1.0)
    inverse = 1.0 / density
    fine_eq = equilibrium(density, [jx * inverse, jy * inverse, jz * inverse], range(19))
    new = load(coarse_new)
    own_density, own_u = moments(new)
    own_eq = equilibrium(own_density, own_u, range(19))
    for q in range(19):
        store_cells(c_cells, q, new[q] + jnp.where(covered, fine_eq[q] - own_eq[q], 0.0))
    coarse_copy = pltpu.make_async_copy(c_cells, coarse_out, sems.at[1])
    coarse_copy.start()
    fine_copy.wait()
    coarse_copy.wait()


VMEM = pl.BlockSpec(memory_space=pltpu.VMEM)
HBM = pl.BlockSpec(memory_space=pltpu.HBM)
SOME_VMEM = 24 * 1024 * 1024
MOST_VMEM = 60 * 1024 * 1024


OCTS = pltpu.VMEM((8, 7, 2, 128), F32)
LINKS = pltpu.SMEM((6, 1, 32), jnp.int32)
SEND_SCRATCH = [
    pltpu.VMEM(CELL_ROWS, F32),
    pltpu.VMEM(CELL_ROWS, F32),
    LINKS,
    LINKS,
    pltpu.SMEM((2, 1, 32), jnp.int32),
    pltpu.VMEM(SLOT1, F32),
    pltpu.VMEM((2, 16, 128), F32),
    OCTS,
    pltpu.SemaphoreType.DMA((10,)),
]
FINAL_SCRATCH = [
    pltpu.VMEM(CELL_ROWS, F32),
    pltpu.VMEM(CELL_ROWS, F32),
    pltpu.SemaphoreType.DMA((2,)),
]


def call(kernel, outs, ins, hbm=(), hbm_outs=(), scratch=(), vmem=SOME_VMEM, name=None):
    return pl.pallas_call(
        kernel,
        out_shape=[jax.ShapeDtypeStruct(s, F32) for s in outs],
        in_specs=[HBM if i in hbm else VMEM for i in range(len(ins))],
        out_specs=[HBM if i in hbm_outs else VMEM for i in range(len(outs))],
        scratch_shapes=list(scratch),
        compiler_params=pltpu.CompilerParams(vmem_limit_bytes=vmem),
        cost_estimate=pl.CostEstimate(
            flops=2_000_000, bytes_accessed=2_000_000, transcendentals=0
        ),
        name=name,
    )(*ins)


def swap(value):
    return lax.all_to_all(value, "dev", split_axis=0, concat_axis=0, tiled=True)


def body(fine_state, coarse_state, fine_depth, coarse_depth, fine_links, coarse_links, parents):
    count = lax.axis_size("group")
    fine_state, coarse_state = fine_state.reshape(CELL_ROWS), coarse_state.reshape(CELL_ROWS)
    fine_depth, coarse_depth = fine_depth.reshape(32, 128), coarse_depth.reshape(32, 128)
    fine_links = fine_links.transpose(2, 0, 1)
    coarse_links = coarse_links.transpose(2, 0, 1)
    parents = parents.transpose(2, 0, 1)
    sent, region = call(
        send_kernel,
        [SLOT1, (2, 16, 128)],
        [coarse_state, fine_state, coarse_links, fine_links, parents],
        hbm=(0, 1, 2, 3, 4),
        hbm_outs=(0, 1),
        scratch=SEND_SCRATCH,
        vmem=MOST_VMEM,
        name="send",
    )
    up = [(i, i + 1) for i in range(count - 1)]
    down = [(b, a) for a, b in up]
    received = swap(sent)
    from_low = lax.ppermute(region[1:2], "group", up)
    from_high = lax.ppermute(region[0:1], "group", down)

    def prepare(state, depth, omega, name):
        def kernel(*refs):
            prepare_kernel(*refs, omega=omega)

        return call(kernel, [FIELD, FIELD, FIELD], [state, depth], name=name)

    c_post, c_start, c_weights = prepare(coarse_state, coarse_depth, OMEGA_COARSE, "prepare_coarse")
    f_post, f_start, f_weights = prepare(fine_state, fine_depth, OMEGA_FINE, "prepare_fine")
    codes = pl.pallas_call(
        codes_kernel,
        out_shape=jax.ShapeDtypeStruct((8, 128), jnp.int32),
        in_specs=[VMEM] * 3,
        out_specs=VMEM,
        compiler_params=pltpu.CompilerParams(vmem_limit_bytes=SOME_VMEM),
        name="codes",
    )(coarse_links, fine_links, parents)
    sent, coarse_new, state, post = call(
        middle_kernel,
        [SLOT2, FIELD, FIELD, FIELD],
        [
            received, from_low, from_high, c_post, c_start, c_weights, f_post, f_start, f_weights,
            codes,
        ],
        scratch=[pltpu.VMEM((8, 3, 4, 128), F32)],
        name="middle",
    )
    received = swap(sent)
    sent, state = call(
        last_kernel,
        [(32, SLOT3, 128), FIELD],
        [received, post, state, f_weights, codes],
        name="last",
    )
    received = swap(sent)
    fine_out, coarse_out = call(
        final_kernel,
        [CELL_ROWS, CELL_ROWS],
        [received, state, coarse_new, codes],
        hbm_outs=(0, 1),
        scratch=FINAL_SCRATCH,
        name="final",
    )
    return fine_out.reshape(1, 19, 4096), coarse_out.reshape(1, 19, 4096)


def solution(mesh):
    placed = (
        P(("group", "dev"), None, None),
        P(("group", "dev"), None, None),
        P(("group", "dev"), None),
        P(("group", "dev"), None),
        P("group", None, None),
        P("group", None, None),
        P("group", None, None),
    )
    return jax.shard_map(
        body,
        mesh=mesh,
        in_specs=placed,
        out_specs=(P(("group", "dev"), None, None), P(("group", "dev"), None, None)),
        check_vma=False,
    )
```

```python
import jax
import jax.numpy as jnp
from jax import lax
from jax.experimental import pallas as pl
from jax.experimental.pallas import tpu as pltpu
from jax.sharding import PartitionSpec as P

VELOCITIES = [
    (0, 0, 0),
    (1, 0, 0),
    (-1, 0, 0),
    (0, 1, 0),
    (0, -1, 0),
    (0, 0, 1),
    (0, 0, -1),
    (1, 1, 0),
    (-1, -1, 0),
    (1, -1, 0),
    (-1, 1, 0),
    (1, 0, 1),
    (-1, 0, -1),
    (1, 0, -1),
    (-1, 0, 1),
    (0, 1, 1),
    (0, -1, -1),
    (0, 1, -1),
    (0, -1, 1),
]
WEIGHTS = [1.0 / 3.0] + [1.0 / 18.0] * 6 + [1.0 / 36.0] * 12
OPPOSITE = [VELOCITIES.index((-v[0], -v[1], -v[2])) for v in VELOCITIES]
OUTGOING = [
    [q for q in range(19) if VELOCITIES[q][face // 2] == 2 * (face % 2) - 1] for face in range(6)
]
OMEGA_FINE = 1.25
OMEGA_COARSE = 1.0 / 0.65
INFLOW = 0.05
F32 = jnp.float32
FIELD = (19, 16, 256)
CELL_ROWS = (19, 32, 128)
SLOT1 = (32, 15, 2, 128)
SLOT2 = (32, 5, 4, 128)
SLOT3 = 16
FINE_LINKS, COARSE_LINKS, PARENT, CHILDREN, OCTANTS = (0, 0), (0, 1), (6, 0), (0, 2), (7, 32)


def inflow_value(q):
    along = VELOCITIES[q][0] * INFLOW
    return WEIGHTS[q] * (1.0 + 3.0 * along + 4.5 * along * along - 1.5 * INFLOW * INFLOW)


def iota(shape, dim):
    return lax.broadcasted_iota(jnp.int32, shape, dim)


def tile(value, row, half):
    return value[8 * row : 8 * row + 8, 128 * half : 128 * half + 128]


def join(tiles):
    return jnp.concatenate([jnp.concatenate(line, axis=1) for line in tiles], axis=0)


def pick(value, index, axis):
    return jnp.take_along_axis(value, index, axis=axis, mode="promise_in_bounds")


def sums(f):
    density = f[0]
    for q in range(1, 19):
        density = density + f[q]
    momentum = []
    for axis in range(3):
        plus = [f[q] for q in range(19) if VELOCITIES[q][axis] == 1]
        minus = [f[q] for q in range(19) if VELOCITIES[q][axis] == -1]
        total = plus[0] - minus[0]
        for a, b in zip(plus[1:], minus[1:]):
            total = total + (a - b)
        momentum.append(total)
    return density, momentum


def moments(f):
    density, momentum = sums(f)
    inverse = 1.0 / density
    return density, [m * inverse for m in momentum]


def equilibrium(density, u, chosen):
    base = 1.0 - 1.5 * (u[0] * u[0] + u[1] * u[1] + u[2] * u[2])
    scaled = {}
    for q in chosen:
        if WEIGHTS[q] not in scaled:
            scaled[WEIGHTS[q]] = WEIGHTS[q] * density
    even, out = {}, {}
    for q in chosen:
        v = VELOCITIES[q]
        weight = scaled[WEIGHTS[q]]
        if q == 0:
            out[q] = weight * base
            continue
        lead = q if q % 2 == 1 else q - 1
        if lead not in even:
            along = None
            for axis in range(3):
                c = VELOCITIES[lead][axis]
                if c != 0:
                    if along is None:
                        along = u[axis]
                    else:
                        along = along + u[axis] if c > 0 else along - u[axis]
            even[lead] = (base + 4.5 * along * along, 3.0 * along)
        part, odd = even[lead]
        out[q] = weight * (part + odd) if q == lead else weight * (part - odd)
    return out


def collide(f, omega):
    density, u = moments(f)
    rest = equilibrium(density, u, range(19))
    return [(1.0 - omega) * f[q] + omega * rest[q] for q in range(19)]


def row_parts(top, bottom, lane, sub):
    both = jnp.where(sub < 4, jnp.broadcast_to(top, (8, 128)), jnp.broadcast_to(bottom, (8, 128)))
    return pick(both, 32 * (sub & 3) + (lane & 31), 1)


def pack_face(post, face):
    axis, side = face // 2, face % 2
    lane = iota((8, 128), 1)
    sub = iota((8, 128), 0)
    chosen = [post[q] for q in OUTGOING[face]]
    if axis == 0:
        at = 15 * side
        rows = [[f[at : at + 1, 128 * h : 128 * h + 128] for h in range(2)] for f in chosen]
        first = None
        for i in range(4):
            for half in range(2):
                line = jnp.broadcast_to(rows[i][half], (8, 128))
                first = line if first is None else jnp.where(sub == 2 * i + half, line, first)
        return first, row_parts(rows[4][0], rows[4][1], lane, sub)
    strips = []
    for f in chosen:
        for row in range(2):
            if axis == 1:
                strips.append(pick(tile(f, row, side), (lane & 15) + 112 * side, 1))
            else:
                index = (lane & 7) * 16 + 15 * side
                a = pick(tile(f, row, 0), index, 1)
                b = pick(tile(f, row, 1), index, 1)
                strips.append(jnp.where((lane & 15) < 8, a, b))
    first = strips[0]
    for t in range(1, 8):
        first = jnp.where((lane >> 4) == t, strips[t], first)
    second = jnp.where(((lane >> 4) & 1) == 0, strips[8], strips[9])
    return first, second


def unpack_face(first, second, offset, face):
    axis, side = face // 2, face % 2
    lane = iota((8, 128), 1)
    out = {}
    for i, q in enumerate(OUTGOING[face ^ 1]):
        if axis == 0:
            halves = []
            for half in range(2):
                if i < 4:
                    line = jnp.broadcast_to(first[2 * i + half : 2 * i + half + 1, :], (8, 128))
                else:
                    line = pick(pick(second, offset + (lane & 31), 1), 4 * half + (lane >> 5), 0)
                halves.append(line)
            out[q] = join([halves, halves])
            continue
        rows = []
        for row in range(2):
            source, base = (first, 16 * (2 * i + row)) if i < 4 else (second, offset + 16 * row)
            if axis == 1:
                piece = pick(source, base + (lane & 15), 1)
                rows.append([piece, piece])
            else:
                step = 1 if side == 0 else 15
                rows.append(
                    [
                        pick(source, base + ((8 * half + (lane >> 4) + step) & 15), 1)
                        for half in range(2)
                    ]
                )
        out[q] = join(rows)
    return out


def join_rows(upper, lower):
    return jnp.concatenate([upper, lower], axis=0)


def shell_places(lane):
    entry = lane - jnp.where(lane < 120, 96, 120)
    along_z = (1 + (entry >> 2)) * 16 + 8 * ((entry >> 1) & 1) + 7 * (entry & 1)
    part = lane & 31
    return jnp.where(lane < 96, part + 96 * (part >> 4), along_z)


def pack_thin_shell(pair):
    lane = iota((8, 128), 1)
    sub = iota((8, 128), 0)
    a, b = pair
    index = shell_places(lane) & 127
    first = (lane < 64) | ((lane >= 96) & (lane < 120))
    inside = jnp.where(first, pick(a, index, 1), pick(b, index, 1))
    entry = 8 + (lane & 15)
    rest = pick(b, (1 + (entry >> 2)) * 16 + 8 * ((entry >> 1) & 1) + 7 * (entry & 1), 1)
    block = ((lane >> 4) - 2) & 3
    rest = pick(rest, jnp.where(sub == 0, 1, 4) + block, 0)
    shared = jnp.where((sub == 0) | (sub == 7), rest, inside)
    rows = jnp.concatenate([a[0:1], a[7:8], b[0:1], b[7:8]], axis=0)
    return shared, rows


def unpack_thin_shell(shared, rows):
    lane = iota((8, 128), 1)
    sub = iota((8, 128), 0)
    rows = join_rows(rows, rows)
    edge = (lane & 15) + jnp.where(lane >= 112, 16, 0)
    z = lane & 15
    entry = 4 * ((lane >> 4) - 1) + 2 * (z >> 3) + jnp.where((z & 7) == 7, 1, 0)
    on_y = (lane < 16) | (lane >= 112)
    block = sub - jnp.where(sub > 3, 4, 1)
    moved = pick(pick(shared, jnp.where(sub <= 3, 0, 7), 0), (24 + 16 * block + entry) & 127, 1)
    out = []
    for k in range(2):
        start = 96 if k == 0 else 120
        tile_k = pick(shared, jnp.where(on_y, 32 + 32 * k + edge, start + entry) & 127, 1)
        if k == 1:
            tile_k = jnp.where(on_y | (entry < 8), tile_k, moved)
        line = pick(rows, 2 * k + jnp.where(sub == 7, 1, 0), 0)
        out.append(jnp.where((sub == 0) | (sub == 7), line, tile_k))
    return out


def z_place(entry):
    return ((1 + (entry >> 2)) * 16 + 8 * ((entry >> 1) & 1) + 7 * (entry & 1)) & 127


def pack_shell(pair):
    lane = iota((8, 128), 1)
    sub = iota((8, 128), 0)
    a, b = pair
    part = lane & 31
    along_y = part + 96 * (part >> 4)
    inside = jnp.where(lane < 96, pick(a, along_y, 1), pick(b, along_y, 1))
    sixth = jnp.full((8, 128), 6, jnp.int32)
    last = [pick(pick(t, z_place(part), 1), sixth, 0) for t in pair]
    shared = jnp.where(sub == 0, last[0], jnp.where(sub == 7, last[1], inside))
    rows = jnp.concatenate([a[0:1], a[7:8], b[0:1], b[7:8]], axis=0)
    block = (lane * 171) >> 12
    lines = [pick(pick(t, z_place(lane - 24 * block), 1), 1 + block, 0) for t in pair]
    return shared, rows, jnp.concatenate([lines[0][0:1], lines[1][0:1]], axis=0)


def unpack_shell(shared, rows, extra):
    lane = iota((8, 128), 1)
    sub = iota((8, 128), 0)
    rows = join_rows(rows, rows)
    extra = jnp.concatenate([extra] * 4, axis=0)
    edge = (lane & 15) + jnp.where(lane >= 112, 16, 0)
    z = lane & 15
    entry = 4 * ((lane >> 4) - 1) + 2 * (z >> 3) + jnp.where((z & 7) == 7, 1, 0)
    on_y = (lane < 16) | (lane >= 112)
    place = (jnp.where(sub == 6, 64, 24 * (sub - 1)) + entry) & 127
    out = []
    for k in range(2):
        whole = jnp.full((8, 128), k, jnp.int32)
        source = jnp.where(sub == 6, pick(shared, 7 * whole, 0), pick(extra, whole, 0))
        along_z = pick(source, place, 1)
        along_y = pick(shared, 64 + 32 * k + edge, 1)
        line = pick(rows, 2 * k + jnp.where(sub == 7, 1, 0), 0)
        tile_k = jnp.where(on_y, along_y, along_z)
        out.append(jnp.where((sub == 0) | (sub == 7), line, tile_k))
    return out


def shifted(value, v):
    if v[0] != 0:
        value = pltpu.roll(value, v[0] % 16, 0)
    lanes = (16 * v[1] + v[2]) % 256
    if lanes != 0:
        value = pltpu.roll(value, lanes, 1)
    return value


def positions():
    row = iota((16, 256), 0)
    lane = iota((16, 256), 1)
    return row, lane >> 4, lane & 15


def wall_weights(depth):
    place = positions()
    solid = depth <= 0
    here = depth.astype(F32)
    out = [jnp.where(solid, 1.0, 0.0).astype(F32)]
    for q in range(1, 19):
        v = VELOCITIES[q]
        outside = []
        for axis in range(3):
            if v[axis] != 0:
                outside.append(place[axis] == (0 if v[axis] > 0 else 15))
        away = outside[0] if len(outside) == 1 else outside[0] | outside[1]
        there = shifted(here, v)
        wall = (there <= 0.0) & jnp.logical_not(away) & jnp.logical_not(solid)
        gap = jnp.where(wall, here - there, 1.0)
        own = jnp.where(wall, here, 1.0)
        far = own + own >= gap
        weight = jnp.where(far, 0.5 * gap, 2.0 * own) / jnp.where(far, own, gap)
        value = jnp.where(wall, weight, -1.0)
        if len(outside) == 2:
            value = jnp.where(outside[0] & outside[1], 1.0, value)
        out.append(value)
    return out


def stream(post, start, weights, ghosts):
    place = positions()
    solid = weights(0) > 0.5
    out = [jnp.where(solid, start(0), post(0))]
    for q in range(1, 19):
        v = VELOCITIES[q]
        own = post(q)
        value = own
        for axis in (1, 0, 2):
            if v[axis] != 0:
                edge = place[axis] == (15 if v[axis] > 0 else 0)
                value = jnp.where(edge, ghosts[axis][q], value)
        value = shifted(value, v)
        weight = weights(q)
        value = jnp.where(weight >= 0.0, own + weight * (post(OPPOSITE[q]) - own), value)
        out.append(jnp.where(solid, start(q), value))
    return out


def pack_octants(fields):
    low = (iota((8, 128), 1) & 15) < 8
    out = {}
    for ox in range(2):
        for oy in range(2):
            a, b, c, d = [tile(f, ox, oy) for f in fields]
            out[4 * ox + 2 * oy] = (
                jnp.where(low, a, pltpu.roll(b, 8, 1)),
                jnp.where(low, c, pltpu.roll(d, 8, 1)),
            )
            out[4 * ox + 2 * oy + 1] = (
                jnp.where(low, pltpu.roll(a, 120, 1), b),
                jnp.where(low, pltpu.roll(c, 120, 1), d),
            )
    return out


def tile_lines(tiles):
    lane = iota((8, 128), 1)

    def at_x(k, half, inner):
        return pick(tiles[k // 2], (4 * half + (lane >> 5)) * 16 + inner, 1)

    def row_of(k, half, side):
        return jnp.full((8, 128), 7 * side, jnp.int32)

    def at_y(k, side, inner):
        return pick(tiles[k // 2], 112 * side + inner, 1)

    def at_z(k, y, side):
        return pick(tiles[k // 2], 16 * y + 8 * (k % 2) + 7 * side, 1)

    return at_x, row_of, at_y, at_z


def below(lines):
    at_x, row_of, at_y, at_z = lines
    lane = iota((8, 128), 1)
    sub = iota((8, 128), 0)
    z = lane & 15
    fields = [[], [], []]
    for k in range(4):
        inner = (z >> 1) + 8 * (k % 2)
        tiles = [[None, None], [None, None]]
        for half in range(2):
            rows = at_x(k, half, inner)
            for row in range(2):
                tiles[row][half] = pick(rows, row_of(k, half, 1 - row), 0)
        fields[0].append(join(tiles))
        for half in range(2):
            line = at_y(k, 1 - half, inner)
            for row in range(2):
                tiles[row][half] = pick(line, 4 * row + (sub >> 1), 0)
        fields[1].append(join(tiles))
        for half in range(2):
            y = 8 * half + (lane >> 4)
            far = z == 15
            line = at_z(k, ((y + jnp.where(far, 1, 15)) & 15) >> 1, jnp.where(far, 0, 1))
            for row in range(2):
                tiles[row][half] = pick(line, 4 * row + (sub >> 1), 0)
        fields[2].append(join(tiles))
    out = []
    for axis in range(3):
        chosen = [q for q in range(19) if VELOCITIES[q][axis] != 0]
        out.append(equilibrium(fields[axis][0], fields[axis][1:], chosen))
    return out


def restrict(f):
    lane = iota((8, 128), 1)
    sub = iota((8, 128), 0)
    density, momentum = sums(f)
    index = ((lane >> 4) & 3) * 32 + (lane & 7) * 2
    even = (2 * sub) & 7
    packed = []
    for field in [density] + momentum:
        halves = []
        for half in range(2):
            lines = [
                jnp.where(
                    sub < 4,
                    pick(tile(field, 0, half), even + odd, 0),
                    pick(tile(field, 1, half), even + odd, 0),
                )
                for odd in range(2)
            ]
            line = lines[0] + lines[1]
            parts = [pick(line, index + step, 1) for step in (0, 1, 16, 17)]
            halves.append(0.125 * ((parts[0] + parts[1]) + (parts[2] + parts[3])))
        packed.append(jnp.where(lane < 64, halves[0], halves[1]))
    low = (lane & 15) < 8
    return jnp.where(low, packed[0], packed[1]), jnp.where(low, packed[2], packed[3])


def load(ref):
    return [ref[q] for q in range(19)]


def load_cells(ref, q):
    halves = [ref[q, pl.ds(half, 16, stride=2), :] for half in range(2)]
    return jnp.concatenate(halves, axis=1)


def store_cells(ref, q, value):
    for half in range(2):
        ref[q, pl.ds(half, 16, stride=2), :] = value[:, 128 * half : 128 * half + 128]


def store_octants(fields, octs):
    for o, pair in pack_octants(fields).items():
        shared, rows, extra = pack_shell(pair)
        for part in range(4):
            octs[o, part] = shared[2 * part : 2 * part + 2]
        for part in range(2):
            octs[o, 4 + part] = rows[2 * part : 2 * part + 2]
        octs[o, 6] = extra


def give_octants(octs, parents, out):
    for d in range(32):
        o = parents[1, 0, d]
        out[d, 8:12, :, 64:128] = octs[o, 0:4, :, 64:128]
        out[d, 12:15] = octs[o, 4:7]


def give_face(post, face, code, me, out, at, lanes):
    first, second = pack_face(post, face)
    slot = jnp.where(code >= 0, code, me)
    for part in range(4):
        rows = slice(2 * part, 2 * part + 2)
        out[slot, at + part] = first[rows]
        out[slot, 8 + part, :, lanes : lanes + 32] = second[rows, lanes : lanes + 32]
    return first, second


def rows_of_pairs(ref, slot, at):
    return jnp.concatenate([ref[slot, at + part] for part in range(4)], axis=0)


def send_kernel(
    coarse_in, fine_in, coarse_table, fine_table, parent_table, out, region_out,
    coarse, fine, coarse_links, fine_links, parents, slots, region, octs, sems,
):
    fetch = [
        pltpu.make_async_copy(source, target, sems.at[i])
        for i, (source, target) in enumerate(
            (
                (coarse_in, coarse),
                (coarse_table, coarse_links),
                (fine_in, fine),
                (fine_table, fine_links),
                (parent_table, parents),
            )
        )
    ]
    for copy in fetch:
        copy.start()

    def put(part):
        rows = pl.ds(4 * part, 4 if part < 3 else 3)
        return pltpu.make_async_copy(slots.at[:, rows], out.at[:, rows], sems.at[5 + part])

    me = lax.axis_index("dev")
    fetch[0].wait()
    fetch[1].wait()
    f = [load_cells(coarse, q) for q in range(19)]
    density, u = moments(f)
    store_octants([density] + u, octs)
    post = collide(f, OMEGA_COARSE)
    for face in range(6):
        first, second = give_face(post, face, coarse_links[face, 0, me], me, slots, 0, 0)
        if face in (2, 3):
            region[face - 2, 0:8, :] = first
            region[face - 2, 8:16, :] = second
    put(0).start()
    beside = pltpu.make_async_copy(region, region_out, sems.at[9])
    beside.start()
    fetch[4].wait()
    give_octants(octs, parents, slots)
    put(3).start()
    fetch[2].wait()
    fetch[3].wait()
    post = collide([load_cells(fine, q) for q in range(19)], OMEGA_FINE)
    for face in range(6):
        give_face(post, face, fine_links[face, 0, me], me, slots, 4, 32)
    put(1).start()
    put(2).start()
    for part in range(4):
        put(part).wait()
    beside.wait()


def prepare_kernel(state, depth, post, start, weights, *old, omega):
    f = [load_cells(state, q) for q in range(19)]
    for q in range(19):
        start[q] = f[q]
    for q, value in enumerate(collide(f, omega)):
        post[q] = value
    if old:
        density, u = moments(f)
        for i, value in enumerate([density] + u):
            old[0][i] = value
    halves = [depth[pl.ds(half, 16, stride=2), :] for half in range(2)]
    for q, value in enumerate(wall_weights(jnp.concatenate(halves, axis=1))):
        weights[q] = value


def codes_kernel(coarse_links, fine_links, parents, codes):
    me = lax.axis_index("dev")
    lane = iota((1, 32), 1)
    place = [iota((8, 128), 0), iota((8, 128), 1)]
    owner, octant = parents[0], parents[1]

    def own(line):
        return jnp.sum(jnp.where(lane == me, line, 0), axis=1, keepdims=True)

    values = {}
    for face in range(6):
        values[FINE_LINKS[0] + face, FINE_LINKS[1]] = own(fine_links[face])
        values[COARSE_LINKS[0] + face, COARSE_LINKS[1]] = own(coarse_links[face])
    values[PARENT] = own(owner)
    for o in range(8):
        child = jnp.where((owner == me) & (octant == o), lane, -1)
        values[CHILDREN[0] + o, CHILDREN[1]] = jnp.max(child, axis=1, keepdims=True)
    tile_of = jnp.zeros((8, 128), jnp.int32)
    for (row, at), value in values.items():
        tile_of = jnp.where((place[0] == row) & (place[1] == at), value, tile_of)
    codes[...] = tile_of
    row, at = OCTANTS
    codes[row : row + 1, at : at + 32] = octant


class Codes:
    def __init__(self, ref):
        self.tile = ref[...]
        self.seen = {}

    def __call__(self, start, step=0):
        row, at = (start[0], start[1] + step) if start == OCTANTS else (start[0] + step, start[1])
        if (row, at) not in self.seen:
            self.seen[row, at] = self.tile[row, at]
        return self.seen[row, at]


def merge_ghosts(take):
    ghosts = [{}, {}, {}]
    for face in range(6):
        ghosts[face // 2].update(take(face))
    return ghosts


def fine_ghosts(codes, plane_of, lanes, under):
    def take(face):
        code = codes(FINE_LINKS, face)
        first, second = plane_of(jnp.maximum(code, 0))
        plane = unpack_face(first, second, lanes, face)
        return {q: jnp.where(code >= 0, plane[q], under[face // 2][q]) for q in plane}

    return merge_ghosts(take)


def middle_kernel(
    received, from_low, from_high, c_post, c_start, c_weights, f_post, f_start, f_weights,
    old, table, out, coarse_new, state, post, octs,
):
    me = lax.axis_index("dev")
    codes = Codes(table)

    def coarse_ghost(face):
        code = codes(COARSE_LINKS, face)
        slot = jnp.maximum(code, 0)
        first = rows_of_pairs(received, slot, 0)
        second = rows_of_pairs(received, slot, 8)
        if face in (2, 3):
            beside = from_low if face == 2 else from_high
            first = jnp.where(code == -2, beside[0, 0:8, :], first)
            second = jnp.where(code == -2, beside[0, 8:16, :], second)
        plane = unpack_face(first, second, 0, face)
        return {q: jnp.where(code == -1, inflow_value(q), plane[q]) for q in plane}

    new = stream(
        lambda q: c_post[q], lambda q: c_start[q], lambda q: c_weights[q], merge_ghosts(coarse_ghost)
    )
    for q in range(19):
        coarse_new[q] = new[q]
    density, u = moments(new)
    mid = [0.5 * (old[i] + value) for i, value in enumerate([density] + u)]
    for o, pair in pack_octants(mid).items():
        shared, rows = pack_thin_shell(pair)
        octs[o, 0] = shared[0:4]
        octs[o, 1] = shared[4:8]
        octs[o, 2] = rows
    parent = codes(PARENT)
    rows = join_rows(received[parent, 12], received[parent, 13])
    shell = unpack_shell(rows_of_pairs(received, parent, 8), rows, received[parent, 14])
    under = below(tile_lines(shell))
    ghosts = fine_ghosts(
        codes,
        lambda d: (rows_of_pairs(received, d, 4), rows_of_pairs(received, d, 8)),
        32,
        under,
    )
    new = stream(lambda q: f_post[q], lambda q: f_start[q], lambda q: f_weights[q], ghosts)
    for q in range(19):
        state[q] = new[q]
    after = collide(new, OMEGA_FINE)
    for q in range(19):
        post[q] = after[q]
    for face in range(6):
        first, second = pack_face(after, face)
        code = codes(FINE_LINKS, face)
        slot = jnp.where(code >= 0, code, me)
        for part in range(2):
            out[slot, part] = first[4 * part : 4 * part + 4]
            out[slot, 2 + part, :, 0:32] = second[4 * part : 4 * part + 4, 0:32]
    for d in range(32):
        o = codes(OCTANTS, d)
        out[d, 2, :, 32:128] = octs[o, 0, :, 32:128]
        out[d, 3, :, 32:128] = octs[o, 1, :, 32:128]
        out[d, 4] = octs[o, 2]


def last_kernel(received, f_post, f_start, f_weights, table, out, state):
    codes = Codes(table)
    def rows_of(d, part):
        return join_rows(received[d, part], received[d, part + 1])

    parent = codes(PARENT)
    under = below(tile_lines(unpack_thin_shell(rows_of(parent, 2), received[parent, 4])))
    ghosts = fine_ghosts(codes, lambda d: (rows_of(d, 0), rows_of(d, 2)), 0, under)
    new = stream(lambda q: f_post[q], lambda q: f_start[q], lambda q: f_weights[q], ghosts)
    for q in range(19):
        store_cells(state, q, new[q])
    first, second = restrict(new)
    out[parent, 0:8, :] = first
    out[parent, 8:16, :] = second


def cover(codes):
    low = (iota((8, 128), 1) & 15) < 8
    tiles = [[None, None], [None, None]]
    for ox in range(2):
        for oy in range(2):
            o = 4 * ox + 2 * oy
            tiles[ox][oy] = jnp.where(low, codes(CHILDREN, o), codes(CHILDREN, o + 1))
    return join(tiles) >= 0


def final_kernel(received, state, coarse_new, table, fine_out, coarse_out, cells, sems):
    fine_copy = pltpu.make_async_copy(state, fine_out, sems.at[0])
    fine_copy.start()
    codes = Codes(table)
    low = (iota((8, 128), 1) & 15) < 8
    tiles = [[[None, None], [None, None]] for _ in range(4)]
    for ox in range(2):
        for oy in range(2):
            o = 4 * ox + 2 * oy
            near = jnp.maximum(codes(CHILDREN, o), 0)
            far = jnp.maximum(codes(CHILDREN, o + 1), 0)
            for k in range(2):
                a = received[near, 8 * k : 8 * k + 8, :]
                b = received[far, 8 * k : 8 * k + 8, :]
                tiles[2 * k][ox][oy] = jnp.where(low, a, pltpu.roll(b, 8, 1))
                tiles[2 * k + 1][ox][oy] = jnp.where(low, pltpu.roll(a, 120, 1), b)
    density, jx, jy, jz = [join(t) for t in tiles]
    covered = cover(codes)
    density = jnp.where(covered, density, 1.0)
    inverse = 1.0 / density
    fine_eq = equilibrium(density, [jx * inverse, jy * inverse, jz * inverse], range(19))
    new = load(coarse_new)
    own_density, own_u = moments(new)
    own_eq = equilibrium(own_density, own_u, range(19))
    for q in range(19):
        store_cells(cells, q, new[q] + jnp.where(covered, fine_eq[q] - own_eq[q], 0.0))
    coarse_copy = pltpu.make_async_copy(cells, coarse_out, sems.at[1])
    coarse_copy.start()
    fine_copy.wait()
    coarse_copy.wait()


VMEM = pl.BlockSpec(memory_space=pltpu.VMEM)
HBM = pl.BlockSpec(memory_space=pltpu.HBM)
SOME_VMEM = 24 * 1024 * 1024
MOST_VMEM = 60 * 1024 * 1024


OCTS = pltpu.VMEM((8, 7, 2, 128), F32)
LINKS = pltpu.SMEM((6, 1, 32), jnp.int32)
SEND_SCRATCH = [
    pltpu.VMEM(CELL_ROWS, F32),
    pltpu.VMEM(CELL_ROWS, F32),
    LINKS,
    LINKS,
    pltpu.SMEM((2, 1, 32), jnp.int32),
    pltpu.VMEM(SLOT1, F32),
    pltpu.VMEM((2, 16, 128), F32),
    OCTS,
    pltpu.SemaphoreType.DMA((10,)),
]
FINAL_SCRATCH = [pltpu.VMEM(CELL_ROWS, F32), pltpu.SemaphoreType.DMA((2,))]


def call(kernel, outs, ins, hbm=(), hbm_outs=(), scratch=(), vmem=SOME_VMEM, name=None):
    return pl.pallas_call(
        kernel,
        out_shape=[jax.ShapeDtypeStruct(s, F32) for s in outs],
        in_specs=[HBM if i in hbm else VMEM for i in range(len(ins))],
        out_specs=[HBM if i in hbm_outs else VMEM for i in range(len(outs))],
        scratch_shapes=list(scratch),
        compiler_params=pltpu.CompilerParams(vmem_limit_bytes=vmem),
        cost_estimate=pl.CostEstimate(
            flops=2_000_000, bytes_accessed=2_000_000, transcendentals=0
        ),
        name=name,
    )(*ins)


def swap(value):
    return lax.all_to_all(value, "dev", split_axis=0, concat_axis=0, tiled=True)


def body(fine_state, coarse_state, fine_depth, coarse_depth, fine_links, coarse_links, parents):
    count = lax.axis_size("group")
    fine_state, coarse_state = fine_state.reshape(CELL_ROWS), coarse_state.reshape(CELL_ROWS)
    fine_depth, coarse_depth = fine_depth.reshape(32, 128), coarse_depth.reshape(32, 128)
    fine_links = fine_links.transpose(2, 0, 1)
    coarse_links = coarse_links.transpose(2, 0, 1)
    parents = parents.transpose(2, 0, 1)
    sent, region = call(
        send_kernel,
        [SLOT1, (2, 16, 128)],
        [coarse_state, fine_state, coarse_links, fine_links, parents],
        hbm=(0, 1, 2, 3, 4),
        hbm_outs=(0, 1),
        scratch=SEND_SCRATCH,
        vmem=MOST_VMEM,
        name="send",
    )
    up = [(i, i + 1) for i in range(count - 1)]
    down = [(b, a) for a, b in up]
    received = swap(sent)
    from_low = lax.ppermute(region[1:2], "group", up)
    from_high = lax.ppermute(region[0:1], "group", down)

    def prepare(state, depth, omega, name, more=()):
        def kernel(*refs):
            prepare_kernel(*refs, omega=omega)

        return call(kernel, [FIELD, FIELD, FIELD, *more], [state, depth], name=name)

    c_post, c_start, c_weights, old = prepare(
        coarse_state, coarse_depth, OMEGA_COARSE, "prepare_coarse", [(4, 16, 256)]
    )
    f_post, f_start, f_weights = prepare(fine_state, fine_depth, OMEGA_FINE, "prepare_fine")
    codes = pl.pallas_call(
        codes_kernel,
        out_shape=jax.ShapeDtypeStruct((8, 128), jnp.int32),
        in_specs=[VMEM] * 3,
        out_specs=VMEM,
        compiler_params=pltpu.CompilerParams(vmem_limit_bytes=SOME_VMEM),
        name="codes",
    )(coarse_links, fine_links, parents)
    sent, coarse_new, state, post = call(
        middle_kernel,
        [SLOT2, FIELD, FIELD, FIELD],
        [
            received, from_low, from_high, c_post, c_start, c_weights, f_post, f_start, f_weights,
            old, codes,
        ],
        scratch=[pltpu.VMEM((8, 3, 4, 128), F32)],
        name="middle",
    )
    received = swap(sent)
    sent, state = call(
        last_kernel,
        [(32, SLOT3, 128), CELL_ROWS],
        [received, post, state, f_weights, codes],
        name="last",
    )
    received = swap(sent)
    fine_out, coarse_out = call(
        final_kernel,
        [CELL_ROWS, CELL_ROWS],
        [received, state, coarse_new, codes],
        hbm_outs=(0, 1),
        scratch=FINAL_SCRATCH,
        name="final",
    )
    return fine_out.reshape(1, 19, 4096), coarse_out.reshape(1, 19, 4096)


def solution(mesh):
    placed = (
        P(("group", "dev"), None, None),
        P(("group", "dev"), None, None),
        P(("group", "dev"), None),
        P(("group", "dev"), None),
        P("group", None, None),
        P("group", None, None),
        P("group", None, None),
    )
    return jax.shard_map(
        body,
        mesh=mesh,
        in_specs=placed,
        out_specs=(P(("group", "dev"), None, None), P(("group", "dev"), None, None)),
        check_vma=False,
    )
```

```python
import jax
import jax.numpy as jnp
from jax import lax
from jax.experimental import pallas as pl
from jax.experimental.pallas import tpu as pltpu
from jax.sharding import PartitionSpec as P

VELOCITIES = [
    (0, 0, 0),
    (1, 0, 0),
    (-1, 0, 0),
    (0, 1, 0),
    (0, -1, 0),
    (0, 0, 1),
    (0, 0, -1),
    (1, 1, 0),
    (-1, -1, 0),
    (1, -1, 0),
    (-1, 1, 0),
    (1, 0, 1),
    (-1, 0, -1),
    (1, 0, -1),
    (-1, 0, 1),
    (0, 1, 1),
    (0, -1, -1),
    (0, 1, -1),
    (0, -1, 1),
]
WEIGHTS = [1.0 / 3.0] + [1.0 / 18.0] * 6 + [1.0 / 36.0] * 12
OPPOSITE = [VELOCITIES.index((-v[0], -v[1], -v[2])) for v in VELOCITIES]
OUTGOING = [
    [q for q in range(19) if VELOCITIES[q][face // 2] == 2 * (face % 2) - 1] for face in range(6)
]
OMEGA_FINE = 1.25
OMEGA_COARSE = 1.0 / 0.65
INFLOW = 0.05
F32 = jnp.float32
FIELD = (19, 16, 256)
CELL_ROWS = (19, 32, 128)
SLOT1 = (32, 15, 2, 128)
SLOT2 = (32, 5, 4, 128)
SLOT3 = 16
FINE_LINKS, COARSE_LINKS, PARENT, CHILDREN, OCTANTS = (0, 0), (0, 1), (6, 0), (0, 2), (7, 32)


def inflow_value(q):
    along = VELOCITIES[q][0] * INFLOW
    return WEIGHTS[q] * (1.0 + 3.0 * along + 4.5 * along * along - 1.5 * INFLOW * INFLOW)


def iota(shape, dim):
    return lax.broadcasted_iota(jnp.int32, shape, dim)


def tile(value, row, half):
    return value[8 * row : 8 * row + 8, 128 * half : 128 * half + 128]


def join(tiles):
    return jnp.concatenate([jnp.concatenate(line, axis=1) for line in tiles], axis=0)


def pick(value, index, axis):
    return jnp.take_along_axis(value, index, axis=axis, mode="promise_in_bounds")


def sums(f):
    density = f[0]
    for q in range(1, 19):
        density = density + f[q]
    momentum = []
    for axis in range(3):
        plus = [f[q] for q in range(19) if VELOCITIES[q][axis] == 1]
        minus = [f[q] for q in range(19) if VELOCITIES[q][axis] == -1]
        total = plus[0] - minus[0]
        for a, b in zip(plus[1:], minus[1:]):
            total = total + (a - b)
        momentum.append(total)
    return density, momentum


def moments(f):
    density, momentum = sums(f)
    inverse = 1.0 / density
    return density, [m * inverse for m in momentum]


def equilibrium(density, u, chosen):
    base = 1.0 - 1.5 * (u[0] * u[0] + u[1] * u[1] + u[2] * u[2])
    scaled = {}
    for q in chosen:
        if WEIGHTS[q] not in scaled:
            scaled[WEIGHTS[q]] = WEIGHTS[q] * density
    even, out = {}, {}
    for q in chosen:
        v = VELOCITIES[q]
        weight = scaled[WEIGHTS[q]]
        if q == 0:
            out[q] = weight * base
            continue
        lead = q if q % 2 == 1 else q - 1
        if lead not in even:
            along = None
            for axis in range(3):
                c = VELOCITIES[lead][axis]
                if c != 0:
                    if along is None:
                        along = u[axis]
                    else:
                        along = along + u[axis] if c > 0 else along - u[axis]
            even[lead] = (base + 4.5 * along * along, 3.0 * along)
        part, odd = even[lead]
        out[q] = weight * (part + odd) if q == lead else weight * (part - odd)
    return out


def collide(f, omega):
    density, u = moments(f)
    rest = equilibrium(density, u, range(19))
    return [(1.0 - omega) * f[q] + omega * rest[q] for q in range(19)]


def row_parts(top, bottom, lane, sub):
    both = jnp.where(sub < 4, jnp.broadcast_to(top, (8, 128)), jnp.broadcast_to(bottom, (8, 128)))
    return pick(both, 32 * (sub & 3) + (lane & 31), 1)


def pack_face(post, face):
    axis, side = face // 2, face % 2
    lane = iota((8, 128), 1)
    sub = iota((8, 128), 0)
    chosen = [post[q] for q in OUTGOING[face]]
    if axis == 0:
        at = 15 * side
        rows = [[f[at : at + 1, 128 * h : 128 * h + 128] for h in range(2)] for f in chosen]
        first = None
        for i in range(4):
            for half in range(2):
                line = jnp.broadcast_to(rows[i][half], (8, 128))
                first = line if first is None else jnp.where(sub == 2 * i + half, line, first)
        return first, row_parts(rows[4][0], rows[4][1], lane, sub)
    strips = []
    for f in chosen:
        for row in range(2):
            if axis == 1:
                strips.append(pick(tile(f, row, side), (lane & 15) + 112 * side, 1))
            else:
                index = (lane & 7) * 16 + 15 * side
                a = pick(tile(f, row, 0), index, 1)
                b = pick(tile(f, row, 1), index, 1)
                strips.append(jnp.where((lane & 15) < 8, a, b))
    first = strips[0]
    for t in range(1, 8):
        first = jnp.where((lane >> 4) == t, strips[t], first)
    second = jnp.where(((lane >> 4) & 1) == 0, strips[8], strips[9])
    return first, second


def unpack_face(first, second, offset, face):
    axis, side = face // 2, face % 2
    lane = iota((8, 128), 1)
    out = {}
    for i, q in enumerate(OUTGOING[face ^ 1]):
        if axis == 0:
            halves = []
            for half in range(2):
                if i < 4:
                    line = jnp.broadcast_to(first[2 * i + half : 2 * i + half + 1, :], (8, 128))
                else:
                    line = pick(pick(second, offset + (lane & 31), 1), 4 * half + (lane >> 5), 0)
                halves.append(line)
            out[q] = join([halves, halves])
            continue
        rows = []
        for row in range(2):
            source, base = (first, 16 * (2 * i + row)) if i < 4 else (second, offset + 16 * row)
            if axis == 1:
                piece = pick(source, base + (lane & 15), 1)
                rows.append([piece, piece])
            else:
                step = 1 if side == 0 else 15
                rows.append(
                    [
                        pick(source, base + ((8 * half + (lane >> 4) + step) & 15), 1)
                        for half in range(2)
                    ]
                )
        out[q] = join(rows)
    return out


def join_rows(upper, lower):
    return jnp.concatenate([upper, lower], axis=0)


def shell_places(lane):
    entry = lane - jnp.where(lane < 120, 96, 120)
    along_z = (1 + (entry >> 2)) * 16 + 8 * ((entry >> 1) & 1) + 7 * (entry & 1)
    part = lane & 31
    return jnp.where(lane < 96, part + 96 * (part >> 4), along_z)


def pack_thin_shell(pair):
    lane = iota((8, 128), 1)
    sub = iota((8, 128), 0)
    a, b = pair
    index = shell_places(lane) & 127
    first = (lane < 64) | ((lane >= 96) & (lane < 120))
    inside = jnp.where(first, pick(a, index, 1), pick(b, index, 1))
    entry = 8 + (lane & 15)
    rest = pick(b, (1 + (entry >> 2)) * 16 + 8 * ((entry >> 1) & 1) + 7 * (entry & 1), 1)
    block = ((lane >> 4) - 2) & 3
    rest = pick(rest, jnp.where(sub == 0, 1, 4) + block, 0)
    shared = jnp.where((sub == 0) | (sub == 7), rest, inside)
    rows = jnp.concatenate([a[0:1], a[7:8], b[0:1], b[7:8]], axis=0)
    return shared, rows


def unpack_thin_shell(shared, rows):
    lane = iota((8, 128), 1)
    sub = iota((8, 128), 0)
    rows = join_rows(rows, rows)
    edge = (lane & 15) + jnp.where(lane >= 112, 16, 0)
    z = lane & 15
    entry = 4 * ((lane >> 4) - 1) + 2 * (z >> 3) + jnp.where((z & 7) == 7, 1, 0)
    on_y = (lane < 16) | (lane >= 112)
    block = sub - jnp.where(sub > 3, 4, 1)
    moved = pick(pick(shared, jnp.where(sub <= 3, 0, 7), 0), (24 + 16 * block + entry) & 127, 1)
    out = []
    for k in range(2):
        start = 96 if k == 0 else 120
        tile_k = pick(shared, jnp.where(on_y, 32 + 32 * k + edge, start + entry) & 127, 1)
        if k == 1:
            tile_k = jnp.where(on_y | (entry < 8), tile_k, moved)
        line = pick(rows, 2 * k + jnp.where(sub == 7, 1, 0), 0)
        out.append(jnp.where((sub == 0) | (sub == 7), line, tile_k))
    return out


def z_place(entry):
    return ((1 + (entry >> 2)) * 16 + 8 * ((entry >> 1) & 1) + 7 * (entry & 1)) & 127


def pack_shell(pair):
    lane = iota((8, 128), 1)
    sub = iota((8, 128), 0)
    a, b = pair
    part = lane & 31
    along_y = part + 96 * (part >> 4)
    inside = jnp.where(lane < 96, pick(a, along_y, 1), pick(b, along_y, 1))
    sixth = jnp.full((8, 128), 6, jnp.int32)
    last = [pick(pick(t, z_place(part), 1), sixth, 0) for t in pair]
    shared = jnp.where(sub == 0, last[0], jnp.where(sub == 7, last[1], inside))
    rows = jnp.concatenate([a[0:1], a[7:8], b[0:1], b[7:8]], axis=0)
    block = (lane * 171) >> 12
    lines = [pick(pick(t, z_place(lane - 24 * block), 1), 1 + block, 0) for t in pair]
    return shared, rows, jnp.concatenate([lines[0][0:1], lines[1][0:1]], axis=0)


def unpack_shell(shared, rows, extra):
    lane = iota((8, 128), 1)
    sub = iota((8, 128), 0)
    rows = join_rows(rows, rows)
    extra = jnp.concatenate([extra] * 4, axis=0)
    edge = (lane & 15) + jnp.where(lane >= 112, 16, 0)
    z = lane & 15
    entry = 4 * ((lane >> 4) - 1) + 2 * (z >> 3) + jnp.where((z & 7) == 7, 1, 0)
    on_y = (lane < 16) | (lane >= 112)
    place = (jnp.where(sub == 6, 64, 24 * (sub - 1)) + entry) & 127
    out = []
    for k in range(2):
        whole = jnp.full((8, 128), k, jnp.int32)
        source = jnp.where(sub == 6, pick(shared, 7 * whole, 0), pick(extra, whole, 0))
        along_z = pick(source, place, 1)
        along_y = pick(shared, 64 + 32 * k + edge, 1)
        line = pick(rows, 2 * k + jnp.where(sub == 7, 1, 0), 0)
        tile_k = jnp.where(on_y, along_y, along_z)
        out.append(jnp.where((sub == 0) | (sub == 7), line, tile_k))
    return out


def shifted(value, v):
    if v[0] != 0:
        value = pltpu.roll(value, v[0] % 16, 0)
    lanes = (16 * v[1] + v[2]) % 256
    if lanes != 0:
        value = pltpu.roll(value, lanes, 1)
    return value


def positions():
    row = iota((16, 256), 0)
    lane = iota((16, 256), 1)
    return row, lane >> 4, lane & 15


def wall_weights(depth):
    place = positions()
    solid = depth <= 0
    here = depth.astype(F32)
    out = [jnp.where(solid, 1.0, 0.0).astype(F32)]
    for q in range(1, 19):
        v = VELOCITIES[q]
        outside = []
        for axis in range(3):
            if v[axis] != 0:
                outside.append(place[axis] == (0 if v[axis] > 0 else 15))
        away = outside[0] if len(outside) == 1 else outside[0] | outside[1]
        there = shifted(here, v)
        wall = (there <= 0.0) & jnp.logical_not(away) & jnp.logical_not(solid)
        gap = jnp.where(wall, here - there, 1.0)
        own = jnp.where(wall, here, 1.0)
        far = own + own >= gap
        weight = jnp.where(far, 0.5 * gap, 2.0 * own) / jnp.where(far, own, gap)
        value = jnp.where(wall, weight, -1.0)
        if len(outside) == 2:
            value = jnp.where(outside[0] & outside[1], 1.0, value)
        out.append(value)
    return out


def stream(post, start, weights, ghosts):
    place = positions()
    solid = weights(0) > 0.5
    out = [jnp.where(solid, start(0), post(0))]
    for q in range(1, 19):
        v = VELOCITIES[q]
        own = post(q)
        value = own
        for axis in (1, 0, 2):
            if v[axis] != 0:
                edge = place[axis] == (15 if v[axis] > 0 else 0)
                value = jnp.where(edge, ghosts[axis][q], value)
        value = shifted(value, v)
        weight = weights(q)
        value = jnp.where(weight >= 0.0, own + weight * (post(OPPOSITE[q]) - own), value)
        out.append(jnp.where(solid, start(q), value))
    return out


def pack_octants(fields):
    low = (iota((8, 128), 1) & 15) < 8
    out = {}
    for ox in range(2):
        for oy in range(2):
            a, b, c, d = [tile(f, ox, oy) for f in fields]
            out[4 * ox + 2 * oy] = (
                jnp.where(low, a, pltpu.roll(b, 8, 1)),
                jnp.where(low, c, pltpu.roll(d, 8, 1)),
            )
            out[4 * ox + 2 * oy + 1] = (
                jnp.where(low, pltpu.roll(a, 120, 1), b),
                jnp.where(low, pltpu.roll(c, 120, 1), d),
            )
    return out


def tile_lines(tiles):
    lane = iota((8, 128), 1)

    def at_x(k, half, inner):
        return pick(tiles[k // 2], (4 * half + (lane >> 5)) * 16 + inner, 1)

    def row_of(k, half, side):
        return jnp.full((8, 128), 7 * side, jnp.int32)

    def at_y(k, side, inner):
        return pick(tiles[k // 2], 112 * side + inner, 1)

    def at_z(k, y, side):
        return pick(tiles[k // 2], 16 * y + 8 * (k % 2) + 7 * side, 1)

    return at_x, row_of, at_y, at_z


def below(lines):
    at_x, row_of, at_y, at_z = lines
    lane = iota((8, 128), 1)
    sub = iota((8, 128), 0)
    z = lane & 15
    fields = [[], [], []]
    for k in range(4):
        inner = (z >> 1) + 8 * (k % 2)
        tiles = [[None, None], [None, None]]
        for half in range(2):
            rows = at_x(k, half, inner)
            for row in range(2):
                tiles[row][half] = pick(rows, row_of(k, half, 1 - row), 0)
        fields[0].append(join(tiles))
        for half in range(2):
            line = at_y(k, 1 - half, inner)
            for row in range(2):
                tiles[row][half] = pick(line, 4 * row + (sub >> 1), 0)
        fields[1].append(join(tiles))
        for half in range(2):
            y = 8 * half + (lane >> 4)
            far = z == 15
            line = at_z(k, ((y + jnp.where(far, 1, 15)) & 15) >> 1, jnp.where(far, 0, 1))
            for row in range(2):
                tiles[row][half] = pick(line, 4 * row + (sub >> 1), 0)
        fields[2].append(join(tiles))
    out = []
    for axis in range(3):
        chosen = [q for q in range(19) if VELOCITIES[q][axis] != 0]
        out.append(equilibrium(fields[axis][0], fields[axis][1:], chosen))
    return out


def restrict(f):
    lane = iota((8, 128), 1)
    sub = iota((8, 128), 0)
    density, momentum = sums(f)
    index = ((lane >> 4) & 3) * 32 + (lane & 7) * 2
    even = (2 * sub) & 7
    packed = []
    for field in [density] + momentum:
        halves = []
        for half in range(2):
            lines = [
                jnp.where(
                    sub < 4,
                    pick(tile(field, 0, half), even + odd, 0),
                    pick(tile(field, 1, half), even + odd, 0),
                )
                for odd in range(2)
            ]
            line = lines[0] + lines[1]
            parts = [pick(line, index + step, 1) for step in (0, 1, 16, 17)]
            halves.append(0.125 * ((parts[0] + parts[1]) + (parts[2] + parts[3])))
        packed.append(jnp.where(lane < 64, halves[0], halves[1]))
    low = (lane & 15) < 8
    return jnp.where(low, packed[0], packed[1]), jnp.where(low, packed[2], packed[3])


def load(ref):
    return [ref[q] for q in range(19)]


def load_cells(ref, q):
    halves = [ref[q, pl.ds(half, 16, stride=2), :] for half in range(2)]
    return jnp.concatenate(halves, axis=1)


def store_cells(ref, q, value):
    for half in range(2):
        ref[q, pl.ds(half, 16, stride=2), :] = value[:, 128 * half : 128 * half + 128]


def store_octants(fields, octs):
    for o, pair in pack_octants(fields).items():
        shared, rows, extra = pack_shell(pair)
        for part in range(4):
            octs[o, part] = shared[2 * part : 2 * part + 2]
        for part in range(2):
            octs[o, 4 + part] = rows[2 * part : 2 * part + 2]
        octs[o, 6] = extra


def give_octants(octs, parents, out):
    for d in range(32):
        o = parents[1, 0, d]
        out[d, 8:12, :, 64:128] = octs[o, 0:4, :, 64:128]
        out[d, 12:15] = octs[o, 4:7]


def give_face(post, face, code, me, out, at, lanes):
    first, second = pack_face(post, face)
    slot = jnp.where(code >= 0, code, me)
    for part in range(4):
        rows = slice(2 * part, 2 * part + 2)
        out[slot, at + part] = first[rows]
        out[slot, 8 + part, :, lanes : lanes + 32] = second[rows, lanes : lanes + 32]
    return first, second


def rows_of_pairs(ref, slot, at):
    return jnp.concatenate([ref[slot, at + part] for part in range(4)], axis=0)


def send_kernel(
    coarse_in, fine_in, coarse_table, fine_table, parent_table, out, region_out,
    coarse, fine, coarse_links, fine_links, parents, slots, region, octs, sems,
):
    fetch = [
        pltpu.make_async_copy(source, target, sems.at[i])
        for i, (source, target) in enumerate(
            (
                (coarse_in, coarse),
                (coarse_table, coarse_links),
                (fine_in, fine),
                (fine_table, fine_links),
                (parent_table, parents),
            )
        )
    ]
    for copy in fetch:
        copy.start()

    def put(part):
        rows = (pl.ds(0, 4), pl.ds(4, 8), pl.ds(12, 3))[part]
        return pltpu.make_async_copy(slots.at[:, rows], out.at[:, rows], sems.at[5 + part])

    me = lax.axis_index("dev")
    fetch[0].wait()
    fetch[1].wait()
    f = [load_cells(coarse, q) for q in range(19)]
    density, u = moments(f)
    store_octants([density] + u, octs)
    post = collide(f, OMEGA_COARSE)
    for face in range(6):
        first, second = give_face(post, face, coarse_links[face, 0, me], me, slots, 0, 0)
        if face in (2, 3):
            region[face - 2, 0:8, :] = first
            region[face - 2, 8:16, :] = second
    put(0).start()
    beside = pltpu.make_async_copy(region, region_out, sems.at[8])
    beside.start()
    fetch[4].wait()
    give_octants(octs, parents, slots)
    put(2).start()
    fetch[2].wait()
    fetch[3].wait()
    post = collide([load_cells(fine, q) for q in range(19)], OMEGA_FINE)
    for face in range(6):
        give_face(post, face, fine_links[face, 0, me], me, slots, 4, 32)
    put(1).start()
    for part in range(3):
        put(part).wait()
    beside.wait()


def prepare_kernel(state, depth, post, start, weights, *old, omega):
    f = [load_cells(state, q) for q in range(19)]
    for q in range(19):
        start[q] = f[q]
    for q, value in enumerate(collide(f, omega)):
        post[q] = value
    if old:
        density, u = moments(f)
        for i, value in enumerate([density] + u):
            old[0][i] = value
    halves = [depth[pl.ds(half, 16, stride=2), :] for half in range(2)]
    for q, value in enumerate(wall_weights(jnp.concatenate(halves, axis=1))):
        weights[q] = value


def codes_kernel(coarse_links, fine_links, parents, codes):
    me = lax.axis_index("dev")
    lane = iota((1, 32), 1)
    place = [iota((8, 128), 0), iota((8, 128), 1)]
    owner, octant = parents[0], parents[1]

    def own(line):
        return jnp.sum(jnp.where(lane == me, line, 0), axis=1, keepdims=True)

    values = {}
    for face in range(6):
        values[FINE_LINKS[0] + face, FINE_LINKS[1]] = own(fine_links[face])
        values[COARSE_LINKS[0] + face, COARSE_LINKS[1]] = own(coarse_links[face])
    values[PARENT] = own(owner)
    for o in range(8):
        child = jnp.where((owner == me) & (octant == o), lane, -1)
        values[CHILDREN[0] + o, CHILDREN[1]] = jnp.max(child, axis=1, keepdims=True)
    tile_of = jnp.zeros((8, 128), jnp.int32)
    for (row, at), value in values.items():
        tile_of = jnp.where((place[0] == row) & (place[1] == at), value, tile_of)
    codes[...] = tile_of
    row, at = OCTANTS
    codes[row : row + 1, at : at + 32] = octant


class Codes:
    def __init__(self, ref):
        self.tile = ref[...]
        self.seen = {}

    def __call__(self, start, step=0):
        row, at = (start[0], start[1] + step) if start == OCTANTS else (start[0] + step, start[1])
        if (row, at) not in self.seen:
            self.seen[row, at] = self.tile[row, at]
        return self.seen[row, at]


def merge_ghosts(take):
    ghosts = [{}, {}, {}]
    for face in range(6):
        ghosts[face // 2].update(take(face))
    return ghosts


def fine_ghosts(codes, plane_of, lanes, under):
    def take(face):
        code = codes(FINE_LINKS, face)
        first, second = plane_of(jnp.maximum(code, 0))
        plane = unpack_face(first, second, lanes, face)
        return {q: jnp.where(code >= 0, plane[q], under[face // 2][q]) for q in plane}

    return merge_ghosts(take)


def middle_kernel(
    received, from_low, from_high, c_post, c_start, c_weights, f_post, f_start, f_weights,
    old, table, out, coarse_new, state, post, octs,
):
    me = lax.axis_index("dev")
    codes = Codes(table)

    def coarse_ghost(face):
        code = codes(COARSE_LINKS, face)
        slot = jnp.maximum(code, 0)
        first = rows_of_pairs(received, slot, 0)
        second = rows_of_pairs(received, slot, 8)
        if face in (2, 3):
            beside = from_low if face == 2 else from_high
            first = jnp.where(code == -2, beside[0, 0:8, :], first)
            second = jnp.where(code == -2, beside[0, 8:16, :], second)
        plane = unpack_face(first, second, 0, face)
        return {q: jnp.where(code == -1, inflow_value(q), plane[q]) for q in plane}

    new = stream(
        lambda q: c_post[q], lambda q: c_start[q], lambda q: c_weights[q], merge_ghosts(coarse_ghost)
    )
    for q in range(19):
        coarse_new[q] = new[q]
    density, u = moments(new)
    mid = [0.5 * (old[i] + value) for i, value in enumerate([density] + u)]
    for o, pair in pack_octants(mid).items():
        shared, rows = pack_thin_shell(pair)
        octs[o, 0] = shared[0:4]
        octs[o, 1] = shared[4:8]
        octs[o, 2] = rows
    parent = codes(PARENT)
    rows = join_rows(received[parent, 12], received[parent, 13])
    shell = unpack_shell(rows_of_pairs(received, parent, 8), rows, received[parent, 14])
    under = below(tile_lines(shell))
    ghosts = fine_ghosts(
        codes,
        lambda d: (rows_of_pairs(received, d, 4), rows_of_pairs(received, d, 8)),
        32,
        under,
    )
    new = stream(lambda q: f_post[q], lambda q: f_start[q], lambda q: f_weights[q], ghosts)
    for q in range(19):
        state[q] = new[q]
    after = collide(new, OMEGA_FINE)
    for q in range(19):
        post[q] = after[q]
    for face in range(6):
        first, second = pack_face(after, face)
        code = codes(FINE_LINKS, face)
        slot = jnp.where(code >= 0, code, me)
        for part in range(2):
            out[slot, part] = first[4 * part : 4 * part + 4]
            out[slot, 2 + part, :, 0:32] = second[4 * part : 4 * part + 4, 0:32]
    for d in range(32):
        o = codes(OCTANTS, d)
        out[d, 2, :, 32:128] = octs[o, 0, :, 32:128]
        out[d, 3, :, 32:128] = octs[o, 1, :, 32:128]
        out[d, 4] = octs[o, 2]


def last_kernel(received, f_post, f_start, f_weights, table, out, state):
    codes = Codes(table)
    def rows_of(d, part):
        return join_rows(received[d, part], received[d, part + 1])

    parent = codes(PARENT)
    under = below(tile_lines(unpack_thin_shell(rows_of(parent, 2), received[parent, 4])))
    ghosts = fine_ghosts(codes, lambda d: (rows_of(d, 0), rows_of(d, 2)), 0, under)
    new = stream(lambda q: f_post[q], lambda q: f_start[q], lambda q: f_weights[q], ghosts)
    for q in range(19):
        store_cells(state, q, new[q])
    first, second = restrict(new)
    out[parent, 0:8, :] = first
    out[parent, 8:16, :] = second


def cover(codes):
    low = (iota((8, 128), 1) & 15) < 8
    tiles = [[None, None], [None, None]]
    for ox in range(2):
        for oy in range(2):
            o = 4 * ox + 2 * oy
            tiles[ox][oy] = jnp.where(low, codes(CHILDREN, o), codes(CHILDREN, o + 1))
    return join(tiles) >= 0


def final_kernel(received, state, coarse_new, table, fine_out, coarse_out, cells, sems):
    fine_copy = pltpu.make_async_copy(state, fine_out, sems.at[0])
    fine_copy.start()
    codes = Codes(table)
    low = (iota((8, 128), 1) & 15) < 8
    tiles = [[[None, None], [None, None]] for _ in range(4)]
    for ox in range(2):
        for oy in range(2):
            o = 4 * ox + 2 * oy
            near = jnp.maximum(codes(CHILDREN, o), 0)
            far = jnp.maximum(codes(CHILDREN, o + 1), 0)
            for k in range(2):
                a = received[near, 8 * k : 8 * k + 8, :]
                b = received[far, 8 * k : 8 * k + 8, :]
                tiles[2 * k][ox][oy] = jnp.where(low, a, pltpu.roll(b, 8, 1))
                tiles[2 * k + 1][ox][oy] = jnp.where(low, pltpu.roll(a, 120, 1), b)
    density, jx, jy, jz = [join(t) for t in tiles]
    covered = cover(codes)
    density = jnp.where(covered, density, 1.0)
    inverse = 1.0 / density
    fine_eq = equilibrium(density, [jx * inverse, jy * inverse, jz * inverse], range(19))
    new = load(coarse_new)
    own_density, own_u = moments(new)
    own_eq = equilibrium(own_density, own_u, range(19))
    for q in range(19):
        store_cells(cells, q, new[q] + jnp.where(covered, fine_eq[q] - own_eq[q], 0.0))
    coarse_copy = pltpu.make_async_copy(cells, coarse_out, sems.at[1])
    coarse_copy.start()
    fine_copy.wait()
    coarse_copy.wait()


VMEM = pl.BlockSpec(memory_space=pltpu.VMEM)
HBM = pl.BlockSpec(memory_space=pltpu.HBM)
SOME_VMEM = 24 * 1024 * 1024
MOST_VMEM = 60 * 1024 * 1024


OCTS = pltpu.VMEM((8, 7, 2, 128), F32)
LINKS = pltpu.SMEM((6, 1, 32), jnp.int32)
SEND_SCRATCH = [
    pltpu.VMEM(CELL_ROWS, F32),
    pltpu.VMEM(CELL_ROWS, F32),
    LINKS,
    LINKS,
    pltpu.SMEM((2, 1, 32), jnp.int32),
    pltpu.VMEM(SLOT1, F32),
    pltpu.VMEM((2, 16, 128), F32),
    OCTS,
    pltpu.SemaphoreType.DMA((9,)),
]
FINAL_SCRATCH = [pltpu.VMEM(CELL_ROWS, F32), pltpu.SemaphoreType.DMA((2,))]


def call(kernel, outs, ins, hbm=(), hbm_outs=(), scratch=(), vmem=SOME_VMEM, name=None):
    return pl.pallas_call(
        kernel,
        out_shape=[jax.ShapeDtypeStruct(s, F32) for s in outs],
        in_specs=[HBM if i in hbm else VMEM for i in range(len(ins))],
        out_specs=[HBM if i in hbm_outs else VMEM for i in range(len(outs))],
        scratch_shapes=list(scratch),
        compiler_params=pltpu.CompilerParams(vmem_limit_bytes=vmem),
        cost_estimate=pl.CostEstimate(
            flops=2_000_000, bytes_accessed=2_000_000, transcendentals=0
        ),
        name=name,
    )(*ins)


def swap(value):
    return lax.all_to_all(value, "dev", split_axis=0, concat_axis=0, tiled=True)


def body(fine_state, coarse_state, fine_depth, coarse_depth, fine_links, coarse_links, parents):
    count = lax.axis_size("group")
    fine_state, coarse_state = fine_state.reshape(CELL_ROWS), coarse_state.reshape(CELL_ROWS)
    fine_depth, coarse_depth = fine_depth.reshape(32, 128), coarse_depth.reshape(32, 128)
    fine_links = fine_links.transpose(2, 0, 1)
    coarse_links = coarse_links.transpose(2, 0, 1)
    parents = parents.transpose(2, 0, 1)
    sent, region = call(
        send_kernel,
        [SLOT1, (2, 16, 128)],
        [coarse_state, fine_state, coarse_links, fine_links, parents],
        hbm=(0, 1, 2, 3, 4),
        hbm_outs=(0, 1),
        scratch=SEND_SCRATCH,
        vmem=MOST_VMEM,
        name="send",
    )
    up = [(i, i + 1) for i in range(count - 1)]
    down = [(b, a) for a, b in up]
    received = swap(sent)
    from_low = lax.ppermute(region[1:2], "group", up)
    from_high = lax.ppermute(region[0:1], "group", down)

    def prepare(state, depth, omega, name, more=()):
        def kernel(*refs):
            prepare_kernel(*refs, omega=omega)

        return call(kernel, [FIELD, FIELD, FIELD, *more], [state, depth], name=name)

    c_post, c_start, c_weights, old = prepare(
        coarse_state, coarse_depth, OMEGA_COARSE, "prepare_coarse", [(4, 16, 256)]
    )
    f_post, f_start, f_weights = prepare(fine_state, fine_depth, OMEGA_FINE, "prepare_fine")
    codes = pl.pallas_call(
        codes_kernel,
        out_shape=jax.ShapeDtypeStruct((8, 128), jnp.int32),
        in_specs=[VMEM] * 3,
        out_specs=VMEM,
        compiler_params=pltpu.CompilerParams(vmem_limit_bytes=SOME_VMEM),
        name="codes",
    )(coarse_links, fine_links, parents)
    sent, coarse_new, state, post = call(
        middle_kernel,
        [SLOT2, FIELD, FIELD, FIELD],
        [
            received, from_low, from_high, c_post, c_start, c_weights, f_post, f_start, f_weights,
            old, codes,
        ],
        scratch=[pltpu.VMEM((8, 3, 4, 128), F32)],
        name="middle",
    )
    received = swap(sent)
    sent, state = call(
        last_kernel,
        [(32, SLOT3, 128), CELL_ROWS],
        [received, post, state, f_weights, codes],
        name="last",
    )
    received = swap(sent)
    fine_out, coarse_out = call(
        final_kernel,
        [CELL_ROWS, CELL_ROWS],
        [received, state, coarse_new, codes],
        hbm_outs=(0, 1),
        scratch=FINAL_SCRATCH,
        name="final",
    )
    return fine_out.reshape(1, 19, 4096), coarse_out.reshape(1, 19, 4096)


def solution(mesh):
    placed = (
        P(("group", "dev"), None, None),
        P(("group", "dev"), None, None),
        P(("group", "dev"), None),
        P(("group", "dev"), None),
        P("group", None, None),
        P("group", None, None),
        P("group", None, None),
    )
    return jax.shard_map(
        body,
        mesh=mesh,
        in_specs=placed,
        out_specs=(P(("group", "dev"), None, None), P(("group", "dev"), None, None)),
        check_vma=False,
    )
```

```python
import jax
import jax.numpy as jnp
from jax import lax
from jax.experimental import pallas as pl
from jax.experimental.pallas import tpu as pltpu
from jax.sharding import PartitionSpec as P

VELOCITIES = [
    (0, 0, 0),
    (1, 0, 0),
    (-1, 0, 0),
    (0, 1, 0),
    (0, -1, 0),
    (0, 0, 1),
    (0, 0, -1),
    (1, 1, 0),
    (-1, -1, 0),
    (1, -1, 0),
    (-1, 1, 0),
    (1, 0, 1),
    (-1, 0, -1),
    (1, 0, -1),
    (-1, 0, 1),
    (0, 1, 1),
    (0, -1, -1),
    (0, 1, -1),
    (0, -1, 1),
]
WEIGHTS = [1.0 / 3.0] + [1.0 / 18.0] * 6 + [1.0 / 36.0] * 12
OPPOSITE = [VELOCITIES.index((-v[0], -v[1], -v[2])) for v in VELOCITIES]
OUTGOING = [
    [q for q in range(19) if VELOCITIES[q][face // 2] == 2 * (face % 2) - 1] for face in range(6)
]
OMEGA_FINE = 1.25
OMEGA_COARSE = 1.0 / 0.65
INFLOW = 0.05
F32 = jnp.float32
FIELD = (19, 16, 256)
CELL_ROWS = (19, 32, 128)
SLOT1 = (32, 15, 2, 128)
SLOT2 = (32, 5, 4, 128)
SLOT3 = 16
FINE_LINKS, COARSE_LINKS, PARENT, CHILDREN, OCTANTS = (0, 0), (0, 1), (6, 0), (0, 2), (7, 32)


def inflow_value(q):
    along = VELOCITIES[q][0] * INFLOW
    return WEIGHTS[q] * (1.0 + 3.0 * along + 4.5 * along * along - 1.5 * INFLOW * INFLOW)


def iota(shape, dim):
    return lax.broadcasted_iota(jnp.int32, shape, dim)


def tile(value, row, half):
    return value[8 * row : 8 * row + 8, 128 * half : 128 * half + 128]


def join(tiles):
    return jnp.concatenate([jnp.concatenate(line, axis=1) for line in tiles], axis=0)


def pick(value, index, axis):
    return jnp.take_along_axis(value, index, axis=axis, mode="promise_in_bounds")


def sums(f):
    density = f[0]
    for q in range(1, 19):
        density = density + f[q]
    momentum = []
    for axis in range(3):
        plus = [f[q] for q in range(19) if VELOCITIES[q][axis] == 1]
        minus = [f[q] for q in range(19) if VELOCITIES[q][axis] == -1]
        total = plus[0] - minus[0]
        for a, b in zip(plus[1:], minus[1:]):
            total = total + (a - b)
        momentum.append(total)
    return density, momentum


def moments(f):
    density, momentum = sums(f)
    inverse = 1.0 / density
    return density, [m * inverse for m in momentum]


def equilibrium(density, u, chosen):
    base = 1.0 - 1.5 * (u[0] * u[0] + u[1] * u[1] + u[2] * u[2])
    scaled = {}
    for q in chosen:
        if WEIGHTS[q] not in scaled:
            scaled[WEIGHTS[q]] = WEIGHTS[q] * density
    even, out = {}, {}
    for q in chosen:
        v = VELOCITIES[q]
        weight = scaled[WEIGHTS[q]]
        if q == 0:
            out[q] = weight * base
            continue
        lead = q if q % 2 == 1 else q - 1
        if lead not in even:
            along = None
            for axis in range(3):
                c = VELOCITIES[lead][axis]
                if c != 0:
                    if along is None:
                        along = u[axis]
                    else:
                        along = along + u[axis] if c > 0 else along - u[axis]
            even[lead] = (base + 4.5 * along * along, 3.0 * along)
        part, odd = even[lead]
        out[q] = weight * (part + odd) if q == lead else weight * (part - odd)
    return out


def collide(f, omega):
    density, u = moments(f)
    rest = equilibrium(density, u, range(19))
    return [(1.0 - omega) * f[q] + omega * rest[q] for q in range(19)]


def row_parts(top, bottom, lane, sub):
    both = jnp.where(sub < 4, jnp.broadcast_to(top, (8, 128)), jnp.broadcast_to(bottom, (8, 128)))
    return pick(both, 32 * (sub & 3) + (lane & 31), 1)


def pack_face(post, face):
    axis, side = face // 2, face % 2
    lane = iota((8, 128), 1)
    sub = iota((8, 128), 0)
    chosen = [post[q] for q in OUTGOING[face]]
    if axis == 0:
        at = 15 * side
        rows = [[f[at : at + 1, 128 * h : 128 * h + 128] for h in range(2)] for f in chosen]
        first = None
        for i in range(4):
            for half in range(2):
                line = jnp.broadcast_to(rows[i][half], (8, 128))
                first = line if first is None else jnp.where(sub == 2 * i + half, line, first)
        return first, row_parts(rows[4][0], rows[4][1], lane, sub)
    strips = []
    for f in chosen:
        for row in range(2):
            if axis == 1:
                strips.append(pick(tile(f, row, side), (lane & 15) + 112 * side, 1))
            else:
                index = (lane & 7) * 16 + 15 * side
                a = pick(tile(f, row, 0), index, 1)
                b = pick(tile(f, row, 1), index, 1)
                strips.append(jnp.where((lane & 15) < 8, a, b))
    first = strips[0]
    for t in range(1, 8):
        first = jnp.where((lane >> 4) == t, strips[t], first)
    second = jnp.where(((lane >> 4) & 1) == 0, strips[8], strips[9])
    return first, second


def unpack_face(first, second, offset, face):
    axis, side = face // 2, face % 2
    lane = iota((8, 128), 1)
    out = {}
    for i, q in enumerate(OUTGOING[face ^ 1]):
        if axis == 0:
            halves = []
            for half in range(2):
                if i < 4:
                    line = jnp.broadcast_to(first[2 * i + half : 2 * i + half + 1, :], (8, 128))
                else:
                    line = pick(pick(second, offset + (lane & 31), 1), 4 * half + (lane >> 5), 0)
                halves.append(line)
            out[q] = join([halves, halves])
            continue
        rows = []
        for row in range(2):
            source, base = (first, 16 * (2 * i + row)) if i < 4 else (second, offset + 16 * row)
            if axis == 1:
                piece = pick(source, base + (lane & 15), 1)
                rows.append([piece, piece])
            else:
                step = 1 if side == 0 else 15
                rows.append(
                    [
                        pick(source, base + ((8 * half + (lane >> 4) + step) & 15), 1)
                        for half in range(2)
                    ]
                )
        out[q] = join(rows)
    return out


def join_rows(upper, lower):
    return jnp.concatenate([upper, lower], axis=0)


def shell_places(lane):
    entry = lane - jnp.where(lane < 120, 96, 120)
    along_z = (1 + (entry >> 2)) * 16 + 8 * ((entry >> 1) & 1) + 7 * (entry & 1)
    part = lane & 31
    return jnp.where(lane < 96, part + 96 * (part >> 4), along_z)


def pack_thin_shell(pair):
    lane = iota((8, 128), 1)
    sub = iota((8, 128), 0)
    a, b = pair
    index = shell_places(lane) & 127
    first = (lane < 64) | ((lane >= 96) & (lane < 120))
    inside = jnp.where(first, pick(a, index, 1), pick(b, index, 1))
    entry = 8 + (lane & 15)
    rest = pick(b, (1 + (entry >> 2)) * 16 + 8 * ((entry >> 1) & 1) + 7 * (entry & 1), 1)
    block = ((lane >> 4) - 2) & 3
    rest = pick(rest, jnp.where(sub == 0, 1, 4) + block, 0)
    shared = jnp.where((sub == 0) | (sub == 7), rest, inside)
    rows = jnp.concatenate([a[0:1], a[7:8], b[0:1], b[7:8]], axis=0)
    return shared, rows


def unpack_thin_shell(shared, rows):
    lane = iota((8, 128), 1)
    sub = iota((8, 128), 0)
    rows = join_rows(rows, rows)
    edge = (lane & 15) + jnp.where(lane >= 112, 16, 0)
    z = lane & 15
    entry = 4 * ((lane >> 4) - 1) + 2 * (z >> 3) + jnp.where((z & 7) == 7, 1, 0)
    on_y = (lane < 16) | (lane >= 112)
    block = sub - jnp.where(sub > 3, 4, 1)
    moved = pick(pick(shared, jnp.where(sub <= 3, 0, 7), 0), (24 + 16 * block + entry) & 127, 1)
    out = []
    for k in range(2):
        start = 96 if k == 0 else 120
        tile_k = pick(shared, jnp.where(on_y, 32 + 32 * k + edge, start + entry) & 127, 1)
        if k == 1:
            tile_k = jnp.where(on_y | (entry < 8), tile_k, moved)
        line = pick(rows, 2 * k + jnp.where(sub == 7, 1, 0), 0)
        out.append(jnp.where((sub == 0) | (sub == 7), line, tile_k))
    return out


def z_place(entry):
    return ((1 + (entry >> 2)) * 16 + 8 * ((entry >> 1) & 1) + 7 * (entry & 1)) & 127


def pack_shell(pair):
    lane = iota((8, 128), 1)
    sub = iota((8, 128), 0)
    a, b = pair
    part = lane & 31
    along_y = part + 96 * (part >> 4)
    inside = jnp.where(lane < 96, pick(a, along_y, 1), pick(b, along_y, 1))
    sixth = jnp.full((8, 128), 6, jnp.int32)
    last = [pick(pick(t, z_place(part), 1), sixth, 0) for t in pair]
    shared = jnp.where(sub == 0, last[0], jnp.where(sub == 7, last[1], inside))
    rows = jnp.concatenate([a[0:1], a[7:8], b[0:1], b[7:8]], axis=0)
    block = (lane * 171) >> 12
    lines = [pick(pick(t, z_place(lane - 24 * block), 1), 1 + block, 0) for t in pair]
    return shared, rows, jnp.concatenate([lines[0][0:1], lines[1][0:1]], axis=0)


def unpack_shell(shared, rows, extra):
    lane = iota((8, 128), 1)
    sub = iota((8, 128), 0)
    rows = join_rows(rows, rows)
    extra = jnp.concatenate([extra] * 4, axis=0)
    edge = (lane & 15) + jnp.where(lane >= 112, 16, 0)
    z = lane & 15
    entry = 4 * ((lane >> 4) - 1) + 2 * (z >> 3) + jnp.where((z & 7) == 7, 1, 0)
    on_y = (lane < 16) | (lane >= 112)
    place = (jnp.where(sub == 6, 64, 24 * (sub - 1)) + entry) & 127
    out = []
    for k in range(2):
        whole = jnp.full((8, 128), k, jnp.int32)
        source = jnp.where(sub == 6, pick(shared, 7 * whole, 0), pick(extra, whole, 0))
        along_z = pick(source, place, 1)
        along_y = pick(shared, 64 + 32 * k + edge, 1)
        line = pick(rows, 2 * k + jnp.where(sub == 7, 1, 0), 0)
        tile_k = jnp.where(on_y, along_y, along_z)
        out.append(jnp.where((sub == 0) | (sub == 7), line, tile_k))
    return out


def shifted(value, v):
    if v[0] != 0:
        value = pltpu.roll(value, v[0] % 16, 0)
    lanes = (16 * v[1] + v[2]) % 256
    if lanes != 0:
        value = pltpu.roll(value, lanes, 1)
    return value


def positions():
    row = iota((16, 256), 0)
    lane = iota((16, 256), 1)
    return row, lane >> 4, lane & 15


def wall_weights(depth):
    place = positions()
    solid = depth <= 0
    here = depth.astype(F32)
    out = [jnp.where(solid, 1.0, 0.0).astype(F32)]
    for q in range(1, 19):
        v = VELOCITIES[q]
        outside = []
        for axis in range(3):
            if v[axis] != 0:
                outside.append(place[axis] == (0 if v[axis] > 0 else 15))
        away = outside[0] if len(outside) == 1 else outside[0] | outside[1]
        there = shifted(here, v)
        wall = (there <= 0.0) & jnp.logical_not(away) & jnp.logical_not(solid)
        gap = jnp.where(wall, here - there, 1.0)
        own = jnp.where(wall, here, 1.0)
        far = own + own >= gap
        weight = jnp.where(far, 0.5 * gap, 2.0 * own) / jnp.where(far, own, gap)
        value = jnp.where(wall, weight, -1.0)
        if len(outside) == 2:
            value = jnp.where(outside[0] & outside[1], 1.0, value)
        out.append(value)
    return out


def stream(post, start, weights, ghosts):
    place = positions()
    solid = weights(0) > 0.5
    out = [jnp.where(solid, start(0), post(0))]
    for q in range(1, 19):
        v = VELOCITIES[q]
        own = post(q)
        value = own
        for axis in (1, 0, 2):
            if v[axis] != 0:
                edge = place[axis] == (15 if v[axis] > 0 else 0)
                value = jnp.where(edge, ghosts[axis][q], value)
        value = shifted(value, v)
        weight = weights(q)
        value = jnp.where(weight >= 0.0, own + weight * (post(OPPOSITE[q]) - own), value)
        out.append(jnp.where(solid, start(q), value))
    return out


def pack_octants(fields):
    low = (iota((8, 128), 1) & 15) < 8
    out = {}
    for ox in range(2):
        for oy in range(2):
            a, b, c, d = [tile(f, ox, oy) for f in fields]
            out[4 * ox + 2 * oy] = (
                jnp.where(low, a, pltpu.roll(b, 8, 1)),
                jnp.where(low, c, pltpu.roll(d, 8, 1)),
            )
            out[4 * ox + 2 * oy + 1] = (
                jnp.where(low, pltpu.roll(a, 120, 1), b),
                jnp.where(low, pltpu.roll(c, 120, 1), d),
            )
    return out


def tile_lines(tiles):
    lane = iota((8, 128), 1)

    def at_x(k, half, inner):
        return pick(tiles[k // 2], (4 * half + (lane >> 5)) * 16 + inner, 1)

    def row_of(k, half, side):
        return jnp.full((8, 128), 7 * side, jnp.int32)

    def at_y(k, side, inner):
        return pick(tiles[k // 2], 112 * side + inner, 1)

    def at_z(k, y, side):
        return pick(tiles[k // 2], 16 * y + 8 * (k % 2) + 7 * side, 1)

    return at_x, row_of, at_y, at_z


def below(lines):
    at_x, row_of, at_y, at_z = lines
    lane = iota((8, 128), 1)
    sub = iota((8, 128), 0)
    z = lane & 15
    fields = [[], [], []]
    for k in range(4):
        inner = (z >> 1) + 8 * (k % 2)
        tiles = [[None, None], [None, None]]
        for half in range(2):
            rows = at_x(k, half, inner)
            for row in range(2):
                tiles[row][half] = pick(rows, row_of(k, half, 1 - row), 0)
        fields[0].append(join(tiles))
        for half in range(2):
            line = at_y(k, 1 - half, inner)
            for row in range(2):
                tiles[row][half] = pick(line, 4 * row + (sub >> 1), 0)
        fields[1].append(join(tiles))
        for half in range(2):
            y = 8 * half + (lane >> 4)
            far = z == 15
            line = at_z(k, ((y + jnp.where(far, 1, 15)) & 15) >> 1, jnp.where(far, 0, 1))
            for row in range(2):
                tiles[row][half] = pick(line, 4 * row + (sub >> 1), 0)
        fields[2].append(join(tiles))
    out = []
    for axis in range(3):
        ghosts = {}
        for sign in (1, -1):
            chosen = [q for q in range(19) if VELOCITIES[q][axis] == sign]
            part = fields[axis]
            if axis < 2:
                size, at = (8, 128)[axis], (8, 128)[axis] if sign > 0 else 0
                part = [lax.slice_in_dim(f, at, at + size, axis=axis) for f in part]
            rest = equilibrium(part[0], part[1:], chosen)
            for q in chosen:
                ghosts[q] = jnp.concatenate([rest[q]] * 2, axis=axis) if axis < 2 else rest[q]
        out.append(ghosts)
    return out


def restrict(f):
    lane = iota((8, 128), 1)
    sub = iota((8, 128), 0)
    density, momentum = sums(f)
    index = ((lane >> 4) & 3) * 32 + (lane & 7) * 2
    even = (2 * sub) & 7
    packed = []
    for field in [density] + momentum:
        halves = []
        for half in range(2):
            lines = [
                jnp.where(
                    sub < 4,
                    pick(tile(field, 0, half), even + odd, 0),
                    pick(tile(field, 1, half), even + odd, 0),
                )
                for odd in range(2)
            ]
            line = lines[0] + lines[1]
            parts = [pick(line, index + step, 1) for step in (0, 1, 16, 17)]
            halves.append(0.125 * ((parts[0] + parts[1]) + (parts[2] + parts[3])))
        packed.append(jnp.where(lane < 64, halves[0], halves[1]))
    low = (lane & 15) < 8
    return jnp.where(low, packed[0], packed[1]), jnp.where(low, packed[2], packed[3])


def load(ref):
    return [ref[q] for q in range(19)]


def load_cells(ref, q):
    halves = [ref[q, pl.ds(half, 16, stride=2), :] for half in range(2)]
    return jnp.concatenate(halves, axis=1)


def store_cells(ref, q, value):
    for half in range(2):
        ref[q, pl.ds(half, 16, stride=2), :] = value[:, 128 * half : 128 * half + 128]


def store_octants(fields, octs):
    for o, pair in pack_octants(fields).items():
        shared, rows, extra = pack_shell(pair)
        for part in range(4):
            octs[o, part] = shared[2 * part : 2 * part + 2]
        for part in range(2):
            octs[o, 4 + part] = rows[2 * part : 2 * part + 2]
        octs[o, 6] = extra


def give_octants(octs, parents, out):
    for d in range(32):
        o = parents[1, 0, d]
        out[d, 8:12, :, 64:128] = octs[o, 0:4, :, 64:128]
        out[d, 12:15] = octs[o, 4:7]


def give_face(post, face, code, me, out, at, lanes):
    first, second = pack_face(post, face)
    slot = jnp.where(code >= 0, code, me)
    for part in range(4):
        rows = slice(2 * part, 2 * part + 2)
        out[slot, at + part] = first[rows]
        out[slot, 8 + part, :, lanes : lanes + 32] = second[rows, lanes : lanes + 32]
    return first, second


def rows_of_pairs(ref, slot, at):
    return jnp.concatenate([ref[slot, at + part] for part in range(4)], axis=0)


def send_kernel(
    coarse_in, fine_in, coarse_table, fine_table, parent_table, out, region_out,
    coarse, fine, coarse_links, fine_links, parents, slots, region, octs, sems,
):
    fetch = [
        pltpu.make_async_copy(source, target, sems.at[i])
        for i, (source, target) in enumerate(
            (
                (coarse_in, coarse),
                (coarse_table, coarse_links),
                (fine_in, fine),
                (fine_table, fine_links),
                (parent_table, parents),
            )
        )
    ]
    for copy in fetch:
        copy.start()

    def put(part):
        rows = pl.ds(4 * part, 4 if part < 3 else 3)
        return pltpu.make_async_copy(slots.at[:, rows], out.at[:, rows], sems.at[5 + part])

    me = lax.axis_index("dev")
    fetch[0].wait()
    fetch[1].wait()
    f = [load_cells(coarse, q) for q in range(19)]
    density, u = moments(f)
    store_octants([density] + u, octs)
    post = collide(f, OMEGA_COARSE)
    for face in range(6):
        first, second = give_face(post, face, coarse_links[face, 0, me], me, slots, 0, 0)
        if face in (2, 3):
            region[face - 2, 0:8, :] = first
            region[face - 2, 8:16, :] = second
    put(0).start()
    beside = pltpu.make_async_copy(region, region_out, sems.at[9])
    beside.start()
    fetch[4].wait()
    give_octants(octs, parents, slots)
    put(3).start()
    fetch[2].wait()
    fetch[3].wait()
    post = collide([load_cells(fine, q) for q in range(19)], OMEGA_FINE)
    for face in range(6):
        give_face(post, face, fine_links[face, 0, me], me, slots, 4, 32)
    put(1).start()
    put(2).start()
    for part in range(4):
        put(part).wait()
    beside.wait()


def prepare_kernel(state, depth, post, start, weights, *old, omega):
    f = [load_cells(state, q) for q in range(19)]
    for q in range(19):
        start[q] = f[q]
    for q, value in enumerate(collide(f, omega)):
        post[q] = value
    if old:
        density, u = moments(f)
        for i, value in enumerate([density] + u):
            old[0][i] = value
    halves = [depth[pl.ds(half, 16, stride=2), :] for half in range(2)]
    for q, value in enumerate(wall_weights(jnp.concatenate(halves, axis=1))):
        weights[q] = value


def codes_kernel(coarse_links, fine_links, parents, codes):
    me = lax.axis_index("dev")
    lane = iota((1, 32), 1)
    place = [iota((8, 128), 0), iota((8, 128), 1)]
    owner, octant = parents[0], parents[1]

    def own(line):
        return jnp.sum(jnp.where(lane == me, line, 0), axis=1, keepdims=True)

    values = {}
    for face in range(6):
        values[FINE_LINKS[0] + face, FINE_LINKS[1]] = own(fine_links[face])
        values[COARSE_LINKS[0] + face, COARSE_LINKS[1]] = own(coarse_links[face])
    values[PARENT] = own(owner)
    for o in range(8):
        child = jnp.where((owner == me) & (octant == o), lane, -1)
        values[CHILDREN[0] + o, CHILDREN[1]] = jnp.max(child, axis=1, keepdims=True)
    tile_of = jnp.zeros((8, 128), jnp.int32)
    for (row, at), value in values.items():
        tile_of = jnp.where((place[0] == row) & (place[1] == at), value, tile_of)
    codes[...] = tile_of
    row, at = OCTANTS
    codes[row : row + 1, at : at + 32] = octant


class Codes:
    def __init__(self, ref):
        self.tile = ref[...]
        self.seen = {}

    def __call__(self, start, step=0):
        row, at = (start[0], start[1] + step) if start == OCTANTS else (start[0] + step, start[1])
        if (row, at) not in self.seen:
            self.seen[row, at] = self.tile[row, at]
        return self.seen[row, at]


def merge_ghosts(take):
    ghosts = [{}, {}, {}]
    for face in range(6):
        ghosts[face // 2].update(take(face))
    return ghosts


def fine_ghosts(codes, plane_of, lanes, under):
    def take(face):
        code = codes(FINE_LINKS, face)
        first, second = plane_of(jnp.maximum(code, 0))
        plane = unpack_face(first, second, lanes, face)
        return {q: jnp.where(code >= 0, plane[q], under[face // 2][q]) for q in plane}

    return merge_ghosts(take)


def middle_kernel(
    received, from_low, from_high, c_post, c_start, c_weights, f_post, f_start, f_weights,
    old, table, out, coarse_new, state, post, octs,
):
    me = lax.axis_index("dev")
    codes = Codes(table)

    def coarse_ghost(face):
        code = codes(COARSE_LINKS, face)
        slot = jnp.maximum(code, 0)
        first = rows_of_pairs(received, slot, 0)
        second = rows_of_pairs(received, slot, 8)
        if face in (2, 3):
            beside = from_low if face == 2 else from_high
            first = jnp.where(code == -2, beside[0, 0:8, :], first)
            second = jnp.where(code == -2, beside[0, 8:16, :], second)
        plane = unpack_face(first, second, 0, face)
        return {q: jnp.where(code == -1, inflow_value(q), plane[q]) for q in plane}

    new = stream(
        lambda q: c_post[q], lambda q: c_start[q], lambda q: c_weights[q], merge_ghosts(coarse_ghost)
    )
    for q in range(19):
        coarse_new[q] = new[q]
    density, u = moments(new)
    mid = [0.5 * (old[i] + value) for i, value in enumerate([density] + u)]
    for o, pair in pack_octants(mid).items():
        shared, rows = pack_thin_shell(pair)
        octs[o, 0] = shared[0:4]
        octs[o, 1] = shared[4:8]
        octs[o, 2] = rows
    parent = codes(PARENT)
    rows = join_rows(received[parent, 12], received[parent, 13])
    shell = unpack_shell(rows_of_pairs(received, parent, 8), rows, received[parent, 14])
    under = below(tile_lines(shell))
    ghosts = fine_ghosts(
        codes,
        lambda d: (rows_of_pairs(received, d, 4), rows_of_pairs(received, d, 8)),
        32,
        under,
    )
    new = stream(lambda q: f_post[q], lambda q: f_start[q], lambda q: f_weights[q], ghosts)
    for q in range(19):
        state[q] = new[q]
    after = collide(new, OMEGA_FINE)
    for q in range(19):
        post[q] = after[q]
    for face in range(6):
        first, second = pack_face(after, face)
        code = codes(FINE_LINKS, face)
        slot = jnp.where(code >= 0, code, me)
        for part in range(2):
            out[slot, part] = first[4 * part : 4 * part + 4]
            out[slot, 2 + part, :, 0:32] = second[4 * part : 4 * part + 4, 0:32]
    for d in range(32):
        o = codes(OCTANTS, d)
        out[d, 2, :, 32:128] = octs[o, 0, :, 32:128]
        out[d, 3, :, 32:128] = octs[o, 1, :, 32:128]
        out[d, 4] = octs[o, 2]


def last_kernel(received, f_post, f_start, f_weights, table, out, state):
    codes = Codes(table)
    def rows_of(d, part):
        return join_rows(received[d, part], received[d, part + 1])

    parent = codes(PARENT)
    under = below(tile_lines(unpack_thin_shell(rows_of(parent, 2), received[parent, 4])))
    ghosts = fine_ghosts(codes, lambda d: (rows_of(d, 0), rows_of(d, 2)), 0, under)
    new = stream(lambda q: f_post[q], lambda q: f_start[q], lambda q: f_weights[q], ghosts)
    for q in range(19):
        store_cells(state, q, new[q])
    first, second = restrict(new)
    out[parent, 0:8, :] = first
    out[parent, 8:16, :] = second


def cover(codes):
    low = (iota((8, 128), 1) & 15) < 8
    tiles = [[None, None], [None, None]]
    for ox in range(2):
        for oy in range(2):
            o = 4 * ox + 2 * oy
            tiles[ox][oy] = jnp.where(low, codes(CHILDREN, o), codes(CHILDREN, o + 1))
    return join(tiles) >= 0


def final_kernel(received, state, coarse_new, table, fine_out, coarse_out, cells, sems):
    fine_copy = pltpu.make_async_copy(state, fine_out, sems.at[0])
    fine_copy.start()
    codes = Codes(table)
    low = (iota((8, 128), 1) & 15) < 8
    tiles = [[[None, None], [None, None]] for _ in range(4)]
    for ox in range(2):
        for oy in range(2):
            o = 4 * ox + 2 * oy
            near = jnp.maximum(codes(CHILDREN, o), 0)
            far = jnp.maximum(codes(CHILDREN, o + 1), 0)
            for k in range(2):
                a = received[near, 8 * k : 8 * k + 8, :]
                b = received[far, 8 * k : 8 * k + 8, :]
                tiles[2 * k][ox][oy] = jnp.where(low, a, pltpu.roll(b, 8, 1))
                tiles[2 * k + 1][ox][oy] = jnp.where(low, pltpu.roll(a, 120, 1), b)
    density, jx, jy, jz = [join(t) for t in tiles]
    covered = cover(codes)
    density = jnp.where(covered, density, 1.0)
    inverse = 1.0 / density
    fine_eq = equilibrium(density, [jx * inverse, jy * inverse, jz * inverse], range(19))
    new = load(coarse_new)
    own_density, own_u = moments(new)
    own_eq = equilibrium(own_density, own_u, range(19))
    for q in range(19):
        store_cells(cells, q, new[q] + jnp.where(covered, fine_eq[q] - own_eq[q], 0.0))
    coarse_copy = pltpu.make_async_copy(cells, coarse_out, sems.at[1])
    coarse_copy.start()
    fine_copy.wait()
    coarse_copy.wait()


VMEM = pl.BlockSpec(memory_space=pltpu.VMEM)
HBM = pl.BlockSpec(memory_space=pltpu.HBM)
SOME_VMEM = 24 * 1024 * 1024
MOST_VMEM = 60 * 1024 * 1024


OCTS = pltpu.VMEM((8, 7, 2, 128), F32)
LINKS = pltpu.SMEM((6, 1, 32), jnp.int32)
SEND_SCRATCH = [
    pltpu.VMEM(CELL_ROWS, F32),
    pltpu.VMEM(CELL_ROWS, F32),
    LINKS,
    LINKS,
    pltpu.SMEM((2, 1, 32), jnp.int32),
    pltpu.VMEM(SLOT1, F32),
    pltpu.VMEM((2, 16, 128), F32),
    OCTS,
    pltpu.SemaphoreType.DMA((10,)),
]
FINAL_SCRATCH = [pltpu.VMEM(CELL_ROWS, F32), pltpu.SemaphoreType.DMA((2,))]


def call(kernel, outs, ins, hbm=(), hbm_outs=(), scratch=(), vmem=SOME_VMEM, name=None):
    return pl.pallas_call(
        kernel,
        out_shape=[jax.ShapeDtypeStruct(s, F32) for s in outs],
        in_specs=[HBM if i in hbm else VMEM for i in range(len(ins))],
        out_specs=[HBM if i in hbm_outs else VMEM for i in range(len(outs))],
        scratch_shapes=list(scratch),
        compiler_params=pltpu.CompilerParams(vmem_limit_bytes=vmem),
        cost_estimate=pl.CostEstimate(
            flops=2_000_000, bytes_accessed=2_000_000, transcendentals=0
        ),
        name=name,
    )(*ins)


def swap(value):
    return lax.all_to_all(value, "dev", split_axis=0, concat_axis=0, tiled=True)


def body(fine_state, coarse_state, fine_depth, coarse_depth, fine_links, coarse_links, parents):
    count = lax.axis_size("group")
    fine_state, coarse_state = fine_state.reshape(CELL_ROWS), coarse_state.reshape(CELL_ROWS)
    fine_depth, coarse_depth = fine_depth.reshape(32, 128), coarse_depth.reshape(32, 128)
    fine_links = fine_links.transpose(2, 0, 1)
    coarse_links = coarse_links.transpose(2, 0, 1)
    parents = parents.transpose(2, 0, 1)
    sent, region = call(
        send_kernel,
        [SLOT1, (2, 16, 128)],
        [coarse_state, fine_state, coarse_links, fine_links, parents],
        hbm=(0, 1, 2, 3, 4),
        hbm_outs=(0, 1),
        scratch=SEND_SCRATCH,
        vmem=MOST_VMEM,
        name="send",
    )
    up = [(i, i + 1) for i in range(count - 1)]
    down = [(b, a) for a, b in up]
    received = swap(sent)
    from_low = lax.ppermute(region[1:2], "group", up)
    from_high = lax.ppermute(region[0:1], "group", down)

    def prepare(state, depth, omega, name, more=()):
        def kernel(*refs):
            prepare_kernel(*refs, omega=omega)

        return call(kernel, [FIELD, FIELD, FIELD, *more], [state, depth], name=name)

    c_post, c_start, c_weights, old = prepare(
        coarse_state, coarse_depth, OMEGA_COARSE, "prepare_coarse", [(4, 16, 256)]
    )
    f_post, f_start, f_weights = prepare(fine_state, fine_depth, OMEGA_FINE, "prepare_fine")
    codes = pl.pallas_call(
        codes_kernel,
        out_shape=jax.ShapeDtypeStruct((8, 128), jnp.int32),
        in_specs=[VMEM] * 3,
        out_specs=VMEM,
        compiler_params=pltpu.CompilerParams(vmem_limit_bytes=SOME_VMEM),
        name="codes",
    )(coarse_links, fine_links, parents)
    sent, coarse_new, state, post = call(
        middle_kernel,
        [SLOT2, FIELD, FIELD, FIELD],
        [
            received, from_low, from_high, c_post, c_start, c_weights, f_post, f_start, f_weights,
            old, codes,
        ],
        scratch=[pltpu.VMEM((8, 3, 4, 128), F32)],
        name="middle",
    )
    received = swap(sent)
    sent, state = call(
        last_kernel,
        [(32, SLOT3, 128), CELL_ROWS],
        [received, post, state, f_weights, codes],
        name="last",
    )
    received = swap(sent)
    fine_out, coarse_out = call(
        final_kernel,
        [CELL_ROWS, CELL_ROWS],
        [received, state, coarse_new, codes],
        hbm_outs=(0, 1),
        scratch=FINAL_SCRATCH,
        name="final",
    )
    return fine_out.reshape(1, 19, 4096), coarse_out.reshape(1, 19, 4096)


def solution(mesh):
    placed = (
        P(("group", "dev"), None, None),
        P(("group", "dev"), None, None),
        P(("group", "dev"), None),
        P(("group", "dev"), None),
        P("group", None, None),
        P("group", None, None),
        P("group", None, None),
    )
    return jax.shard_map(
        body,
        mesh=mesh,
        in_specs=placed,
        out_specs=(P(("group", "dev"), None, None), P(("group", "dev"), None, None)),
        check_vma=False,
    )
```
